512 devices in a mesh: ens: 32 (over x, z_lo, core), node: 16 (over z_hi, y).
Axes of the slice: x: 4, y: 8, z: 8 (z_hi: 2, z_lo: 4; z = z_hi * 4 + z_lo), core: 2. Of those that a mesh axis runs over, the one named last changes fastest.
Arguments:
- hidden: bfloat16 [32, 2048, 1024], P('ens', 'node'), may hold values from -30 to 30
- forcing: bfloat16 [2048, 1024], P('node'), may hold values from -3 to 3
- norm_gain: float32 [1024], replicated, may hold values from 0.1 to 1.9
- w_query: bfloat16 [1024, 1024], P('ens'), may hold values from -0.375 to 0.375
- w_key: bfloat16 [1024, 1024], P('ens'), may hold values from -0.375 to 0.375
- w_value: bfloat16 [1024, 1024], P('ens'), may hold values from -0.1875 to 0.1875
- w_out: bfloat16 [1024, 1024], P('ens'), may hold values from -0.1875 to 0.1875
- w_decode: bfloat16 [1024, 100], replicated, may hold values from -0.1875 to 0.1875
- targets: bfloat16 [100, 2048], P(None, 'node'), may hold values from -6 to 6
- area_weight: float32 [2048], P('node'), may hold values from 0.4 to 14, as said below
Outputs:
- grad_hidden: bfloat16 [32, 2048, 1024], P('ens', 'node')
- grad_out_proj: float32 [1024, 1024], P('ens')
- loss: float32 [], replicated
The draws below stay inside these ranges and needn't reach their ends.
Inputs may be any that keep to these rules, and one draw needn't show every extreme that they name: `area_weight`: positive.
All inputs are finite; a program needn't handle non-finite values.
Results may differ from the reference program's by a relative error of at most 0.035.
Values may be sent and summed in bfloat16 or wider, within the bound.
No kernel may reach another device: no remote copies, remote signals or barrier semaphores. Data moves between devices by JAX's collectives and lax.ppermute only.
A program may use at most 128 MiB of HBM per device.

```python
import math
import jax
import jax.numpy as jnp
from jax import lax

D = 1024
HEADS = 16
V = 100
NODE_DEV = 128
HALO = 128
HD = 64
MEMBERS = 32
NODES = 2048


def draw_area_weight(key, part):
    key = jax.random.fold_in(key, 7)
    position = jnp.arange(NODES, dtype=jnp.float32) / NODES
    rough = jnp.exp(jax.random.uniform(key, (NODES,), jnp.float32, -0.69, 0.69))
    return (1.0 + 3.0 * position) * rough


def member_scales(top):
    rank = jnp.arange(MEMBERS, dtype=jnp.float32) / (MEMBERS - 1)
    return jnp.exp(jnp.log(top) * rank)[:, None, None]


def draw_hidden(key, part):
    key = jax.random.fold_in(key, 11)
    base = jax.random.truncated_normal(key, -6.0, 6.0, (MEMBERS, NODES, D), jnp.float32)
    return (base * member_scales(3.0)).astype(jnp.bfloat16)


def block_scale(own_key, dims, shards, smallest, largest):
    level = 1.0
    for dim, blocks in shards:
        heights = jax.random.uniform(jax.random.fold_in(jax.random.fold_in(own_key, 6), dim), (blocks,), jnp.float32, smallest / len(shards), largest / len(shards))
        level = level * jnp.repeat(jnp.exp(heights), dims[dim] // blocks).reshape((-1,) + (1,) * (len(dims) - 1 - dim))
    return level


def scatter_about(stream_key, dims, spread, reach, cuts=(), kind=jnp.bfloat16):
    loudness = block_scale(stream_key, dims, cuts, -0.22, 0.18) if cuts else 1.0
    values = jax.random.normal(stream_key, dims, jnp.float32) * spread * loudness
    return jnp.minimum(jnp.maximum(values, -reach), reach).astype(kind)


def setup_inputs(seed: int = 0) -> dict:
    key_list = jax.random.split(jax.random.key(seed), 11)
    return {
        "hidden": draw_hidden(jax.random.fold_in(key_list[10], 71), 0),
        "forcing": scatter_about(key_list[1], (NODES, D), 0.5, 3.0, ((0, 16),)),
        "norm_gain": jnp.clip(1.0 + 0.18 * jax.random.normal(key_list[2], (D,), jnp.float32), 0.1, 1.9),
        "w_query": scatter_about(key_list[3], (D, D), (D // 4) ** -0.5, 0.375, ((0, 32),)),
        "w_key": scatter_about(key_list[4], (D, D), (D // 4) ** -0.5, 0.375, ((0, 32),)),
        "w_value": scatter_about(key_list[5], (D, D), D ** -0.5, 0.1875, ((0, 32),)),
        "w_out": scatter_about(key_list[6], (D, D), D ** -0.5, 0.1875, ((0, 32),)),
        "w_decode": scatter_about(key_list[7], (D, V), D ** -0.5, 0.1875),
        "targets": scatter_about(key_list[8], (V, NODES), 1.0, 6.0, ((1, 16),)),
        "area_weight": draw_area_weight(jax.random.fold_in(key_list[10], 71), 0),
    }


ALPHA = 0.95
KAPPA = 0.25
EPS_NORM = 1e-05

def smooth_abs(delta):
    return jnp.sqrt(delta * delta + KAPPA * KAPPA) - KAPPA

def smooth_slope(delta):
    return delta / jnp.sqrt(delta * delta + KAPPA * KAPPA)

def band_mask(count):
    query_pos = lax.broadcasted_iota(jnp.int32, (count, count + 2 * HALO), 0)
    key_pos = lax.broadcasted_iota(jnp.int32, (count, count + 2 * HALO), 1)
    offset = key_pos - query_pos
    return (offset >= 0) & (offset <= 2 * HALO)

def extend(field):
    return jnp.concatenate([field[-HALO:], field, field[:HALO]], 0)

def block_probs(query_block, key_block):
    count = query_block.shape[0]
    query3 = query_block.reshape(count, HEADS, HD).astype(jnp.float32)
    key3 = key_block.reshape(count + 2 * HALO, HEADS, HD).astype(jnp.float32)
    scores = jnp.einsum('qhd,khd->hqk', query3, key3) * (1.0 / math.sqrt(HD))
    expo = jnp.where(band_mask(count)[None], jnp.exp(scores), jnp.float32(0.0))
    return expo / lax.optimization_barrier(jnp.sum(expo, -1, keepdims=True))

def forward_member(member_hidden, forcing, norm_gain, w_query, w_key, w_value, w_out, w_decode):
    xfield = member_hidden.astype(jnp.float32) + forcing.astype(jnp.float32)
    inverse_rms = lax.rsqrt(lax.optimization_barrier(jnp.mean(xfield * xfield, -1, keepdims=True)) + EPS_NORM)
    normed = (xfield * inverse_rms * norm_gain).astype(jnp.bfloat16)
    queries = jnp.dot(normed, w_query, preferred_element_type=jnp.float32).astype(jnp.bfloat16)
    keys_all = jnp.dot(normed, w_key, preferred_element_type=jnp.float32).astype(jnp.bfloat16)
    values_all = jnp.dot(normed, w_value, preferred_element_type=jnp.float32).astype(jnp.bfloat16)
    key_ext = extend(keys_all)
    value_ext = extend(values_all)
    block_rows = NODE_DEV
    span = block_rows + 2 * HALO

    def one_block(block):
        start = block * block_rows
        query_block = lax.dynamic_slice_in_dim(queries, start, block_rows, 0)
        key_block = lax.dynamic_slice_in_dim(key_ext, start, span, 0)
        value_block = lax.dynamic_slice_in_dim(value_ext, start, span, 0)
        probs_b = block_probs(query_block, key_block).astype(jnp.bfloat16)
        value3 = value_block.reshape(span, HEADS, HD).astype(jnp.float32)
        out = jnp.einsum('hqk,khd->qhd', probs_b.astype(jnp.float32), value3)
        return out.astype(jnp.bfloat16).reshape(block_rows, D)
    attended = lax.map(one_block, jnp.arange(NODES // block_rows, dtype=jnp.int32)).reshape(NODES, D)
    resid = xfield + jnp.dot(attended, w_out, preferred_element_type=jnp.float32)
    resid_b = resid.astype(jnp.bfloat16)
    pred = lax.dot_general(w_decode, resid_b, (((0,), (1,)), ((), ())), preferred_element_type=jnp.float32)
    saved = (xfield, inverse_rms, queries, key_ext, value_ext, attended)
    return (pred.astype(jnp.bfloat16), saved)

def backward_member(member_hidden, grad_pred, forcing, norm_gain, w_query, w_key, w_value, w_out, w_decode):
    unused, saved = forward_member(member_hidden, forcing, norm_gain, w_query, w_key, w_value, w_out, w_decode)
    xfield, inverse_rms, queries, key_ext, value_ext, attended = saved
    grad_resid = lax.dot_general(grad_pred, w_decode, (((0,), (1,)), ((), ())), preferred_element_type=jnp.float32)
    grad_resid_b = grad_resid.astype(jnp.bfloat16)
    grad_wout = lax.dot_general(attended, grad_resid_b, (((0,), (0,)), ((), ())), preferred_element_type=jnp.float32)
    grad_attended = lax.dot_general(grad_resid_b, w_out, (((1,), (1,)), ((), ())), preferred_element_type=jnp.float32).astype(jnp.bfloat16)
    block_rows = NODE_DEV
    span = block_rows + 2 * HALO
    scale = 1.0 / math.sqrt(HD)

    def step(carry, block):
        start = block * block_rows
        query_block = lax.dynamic_slice_in_dim(queries, start, block_rows, 0)
        key_block = lax.dynamic_slice_in_dim(key_ext, start, span, 0)
        value_block = lax.dynamic_slice_in_dim(value_ext, start, span, 0)
        grad_block = lax.dynamic_slice_in_dim(grad_attended, start, block_rows, 0)
        probs = block_probs(query_block, key_block)
        probs_b = probs.astype(jnp.bfloat16)
        query3 = query_block.reshape(block_rows, HEADS, HD).astype(jnp.float32)
        key3 = key_block.reshape(span, HEADS, HD).astype(jnp.float32)
        value3 = value_block.reshape(span, HEADS, HD).astype(jnp.float32)
        grad3 = grad_block.reshape(block_rows, HEADS, HD).astype(jnp.float32)
        grad_probs = jnp.einsum('qhd,khd->hqk', grad3, value3)
        delta = lax.optimization_barrier(jnp.sum(probs * grad_probs, -1, keepdims=True))
        grad_scores = (probs * (grad_probs - delta) * scale).astype(jnp.bfloat16).astype(jnp.float32)
        grad_query = jnp.einsum('hqk,khd->qhd', grad_scores, key3).astype(jnp.bfloat16).reshape(block_rows, D)
        grad_key = jnp.einsum('hqk,qhd->khd', grad_scores, query3).reshape(span, D)
        grad_value = jnp.einsum('hqk,qhd->khd', probs_b.astype(jnp.float32), grad3).reshape(span, D)
        contrib = jnp.concatenate([grad_key, grad_value], 1)
        old = lax.dynamic_slice_in_dim(carry, start, span, 0)
        return (lax.dynamic_update_slice_in_dim(carry, old + contrib, start, 0), grad_query)
    zeros_ext = jnp.zeros((NODES + 2 * HALO, 2 * D), jnp.float32)
    grad_ext, grad_blocks = lax.scan(step, zeros_ext, jnp.arange(NODES // block_rows, dtype=jnp.int32))
    grad_queries = grad_blocks.reshape(NODES, D)
    inner = grad_ext[HALO:HALO + NODES]
    inner = inner.at[:HALO].add(grad_ext[NODES + HALO:])
    inner = inner.at[NODES - HALO:].add(grad_ext[:HALO])
    grad_keys = inner[:, :D].astype(jnp.bfloat16)
    grad_values = inner[:, D:].astype(jnp.bfloat16)
    contract = (((1,), (1,)), ((), ()))
    grad_normed = lax.dot_general(grad_queries, w_query, contract, preferred_element_type=jnp.float32) + lax.dot_general(grad_keys, w_key, contract, preferred_element_type=jnp.float32) + lax.dot_general(grad_values, w_value, contract, preferred_element_type=jnp.float32)
    scaled = norm_gain * grad_normed
    grad_x = inverse_rms * scaled - xfield * inverse_rms ** 3 * lax.optimization_barrier(jnp.mean(xfield * scaled, -1, keepdims=True))
    return ((grad_resid + grad_x).astype(jnp.bfloat16), grad_wout)

def reference(hidden, forcing, norm_gain, w_query, w_key, w_value, w_out, w_decode, targets, area_weight):

    def member_pred(member_hidden):
        return forward_member(member_hidden, forcing, norm_gain, w_query, w_key, w_value, w_out, w_decode)[0]
    preds = lax.map(member_pred, hidden).astype(jnp.float32)
    truth = targets.astype(jnp.float32)[None]

    def member_terms(member_pred_row):
        delta = member_pred_row[None] - preds
        return (lax.optimization_barrier(jnp.sum(smooth_abs(delta), 0)), lax.optimization_barrier(jnp.sum(smooth_slope(delta), 0)))
    pair_abs, pair_slope = lax.map(member_terms, preds)
    members = MEMBERS
    eps = (1.0 - ALPHA) / members
    coeff = (1.0 - eps) / (2.0 * (members - 1))
    weights = area_weight[None, None, :]
    entries = smooth_abs(preds - truth) - coeff * pair_abs
    loss = jnp.sum(weights * entries) / (members * NODES * V)
    grad_pred = (weights * (smooth_slope(preds - truth) - 2.0 * coeff * pair_slope)).astype(jnp.bfloat16)

    def member_step(total, inputs):
        member_hidden, member_grad = inputs
        grad_member, grad_wout = backward_member(member_hidden, member_grad, forcing, norm_gain, w_query, w_key, w_value, w_out, w_decode)
        return (total + grad_wout, grad_member)
    grad_out_proj, grad_hidden = lax.scan(member_step, jnp.zeros((D, D), jnp.float32), (hidden, grad_pred))
    return (grad_hidden, grad_out_proj, loss)
```

```python
import math

import jax
import jax.numpy as jnp
from jax import lax
from jax.sharding import PartitionSpec as P

HEADS = 16
HALO = 128
LANES = 128


ALPHA = 0.95
KAPPA = 0.25
EPS_NORM = 1e-05


def extended_2(block, sides, width):
    for axis, dim in sides:
        count = lax.axis_size(axis)
        forward = [(i, i + 1) for i in range(count - 1)]
        forward.append((count - 1, 0))
        backward = [(target, source) for source, target in forward]
        low = lax.ppermute(
            lax.slice_in_dim(block, block.shape[dim] - width, None, axis=dim), axis, forward
        )
        high = lax.ppermute(lax.slice_in_dim(block, 0, width, axis=dim), axis, backward)
        block = jnp.concatenate([low, block, high], axis=dim)
    return block


def shifted(value, axis, steps):
    count = lax.axis_size(axis)
    pairs = [(source, (source + steps) % count) for source in range(count)]
    return lax.ppermute(value, axis, pairs)


def smooth_abs(delta):
    return jnp.sqrt(delta * delta + KAPPA * KAPPA) - KAPPA


def smooth_slope(delta):
    return delta / jnp.sqrt(delta * delta + KAPPA * KAPPA)


def per_device(
    hidden, forcing, norm_gain, w_query, w_key, w_value, w_out, w_decode, targets, area_weight
):
    f32, b16 = jnp.float32, jnp.bfloat16
    node_rows = hidden.shape[1]
    width = hidden.shape[2]
    head_size = width // HEADS
    span = node_rows + 2 * HALO
    scale = 1.0 / math.sqrt(head_size)
    members = lax.axis_size("ens")
    shards = lax.axis_size("node")
    rows = w_query.shape[0]
    variables = w_decode.shape[1]
    decode = jnp.pad(w_decode, ((0, 0), (0, LANES - variables)))
    mixed = jnp.dot(w_out, decode, preferred_element_type=f32).astype(b16)
    packed = jnp.concatenate([w_query, w_key, w_value, mixed], 1)
    full = lax.all_gather(packed, "ens", axis=0, tiled=True)
    full_query = full[:, :width]
    full_key = full[:, width : 2 * width]
    full_value = full[:, 2 * width : 3 * width]
    full_mixed = full[:, 3 * width :]
    xfield = hidden[0].astype(f32) + forcing.astype(f32)
    inverse_rms = lax.rsqrt(jnp.mean(xfield * xfield, -1, keepdims=True) + EPS_NORM)
    normed = (xfield * inverse_rms * norm_gain).astype(b16)
    queries = jnp.dot(normed, full_query, preferred_element_type=f32).astype(b16)
    keys_local = jnp.dot(normed, full_key, preferred_element_type=f32).astype(b16)
    values_local = jnp.dot(normed, full_value, preferred_element_type=f32).astype(b16)
    paired = jnp.concatenate([keys_local, values_local], 1)
    extended = extended_2(paired, (("node", 0),), HALO)
    query3 = queries.reshape(node_rows, HEADS, head_size)
    key3 = extended[:, :width].reshape(span, HEADS, head_size)
    value3 = extended[:, width:].reshape(span, HEADS, head_size)
    query_pos = lax.broadcasted_iota(jnp.int32, (node_rows, span), 0)
    key_pos = lax.broadcasted_iota(jnp.int32, (node_rows, span), 1)
    offset = key_pos - query_pos
    window = (offset >= 0) & (offset <= 2 * HALO)
    scores = jnp.einsum("qhd,khd->hqk", query3, key3, preferred_element_type=f32) * scale
    expo = jnp.where(window[None], jnp.exp(scores), f32(0.0))
    probs = expo / jnp.sum(expo, -1, keepdims=True)
    probs_b = probs.astype(b16)
    attended = jnp.einsum("hqk,khd->qhd", probs_b, value3, preferred_element_type=f32)
    attended = attended.astype(b16).reshape(node_rows, width)
    contract0 = (((0,), (1,)), ((), ()))
    pred_b = (
        lax.dot_general(decode, hidden[0], contract0, preferred_element_type=f32)
        + lax.dot_general(decode, forcing, contract0, preferred_element_type=f32)
        + lax.dot_general(full_mixed, attended, contract0, preferred_element_type=f32)
    )[:variables].astype(b16)
    eps = (1.0 - ALPHA) / members
    coeff = (1.0 - eps) / (2.0 * (members - 1))
    own = pred_b.astype(f32)
    others = lax.all_to_all(
        jnp.broadcast_to(pred_b[None], (members,) + pred_b.shape), "ens", 0, 0, tiled=True
    )
    delta = own[None] - others.astype(f32)
    pair_abs = jnp.sum(smooth_abs(delta), 0)
    pair_slope = jnp.sum(smooth_slope(delta), 0)
    truth = targets.astype(f32)
    weights = area_weight[None, :]
    entries = smooth_abs(own - truth) - coeff * pair_abs
    loss_part = jnp.sum(weights * entries)
    grad_pred = (weights * (smooth_slope(own - truth) - 2.0 * coeff * pair_slope)).astype(b16)
    grad_pred = jnp.pad(grad_pred, ((0, LANES - variables), (0, 0)))
    grad_resid = lax.dot_general(
        grad_pred, decode, (((0,), (1,)), ((), ())), preferred_element_type=f32
    )
    gram = lax.dot_general(
        attended, grad_pred, (((0,), (1,)), ((), ())), preferred_element_type=f32
    ).astype(b16)
    loss_high = loss_part.astype(b16)
    loss_rest = loss_part - loss_high.astype(f32)
    loss_mid = loss_rest.astype(b16)
    loss_low = (loss_rest - loss_mid.astype(f32)).astype(b16)
    column = lax.broadcasted_iota(jnp.int32, gram.shape, 1)
    gram = jnp.where(column == variables, loss_high, gram)
    gram = jnp.where(column == variables + 1, loss_mid, gram)
    gram = jnp.where(column == variables + 2, loss_low, gram)
    parts = lax.all_to_all(gram.reshape(members, rows, LANES), "ens", 0, 0, tiled=True)
    part = jnp.sum(parts.astype(f32), 0)
    parts = lax.all_to_all(
        jnp.broadcast_to(part[None], (shards,) + part.shape), "node", 0, 0, tiled=True
    )
    total = jnp.sum(parts, 0)
    grad_out_proj = lax.dot_general(
        total[:, :variables],
        w_decode.astype(f32),
        (((1,), (1,)), ((), ())),
        preferred_element_type=f32,
    )
    loss = jnp.sum(total[0, variables : variables + 3]) / (members * node_rows * shards * variables)
    grad_attended = lax.dot_general(
        grad_pred, full_mixed, (((0,), (1,)), ((), ())), preferred_element_type=f32
    ).astype(b16)
    grad3 = grad_attended.reshape(node_rows, HEADS, head_size)
    grad_probs = jnp.einsum("qhd,khd->hqk", grad3, value3, preferred_element_type=f32)
    delta_row = jnp.sum(probs * grad_probs, -1, keepdims=True)
    grad_scores = (probs * (grad_probs - delta_row) * scale).astype(b16)
    grad_queries = jnp.einsum("hqk,khd->qhd", grad_scores, key3, preferred_element_type=f32)
    grad_queries = grad_queries.astype(b16).reshape(node_rows, width)
    grad_key_ext = jnp.einsum(
        "hqk,qhd->khd", grad_scores, query3, preferred_element_type=f32
    ).reshape(span, width)
    grad_value_ext = jnp.einsum(
        "hqk,qhd->khd", probs_b, grad3, preferred_element_type=f32
    ).reshape(span, width)
    grad_ext = jnp.concatenate([grad_key_ext, grad_value_ext], 1)
    from_right = shifted(grad_ext[:HALO].astype(b16), "node", -1).astype(f32)
    from_left = shifted(grad_ext[node_rows + HALO :].astype(b16), "node", 1).astype(f32)
    inner = grad_ext[HALO : HALO + node_rows]
    inner = inner.at[:HALO].add(from_left)
    inner = inner.at[node_rows - HALO :].add(from_right)
    grad_keys = inner[:, :width].astype(b16)
    grad_values = inner[:, width:].astype(b16)
    contract = (((1,), (1,)), ((), ()))
    grad_normed = (
        lax.dot_general(grad_queries, full_query, contract, preferred_element_type=f32)
        + lax.dot_general(grad_keys, full_key, contract, preferred_element_type=f32)
        + lax.dot_general(grad_values, full_value, contract, preferred_element_type=f32)
    )
    scaled = norm_gain * grad_normed
    grad_x = inverse_rms * scaled - xfield * inverse_rms**3 * jnp.mean(
        xfield * scaled, -1, keepdims=True
    )
    grad_hidden = (grad_resid + grad_x).astype(b16)[None]
    return (grad_hidden, grad_out_proj, loss)


def solution(mesh):
    placed = (
        P("ens", "node", None),
        P("node", None),
        P(),
        P("ens", None),
        P("ens", None),
        P("ens", None),
        P("ens", None),
        P(),
        P(None, "node"),
        P("node"),
    )
    return jax.shard_map(
        per_device,
        mesh=mesh,
        in_specs=placed,
        out_specs=(P("ens", "node", None), P("ens", None), P()),
        check_vma=False,
    )
```

```python
import math

import jax
import jax.numpy as jnp
from jax import lax
from jax.experimental import pallas as pl
from jax.experimental.pallas import tpu as pltpu
from jax.sharding import PartitionSpec as P

HEADS = 16
HALO = 128
LANES = 128
STEP = 256
VROWS = 112


ALPHA = 0.95
KAPPA = 0.25
EPS_NORM = 1e-05
FAR = -1e30

f32 = jnp.float32
b16 = jnp.bfloat16


def nn(a, b):
    return lax.dot_general(a, b, (((1,), (0,)), ((), ())), preferred_element_type=f32)


def nt(a, b):
    return lax.dot_general(a, b, (((1,), (1,)), ((), ())), preferred_element_type=f32)


def tn(a, b):
    return lax.dot_general(a, b, (((0,), (0,)), ((), ())), preferred_element_type=f32)


def whole(shape):
    return pl.BlockSpec(shape, lambda i: (0,) * len(shape))


def head_masks(value):
    lane = lax.broadcasted_iota(jnp.int32, (1, LANES), 1)
    first = jnp.where(lane < LANES // 2, value, 0.0).astype(b16)
    second = jnp.where(lane < LANES // 2, 0.0, value).astype(b16)
    return first, second


def window_mask(rows, span):
    offset = lax.broadcasted_iota(jnp.int32, (rows, span), 1) - lax.broadcasted_iota(
        jnp.int32, (rows, span), 0
    )
    return (offset >= 0) & (offset <= 2 * HALO)


def split_bf16(value, pieces):
    out = []
    for _ in range(pieces):
        piece = value.astype(b16)
        out.append(piece)
        value = value - piece.astype(f32)
    return out


def forward_kernel(
    scale, variables, low, own, high, wq, wk, wv, mixed, hidden, forcing, decode,
    queries, keys, values, attended, lse, pred, normed, total,
):
    step = pl.program_id(0)
    rows = own.shape[0]
    span = rows + 2 * HALO

    @pl.when(step == 0)
    def _():
        normed[:HALO] = low[...]
        normed[HALO : HALO + rows] = own[...]
        normed[HALO + rows :] = high[...]
        total[...] = nn(hidden[0], decode[...]) + nn(forcing[...], decode[...])

    field = normed[...]
    queries[...] = nn(field, wq[...]).astype(b16)
    keys[...] = nn(field, wk[...]).astype(b16)
    values[...] = nn(field, wv[...]).astype(b16)
    window = window_mask(rows, span)
    masks = head_masks(scale)
    lower = lax.broadcasted_iota(jnp.int32, (rows, LANES), 1) < LANES // 2
    for pair in range(STEP // LANES):
        cols = slice(pair * LANES, (pair + 1) * LANES)
        query = queries[HALO : HALO + rows, cols]
        key = keys[:, cols]
        value = values[:, cols]
        outs, stats = [], []
        for mask in masks:
            scores = jnp.where(window, nt(query * mask, key), FAR)
            top = jnp.max(scores, -1, keepdims=True)
            expo = jnp.exp(scores - top)
            norm = jnp.sum(expo, -1, keepdims=True)
            probs = (expo * (1.0 / norm)).astype(b16)
            outs.append(nn(probs, value))
            stats.append(top + jnp.log(norm))
        attended[:, cols] = jnp.where(lower, outs[0], outs[1]).astype(b16)
        lse[:, cols] = jnp.where(lower, stats[0], stats[1])
    total[...] += nn(attended[...], mixed[...])

    @pl.when(step == pl.num_programs(0) - 1)
    def _():
        pred[...] = total[...].T[:VROWS].astype(b16)


def loss_kernel(
    coeff, variables, others, pred, targets, weight, attended, mixed, lse,
    gram, halo, grad_attended,
):
    own = pred[...].astype(f32)
    rows = attended.shape[0]
    width = attended.shape[1]

    def member(index, carry):
        pair_abs, pair_slope = carry
        delta = own - others[index].astype(f32)
        square = delta * delta + KAPPA * KAPPA
        inverse = lax.rsqrt(square)
        return pair_abs + (square * inverse - KAPPA), pair_slope + delta * inverse

    zero = jnp.zeros((VROWS, LANES), f32)
    pair_abs, pair_slope = lax.fori_loop(0, others.shape[0], member, (zero, zero), unroll=4)
    delta = own - targets[...].astype(f32)
    square = delta * delta + KAPPA * KAPPA
    inverse = lax.rsqrt(square)
    real = lax.broadcasted_iota(jnp.int32, (VROWS, LANES), 0) < variables
    scale = weight[...]
    entries = jnp.where(real, scale * (square * inverse - KAPPA - coeff * pair_abs), 0.0)
    loss = jnp.sum(jnp.sum(entries, 0, keepdims=True), 1, keepdims=True)
    grad = jnp.where(real, scale * (delta * inverse - 2.0 * coeff * pair_slope), 0.0)
    grad_b = grad.astype(b16)
    halo[:VROWS] = grad_b
    grad_full = jnp.concatenate([grad, jnp.zeros((LANES - VROWS, LANES), f32)], 0)
    grad_t = grad_full.T.astype(b16)
    parts = nn(grad_full.astype(b16), attended[...])
    parts = parts.T
    column = lax.broadcasted_iota(jnp.int32, (width, LANES), 1)
    for index, piece in enumerate(split_bf16(loss, 3)):
        parts = jnp.where(column == variables + index, piece.astype(f32), parts)
    gram[...] = parts.astype(b16)
    grad_att = nt(grad_t, mixed[...]).astype(b16)
    grad_attended[...] = grad_att
    size = width // HEADS
    head = lax.broadcasted_iota(jnp.int32, (HEADS, width), 0)
    feature = lax.broadcasted_iota(jnp.int32, (HEADS, width), 1)
    inside = jnp.where((feature >= head * size) & (feature < (head + 1) * size), 1.0, 0.0)
    chosen = jnp.where(feature == head * size, 1.0, 0.0).astype(b16)
    inside = inside.astype(b16)
    product = grad_att.astype(f32) * attended[...].astype(f32)
    row_delta = sum(nt(inside, piece) for piece in split_bf16(product, 2))
    row_lse = sum(nt(chosen, piece) for piece in split_bf16(lse[...], 3))
    at = VROWS
    for piece in split_bf16(row_delta, 2) + split_bf16(row_lse, 3):
        halo[at : at + HEADS] = piece
        at += HEADS


def own_kernel(scale, query, keys, values, grad_att, lse, grad_query, grad_key, grad_value):
    rows = query.shape[0]
    span = keys.shape[0]
    window = window_mask(rows, span)
    scaled = head_masks(scale)
    plain = head_masks(1.0)
    center = slice(HALO, HALO + rows)
    for pair in range(STEP // LANES):
        cols = slice(pair * LANES, (pair + 1) * LANES)
        q, k, v, g = query[:, cols], keys[:, cols], values[:, cols], grad_att[:, cols]
        stats = lse[:, cols]
        d_query = d_key = d_value = None
        for half in range(2):
            q_half = q * scaled[half]
            g_half = g * plain[half]
            at = half * (LANES // 2)
            probs = jnp.where(window, jnp.exp(nt(q_half, k) - stats[:, at : at + 1]), 0.0)
            d_probs = nt(g_half, v)
            delta = jnp.sum(probs * d_probs, -1, keepdims=True)
            d_scores = (probs * (d_probs - delta)).astype(b16)
            probs = probs.astype(b16)
            dq = nn(d_scores, k * scaled[half])
            dk = tn(d_scores[:, center], q_half)
            dv = tn(probs[:, center], g_half)
            d_query = dq if d_query is None else d_query + dq
            d_key = dk if d_key is None else d_key + dk
            d_value = dv if d_value is None else d_value + dv
        grad_query[:, cols] = d_query.astype(b16)
        grad_key[:, cols] = d_key
        grad_value[:, cols] = d_value


def halo_kernel(
    scale, low, high, query_low, query_high, keys, values, grad_query, key_part, value_part,
    wq, wk, wv, mixed, hidden, forcing, inverse_rms, gain, halo, decode,
    grad_hidden, grad_t, stats, total,
):
    step = pl.program_id(0)
    rows = keys.shape[0]

    @pl.when(step == 0)
    def _():
        zero = jnp.zeros((LANES - VROWS, LANES), b16)
        for side, part in enumerate((low, high)):
            grad = jnp.concatenate([part[:VROWS], zero], 0)
            grad_t[side * HALO : (side + 1) * HALO] = grad.astype(f32).T.astype(b16)
            at = slice(side * HALO, (side + 1) * HALO)
            pieces = [
                part[VROWS + HEADS * n : VROWS + HEADS * (n + 1)].astype(f32) for n in range(5)
            ]
            stats[0, :, at] = pieces[0] + pieces[1]
            stats[1, :, at] = pieces[2] + pieces[3] + pieces[4]
        total[...] = jnp.zeros_like(total)

    key_at = lax.broadcasted_iota(jnp.int32, (rows, 2 * HALO), 0)
    query_at = lax.broadcasted_iota(jnp.int32, (rows, 2 * HALO), 1)
    window = ((query_at < HALO) & (query_at >= key_at)) | (
        (query_at >= HALO) & (query_at - HALO <= key_at)
    )
    scaled = head_masks(scale)
    plain = head_masks(1.0)
    grad_att = nt(grad_t[...], mixed[...]).astype(b16)
    per_step = 2 * (STEP // LANES)
    d_keys, d_values = [], []
    for pair in range(STEP // LANES):
        cols = slice(pair * LANES, (pair + 1) * LANES)
        q = jnp.concatenate([query_low[:, cols], query_high[:, cols]], 0)
        k, v, g = keys[:, cols], values[:, cols], grad_att[:, cols]
        d_key = key_part[:, cols]
        d_value = value_part[:, cols]
        for half in range(2):
            row = step * per_step + 2 * pair + half
            delta = stats[0, pl.ds(row, 1), :]
            lse = stats[1, pl.ds(row, 1), :]
            probs = jnp.where(window, jnp.exp(nt(k * scaled[half], q) - lse), 0.0)
            d_probs = nt(v * plain[half], g)
            d_scores = (probs * (d_probs - delta)).astype(b16)
            d_key = d_key + nn(d_scores, q * scaled[half])
            d_value = d_value + nn(probs.astype(b16), g * plain[half])
        d_keys.append(d_key.astype(b16))
        d_values.append(d_value.astype(b16))
    total[...] += (
        nt(grad_query[...], wq[...])
        + nt(jnp.concatenate(d_keys, 1), wk[...])
        + nt(jnp.concatenate(d_values, 1), wv[...])
    )

    @pl.when(step == pl.num_programs(0) - 1)
    def _():
        zero = jnp.zeros((LANES - VROWS, LANES), b16)
        own = jnp.concatenate([halo[:VROWS], zero], 0).astype(f32).T.astype(b16)
        grad_resid = nt(own, decode[...])
        xfield = hidden[0].astype(f32) + forcing[...].astype(f32)
        inverse = inverse_rms[...]
        grad = gain[...] * total[...]
        mean = jnp.mean(xfield * grad, -1, keepdims=True)
        result = grad_resid + inverse * grad - xfield * (inverse * inverse * inverse * mean)
        grad_hidden[0] = result.astype(b16)


def shifted(value, axis, steps):
    count = lax.axis_size(axis)
    pairs = [(source, (source + steps) % count) for source in range(count)]
    return lax.ppermute(value, axis, pairs)


def per_device(
    hidden, forcing, norm_gain, w_query, w_key, w_value, w_out, w_decode, targets, area_weight
):
    node_rows = hidden.shape[1]
    width = hidden.shape[2]
    head_size = width // HEADS
    span = node_rows + 2 * HALO
    scale = 1.0 / math.sqrt(head_size)
    members = lax.axis_size("ens")
    shards = lax.axis_size("node")
    rows = w_query.shape[0]
    variables = w_decode.shape[1]
    steps = width // STEP
    shape = jax.ShapeDtypeStruct
    params = pltpu.CompilerParams(
        dimension_semantics=("arbitrary",), vmem_limit_bytes=48 * 1024 * 1024
    )
    decode = jnp.pad(w_decode, ((0, 0), (0, LANES - variables)))
    mixed = jnp.dot(w_out, decode, preferred_element_type=f32).astype(b16)
    packed = jnp.concatenate([w_query, w_key, w_value, mixed], 1)
    full = lax.all_gather(packed, "ens", axis=0, tiled=True)
    xfield = hidden[0].astype(f32) + forcing.astype(f32)
    inverse_rms = lax.rsqrt(jnp.mean(xfield * xfield, -1, keepdims=True) + EPS_NORM)
    normed = (xfield * inverse_rms * norm_gain).astype(b16)
    low = shifted(normed, "node", 1)
    high = shifted(normed, "node", -1)

    def columns(at):
        return pl.BlockSpec((width, STEP), lambda i: (0, at * steps + i))

    def blocks(height, at=0):
        return pl.BlockSpec((height, STEP), lambda i: (at, i))

    mixed_block = pl.BlockSpec((STEP, LANES), lambda i: (i, 3 * width // LANES))
    own_block = whole((1, node_rows, width))
    queries, keys, values, attended, lse, pred = pl.pallas_call(
        lambda *refs: forward_kernel(scale, variables, *refs),
        grid=(steps,),
        in_specs=[
            whole((HALO, width)),
            whole((node_rows, width)),
            whole((HALO, width)),
            columns(0),
            columns(1),
            columns(2),
            mixed_block,
            own_block,
            whole((node_rows, width)),
            whole((width, LANES)),
        ],
        out_specs=[
            blocks(span),
            blocks(span),
            blocks(span),
            blocks(node_rows),
            blocks(node_rows),
            whole((VROWS, node_rows)),
        ],
        out_shape=[
            shape((span, width), b16),
            shape((span, width), b16),
            shape((span, width), b16),
            shape((node_rows, width), b16),
            shape((node_rows, width), f32),
            shape((VROWS, node_rows), b16),
        ],
        scratch_shapes=[
            pltpu.VMEM((span, width), b16),
            pltpu.VMEM((node_rows, LANES), f32),
        ],
        compiler_params=params,
        name="forward",
    )(low, normed, high, full, full, full, full, hidden, forcing, decode)

    others = lax.all_to_all(
        jnp.broadcast_to(pred[None], (members,) + pred.shape), "ens", 0, 0, tiled=True
    )
    eps = (1.0 - ALPHA) / members
    coeff = (1.0 - eps) / (2.0 * (members - 1))
    truth = jnp.pad(targets, ((0, VROWS - variables), (0, 0)))
    payload = VROWS + 5 * HEADS
    gram, halo, grad_attended = pl.pallas_call(
        lambda *refs: loss_kernel(coeff, variables, *refs),
        grid=(1,),
        in_specs=[
            whole((members, VROWS, node_rows)),
            whole((VROWS, node_rows)),
            whole((VROWS, node_rows)),
            whole((1, node_rows)),
            whole((node_rows, width)),
            pl.BlockSpec((width, LANES), lambda i: (0, 3 * width // LANES)),
            whole((node_rows, width)),
        ],
        out_specs=[
            whole((width, LANES)),
            whole((payload, node_rows)),
            whole((node_rows, width)),
        ],
        out_shape=[
            shape((width, LANES), b16),
            shape((payload, node_rows), b16),
            shape((node_rows, width), b16),
        ],
        compiler_params=params,
        name="crps",
    )(others, pred, truth, area_weight[None], attended, full, lse)

    halo_low = shifted(halo, "node", 1)
    halo_high = shifted(halo, "node", -1)
    parts = lax.all_to_all(gram.reshape(members, rows, LANES), "ens", 0, 0, tiled=True)
    part = jnp.sum(parts.astype(f32), 0)
    parts = lax.all_to_all(
        jnp.broadcast_to(part[None], (shards,) + part.shape), "node", 0, 0, tiled=True
    )
    total = jnp.sum(parts, 0)
    grad_out_proj = lax.dot_general(
        total[:, :variables],
        w_decode.astype(f32),
        (((1,), (1,)), ((), ())),
        preferred_element_type=f32,
    )
    loss = jnp.sum(total[0, variables : variables + 3]) / (members * node_rows * shards * variables)

    grad_query, key_part, value_part = pl.pallas_call(
        lambda *refs: own_kernel(scale, *refs),
        grid=(steps,),
        in_specs=[
            blocks(node_rows, HALO // node_rows),
            blocks(span),
            blocks(span),
            blocks(node_rows),
            blocks(node_rows),
        ],
        out_specs=[blocks(node_rows)] * 3,
        out_shape=[
            shape((node_rows, width), b16),
            shape((node_rows, width), f32),
            shape((node_rows, width), f32),
        ],
        compiler_params=params,
        name="own_queries",
    )(queries, keys, values, grad_attended, lse)

    (grad_hidden,) = pl.pallas_call(
        lambda *refs: halo_kernel(scale, *refs),
        grid=(steps,),
        in_specs=[
            whole((payload, node_rows)),
            whole((payload, node_rows)),
            blocks(HALO, 0),
            blocks(HALO, 2),
            blocks(node_rows, 1),
            blocks(node_rows, 1),
            blocks(node_rows),
            blocks(node_rows),
            blocks(node_rows),
            columns(0),
            columns(1),
            columns(2),
            mixed_block,
            own_block,
            whole((node_rows, width)),
            whole((node_rows, 1)),
            whole((1, width)),
            whole((payload, node_rows)),
            whole((width, LANES)),
        ],
        out_specs=[own_block],
        out_shape=[shape((1, node_rows, width), b16)],
        scratch_shapes=[
            pltpu.VMEM((2 * HALO, LANES), b16),
            pltpu.VMEM((2, HEADS, 2 * HALO), f32),
            pltpu.VMEM((node_rows, width), f32),
        ],
        compiler_params=params,
        name="neighbour_queries",
    )(
        halo_low, halo_high, queries, queries, keys, values, grad_query, key_part, value_part,
        full, full, full, full, hidden, forcing, inverse_rms, norm_gain[None], halo, decode,
    )
    return (grad_hidden, grad_out_proj, loss)


def solution(mesh):
    placed = (
        P("ens", "node", None),
        P("node", None),
        P(),
        P("ens", None),
        P("ens", None),
        P("ens", None),
        P("ens", None),
        P(),
        P(None, "node"),
        P("node"),
    )
    return jax.shard_map(
        per_device,
        mesh=mesh,
        in_specs=placed,
        out_specs=(P("ens", "node", None), P("ens", None), P()),
        check_vma=False,
    )
```

```python
import math

import jax
import jax.numpy as jnp
from jax import lax
from jax.experimental import pallas as pl
from jax.experimental.pallas import tpu as pltpu
from jax.sharding import PartitionSpec as P

HEADS = 16
HALO = 128
LANES = 128
STEP = 256
VROWS = 112
SIDE = 4
RING_Z = 8
RING_Y = 8
HOPS = (0, SIDE - 1, 1, 2)


ALPHA = 0.95
KAPPA = 0.25
EPS_NORM = 1e-05
FAR = -1e30

f32 = jnp.float32
b16 = jnp.bfloat16


def nn(a, b):
    return lax.dot_general(a, b, (((1,), (0,)), ((), ())), preferred_element_type=f32)


def nt(a, b):
    return lax.dot_general(a, b, (((1,), (1,)), ((), ())), preferred_element_type=f32)


def tn(a, b):
    return lax.dot_general(a, b, (((0,), (0,)), ((), ())), preferred_element_type=f32)


def whole(shape):
    return pl.BlockSpec(shape, lambda i: (0,) * len(shape))


def head_masks(value):
    lane = lax.broadcasted_iota(jnp.int32, (1, LANES), 1)
    first = jnp.where(lane < LANES // 2, value, 0.0).astype(b16)
    second = jnp.where(lane < LANES // 2, 0.0, value).astype(b16)
    return first, second


def window_mask(rows, span):
    offset = lax.broadcasted_iota(jnp.int32, (rows, span), 1) - lax.broadcasted_iota(
        jnp.int32, (rows, span), 0
    )
    return (offset >= 0) & (offset <= 2 * HALO)


def split_bf16(value, pieces):
    out = []
    for _ in range(pieces):
        piece = value.astype(b16)
        out.append(piece)
        value = value - piece.astype(f32)
    return out


def forward_kernel(scale, place, low, own, high, hidden, forcing, decode, *refs):
    pieces, refs = refs[: 2 * len(HOPS)], refs[2 * len(HOPS) :]
    queries, keys, values, attended, lse, pred, full, normed, total, weights, load, store = refs
    step = pl.program_id(0)
    rows = own.shape[0]
    span = rows + 2 * HALO
    x, z, core = place[0], place[1], place[2]
    side = len(HOPS)
    block = pieces[0].shape[0] // side

    def loads():
        copies = []
        for mine in (True, False):
            which = core if mine else 1 - core
            for outer, far in enumerate(HOPS):
                piece = pieces[outer if mine else side + outer]
                for inner, near in enumerate(HOPS):
                    along_x = jnp.where(which == 0, near, far)
                    along_z = jnp.where(which == 0, far, near)
                    chip = lax.rem(x + along_x, side) * side + lax.rem(z + along_z, side)
                    copies.append(
                        pltpu.make_async_copy(
                            piece.at[pl.ds(inner * block, block)],
                            weights.at[which, pl.ds(chip * block, block)],
                            load.at[(0 if mine else side * side) + outer * side + inner],
                        )
                    )
        return copies

    @pl.when(step == 0)
    def _():
        copies = loads()
        for copy in copies:
            copy.start()
        for copy in copies:
            copy.wait()
        pltpu.make_async_copy(weights, full, store.at[0]).start()

    @pl.when(step == 0)
    def _():
        normed[:HALO] = low[...]
        normed[HALO : HALO + rows] = own[...]
        normed[HALO + rows :] = high[...]
        total[...] = nn(hidden[0], decode[...]) + nn(forcing[...], decode[...])

    field = normed[...]
    per_half = pl.num_programs(0) // 2
    half = step // per_half
    at = (step - half * per_half) * STEP
    third = per_half * STEP
    for index, out in enumerate((queries, keys, values)):
        cols = pl.ds(pl.multiple_of(index * third + at, STEP), STEP)
        out[...] = nn(field, weights[half, :, cols]).astype(b16)
    mixed = weights[0, pl.ds(pl.multiple_of(step * STEP, STEP), STEP), 3 * third :]
    window = window_mask(rows, span)
    masks = head_masks(scale)
    lower = lax.broadcasted_iota(jnp.int32, (rows, LANES), 1) < LANES // 2
    for pair in range(STEP // LANES):
        cols = slice(pair * LANES, (pair + 1) * LANES)
        query = queries[HALO : HALO + rows, cols]
        key = keys[:, cols]
        value = values[:, cols]
        outs, stats = [], []
        for mask in masks:
            scores = jnp.where(window, nt(query * mask, key), FAR)
            top = jnp.max(scores, -1, keepdims=True)
            expo = jnp.exp(scores - top)
            norm = jnp.sum(expo, -1, keepdims=True)
            probs = (expo * (1.0 / norm)).astype(b16)
            outs.append(nn(probs, value))
            stats.append(top + jnp.log(norm))
        attended[:, cols] = jnp.where(lower, outs[0], outs[1]).astype(b16)
        lse[:, cols] = jnp.where(lower, stats[0], stats[1])
    total[...] += nn(attended[...], mixed)

    @pl.when(step == pl.num_programs(0) - 1)
    def _():
        pltpu.make_async_copy(weights, full, store.at[0]).wait()
        pred[...] = total[...].T[:VROWS].astype(b16)


def loss_kernel(
    coeff, variables, others, pred, targets, weight, attended, mixed, lse,
    gram, halo, grad_attended,
):
    own = pred[...].astype(f32)
    rows = attended.shape[0]
    width = attended.shape[1]

    def member(index, carry):
        pair_abs, pair_slope = carry
        delta = own - others[index].astype(f32)
        square = delta * delta + KAPPA * KAPPA
        inverse = lax.rsqrt(square)
        return pair_abs + (square * inverse - KAPPA), pair_slope + delta * inverse

    zero = jnp.zeros((VROWS, LANES), f32)
    pair_abs, pair_slope = lax.fori_loop(0, others.shape[0], member, (zero, zero), unroll=4)
    delta = own - targets[...].astype(f32)
    square = delta * delta + KAPPA * KAPPA
    inverse = lax.rsqrt(square)
    real = lax.broadcasted_iota(jnp.int32, (VROWS, LANES), 0) < variables
    scale = weight[...]
    entries = jnp.where(real, scale * (square * inverse - KAPPA - coeff * pair_abs), 0.0)
    loss = jnp.sum(jnp.sum(entries, 0, keepdims=True), 1, keepdims=True)
    grad = jnp.where(real, scale * (delta * inverse - 2.0 * coeff * pair_slope), 0.0)
    grad_b = grad.astype(b16)
    halo[:VROWS] = grad_b
    grad_full = jnp.concatenate([grad, jnp.zeros((LANES - VROWS, LANES), f32)], 0)
    grad_t = grad_full.T.astype(b16)
    parts = nn(grad_full.astype(b16), attended[...])
    parts = parts.T
    column = lax.broadcasted_iota(jnp.int32, (width, LANES), 1)
    for index, piece in enumerate(split_bf16(loss, 3)):
        parts = jnp.where(column == variables + index, piece.astype(f32), parts)
    gram[...] = parts.astype(b16)
    grad_att = nt(grad_t, mixed[0]).astype(b16)
    grad_attended[...] = grad_att
    size = width // HEADS
    head = lax.broadcasted_iota(jnp.int32, (HEADS, width), 0)
    feature = lax.broadcasted_iota(jnp.int32, (HEADS, width), 1)
    inside = jnp.where((feature >= head * size) & (feature < (head + 1) * size), 1.0, 0.0)
    chosen = jnp.where(feature == head * size, 1.0, 0.0).astype(b16)
    inside = inside.astype(b16)
    product = grad_att.astype(f32) * attended[...].astype(f32)
    row_delta = sum(nt(inside, piece) for piece in split_bf16(product, 2))
    row_lse = sum(nt(chosen, piece) for piece in split_bf16(lse[...], 3))
    at = VROWS
    for piece in split_bf16(row_delta, 2) + split_bf16(row_lse, 3):
        halo[at : at + HEADS] = piece
        at += HEADS


def own_kernel(scale, query, keys, values, grad_att, lse, grad_query, grad_key, grad_value):
    rows = query.shape[0]
    span = keys.shape[0]
    window = window_mask(rows, span)
    scaled = head_masks(scale)
    plain = head_masks(1.0)
    center = slice(HALO, HALO + rows)
    for pair in range(STEP // LANES):
        cols = slice(pair * LANES, (pair + 1) * LANES)
        q, k, v, g = query[:, cols], keys[:, cols], values[:, cols], grad_att[:, cols]
        stats = lse[:, cols]
        d_query = d_key = d_value = None
        for half in range(2):
            q_half = q * scaled[half]
            g_half = g * plain[half]
            at = half * (LANES // 2)
            probs = jnp.where(window, jnp.exp(nt(q_half, k) - stats[:, at : at + 1]), 0.0)
            d_probs = nt(g_half, v)
            delta = jnp.sum(probs * d_probs, -1, keepdims=True)
            d_scores = (probs * (d_probs - delta)).astype(b16)
            probs = probs.astype(b16)
            dq = nn(d_scores, k * scaled[half])
            dk = tn(d_scores[:, center], q_half)
            dv = tn(probs[:, center], g_half)
            d_query = dq if d_query is None else d_query + dq
            d_key = dk if d_key is None else d_key + dk
            d_value = dv if d_value is None else d_value + dv
        grad_query[:, cols] = d_query.astype(b16)
        grad_key[:, cols] = d_key
        grad_value[:, cols] = d_value


def halo_kernel(
    scale, low, high, query_low, query_high, keys, values, grad_query, key_part, value_part,
    wq, wk, wv, mixed, hidden, forcing, inverse_rms, gain, halo, decode,
    grad_hidden, grad_t, stats, total,
):
    step = pl.program_id(0)
    rows = keys.shape[0]

    @pl.when(step == 0)
    def _():
        zero = jnp.zeros((LANES - VROWS, LANES), b16)
        for side, part in enumerate((low, high)):
            grad = jnp.concatenate([part[:VROWS], zero], 0)
            grad_t[side * HALO : (side + 1) * HALO] = grad.astype(f32).T.astype(b16)
            at = slice(side * HALO, (side + 1) * HALO)
            pieces = [
                part[VROWS + HEADS * n : VROWS + HEADS * (n + 1)].astype(f32) for n in range(5)
            ]
            stats[0, :, at] = pieces[0] + pieces[1]
            stats[1, :, at] = pieces[2] + pieces[3] + pieces[4]
        total[...] = jnp.zeros_like(total)

    key_at = lax.broadcasted_iota(jnp.int32, (rows, 2 * HALO), 0)
    query_at = lax.broadcasted_iota(jnp.int32, (rows, 2 * HALO), 1)
    window = ((query_at < HALO) & (query_at >= key_at)) | (
        (query_at >= HALO) & (query_at - HALO <= key_at)
    )
    scaled = head_masks(scale)
    plain = head_masks(1.0)
    grad_att = nt(grad_t[...], mixed[0]).astype(b16)
    per_step = 2 * (STEP // LANES)
    d_keys, d_values = [], []
    for pair in range(STEP // LANES):
        cols = slice(pair * LANES, (pair + 1) * LANES)
        q = jnp.concatenate([query_low[:, cols], query_high[:, cols]], 0)
        k, v, g = keys[:, cols], values[:, cols], grad_att[:, cols]
        d_key = key_part[:, cols]
        d_value = value_part[:, cols]
        for half in range(2):
            row = step * per_step + 2 * pair + half
            delta = stats[0, pl.ds(row, 1), :]
            lse = stats[1, pl.ds(row, 1), :]
            probs = jnp.where(window, jnp.exp(nt(k * scaled[half], q) - lse), 0.0)
            d_probs = nt(v * plain[half], g)
            d_scores = (probs * (d_probs - delta)).astype(b16)
            d_key = d_key + nn(d_scores, q * scaled[half])
            d_value = d_value + nn(probs.astype(b16), g * plain[half])
        d_keys.append(d_key.astype(b16))
        d_values.append(d_value.astype(b16))
    total[...] += (
        nt(grad_query[...], wq[0])
        + nt(jnp.concatenate(d_keys, 1), wk[0])
        + nt(jnp.concatenate(d_values, 1), wv[0])
    )

    @pl.when(step == pl.num_programs(0) - 1)
    def _():
        zero = jnp.zeros((LANES - VROWS, LANES), b16)
        own = jnp.concatenate([halo[:VROWS], zero], 0).astype(f32).T.astype(b16)
        grad_resid = nt(own, decode[...])
        xfield = hidden[0].astype(f32) + forcing[...].astype(f32)
        inverse = inverse_rms[...]
        grad = gain[...] * total[...]
        mean = jnp.mean(xfield * grad, -1, keepdims=True)
        result = grad_resid + inverse * grad - xfield * (inverse * inverse * inverse * mean)
        grad_hidden[0] = result.astype(b16)


def shifted(value, axis, steps):
    count = lax.axis_size(axis)
    pairs = [(source, (source + steps) % count) for source in range(count)]
    return lax.ppermute(value, axis, pairs)


def permute(value, moves):
    pairs = []
    for x in range(SIDE):
        for z in range(RING_Z):
            for y in range(RING_Y):
                for core in range(2):
                    dx, dz, dc = moves[core]
                    at = (x, z, core)
                    to = ((x + dx) % SIDE, (z + dz) % RING_Z, core ^ dc)
                    pairs.append(
                        tuple(
                            ((px * SIDE + pz % SIDE) * 2 + pc) * 2 * RING_Y + pz // SIDE * RING_Y + y
                            for px, pz, pc in (at, to)
                        )
                    )
    return lax.ppermute(value, ("ens", "node"), pairs)


def ring(value, along):
    out = [value]
    for hop in (1, -1, -2):
        moves = [(hop, 0, 0) if axis == 0 else (0, hop, 0) for axis in along]
        out.append(permute(value, moves))
    return out


def swapped(value):
    return permute(value, [(0, 0, 1)] * 2)


def gathered(w_query, w_key, w_value, mixed, core):
    half = w_query.shape[1] // 2
    both = jnp.stack(
        [
            jnp.concatenate(
                [w[:, at : at + half] for w in (w_query, w_key, w_value)] + [mixed], 1
            )
            for at in (0, half)
        ]
    )
    first = core == 0
    keep = jnp.where(first, both[0], both[1])
    other = swapped(jnp.where(first, both[1], both[0]))
    block = jnp.where(
        first, jnp.concatenate([keep, other], 0), jnp.concatenate([other, keep], 0)
    )
    row = jnp.concatenate(ring(block, (0, 1)), 0)
    mine = ring(row, (1, 0))
    return mine + [swapped(piece) for piece in mine]


def per_device(
    hidden, forcing, norm_gain, w_query, w_key, w_value, w_out, w_decode, targets, area_weight
):
    node_rows = hidden.shape[1]
    width = hidden.shape[2]
    head_size = width // HEADS
    span = node_rows + 2 * HALO
    scale = 1.0 / math.sqrt(head_size)
    members = lax.axis_size("ens")
    shards = lax.axis_size("node")
    rows = w_query.shape[0]
    variables = w_decode.shape[1]
    steps = width // STEP
    shape = jax.ShapeDtypeStruct
    params = pltpu.CompilerParams(
        dimension_semantics=("arbitrary",), vmem_limit_bytes=48 * 1024 * 1024
    )
    decode = jnp.pad(w_decode, ((0, 0), (0, LANES - variables)))
    mixed = jnp.dot(w_out, decode, preferred_element_type=f32).astype(b16)
    position = lax.axis_index("ens")
    core = position % 2
    place = jnp.stack([position // (2 * SIDE), position // 2 % SIDE, core]).astype(jnp.int32)
    pieces = gathered(w_query, w_key, w_value, mixed, core)
    half_width = pieces[0].shape[1]
    xfield = hidden[0].astype(f32) + forcing.astype(f32)
    inverse_rms = lax.rsqrt(jnp.mean(xfield * xfield, -1, keepdims=True) + EPS_NORM)
    normed = (xfield * inverse_rms * norm_gain).astype(b16)
    low = shifted(normed, "node", 1)
    high = shifted(normed, "node", -1)

    def columns(at):
        per_half = steps // 2
        return pl.BlockSpec(
            (1, width, STEP), lambda i: (i // per_half, 0, at * per_half + i % per_half)
        )

    def blocks(height, at=0):
        return pl.BlockSpec((height, STEP), lambda i: (at, i))

    mixed_at = half_width // LANES - 1
    mixed_block = pl.BlockSpec((1, STEP, LANES), lambda i: (0, i, mixed_at))
    anywhere = pl.BlockSpec(memory_space=pl.ANY)
    own_block = whole((1, node_rows, width))
    queries, keys, values, attended, lse, pred, full = pl.pallas_call(
        lambda *refs: forward_kernel(scale, *refs),
        grid=(steps,),
        in_specs=[
            pl.BlockSpec(memory_space=pltpu.SMEM),
            whole((HALO, width)),
            whole((node_rows, width)),
            whole((HALO, width)),
            own_block,
            whole((node_rows, width)),
            whole((width, LANES)),
        ]
        + [anywhere] * len(pieces),
        out_specs=[
            blocks(span),
            blocks(span),
            blocks(span),
            blocks(node_rows),
            blocks(node_rows),
            whole((VROWS, node_rows)),
            anywhere,
        ],
        out_shape=[
            shape((span, width), b16),
            shape((span, width), b16),
            shape((span, width), b16),
            shape((node_rows, width), b16),
            shape((node_rows, width), f32),
            shape((VROWS, node_rows), b16),
            shape((2, width, half_width), b16),
        ],
        scratch_shapes=[
            pltpu.VMEM((span, width), b16),
            pltpu.VMEM((node_rows, LANES), f32),
            pltpu.VMEM((2, width, half_width), b16),
            pltpu.SemaphoreType.DMA((len(pieces) * SIDE,)),
            pltpu.SemaphoreType.DMA((1,)),
        ],
        compiler_params=params,
        name="forward",
    )(place, low, normed, high, hidden, forcing, decode, *pieces)

    others = lax.all_to_all(
        jnp.broadcast_to(pred[None], (members,) + pred.shape), "ens", 0, 0, tiled=True
    )
    eps = (1.0 - ALPHA) / members
    coeff = (1.0 - eps) / (2.0 * (members - 1))
    truth = jnp.pad(targets, ((0, VROWS - variables), (0, 0)))
    payload = VROWS + 5 * HEADS
    gram, halo, grad_attended = pl.pallas_call(
        lambda *refs: loss_kernel(coeff, variables, *refs),
        grid=(1,),
        in_specs=[
            whole((members, VROWS, node_rows)),
            whole((VROWS, node_rows)),
            whole((VROWS, node_rows)),
            whole((1, node_rows)),
            whole((node_rows, width)),
            pl.BlockSpec((1, width, LANES), lambda i: (0, 0, mixed_at)),
            whole((node_rows, width)),
        ],
        out_specs=[
            whole((width, LANES)),
            whole((payload, node_rows)),
            whole((node_rows, width)),
        ],
        out_shape=[
            shape((width, LANES), b16),
            shape((payload, node_rows), b16),
            shape((node_rows, width), b16),
        ],
        compiler_params=params,
        name="crps",
    )(others, pred, truth, area_weight[None], attended, full, lse)

    halo_low = shifted(halo, "node", 1)
    halo_high = shifted(halo, "node", -1)
    parts = lax.all_to_all(gram.reshape(members, rows, LANES), "ens", 0, 0, tiled=True)
    part = jnp.sum(parts.astype(f32), 0)
    parts = lax.all_to_all(
        jnp.broadcast_to(part[None], (shards,) + part.shape), "node", 0, 0, tiled=True
    )
    total = jnp.sum(parts, 0)
    grad_out_proj = lax.dot_general(
        total[:, :variables],
        w_decode.astype(f32),
        (((1,), (1,)), ((), ())),
        preferred_element_type=f32,
    )
    loss = jnp.sum(total[0, variables : variables + 3]) / (members * node_rows * shards * variables)

    grad_query, key_part, value_part = pl.pallas_call(
        lambda *refs: own_kernel(scale, *refs),
        grid=(steps,),
        in_specs=[
            blocks(node_rows, HALO // node_rows),
            blocks(span),
            blocks(span),
            blocks(node_rows),
            blocks(node_rows),
        ],
        out_specs=[blocks(node_rows)] * 3,
        out_shape=[
            shape((node_rows, width), b16),
            shape((node_rows, width), f32),
            shape((node_rows, width), f32),
        ],
        compiler_params=params,
        name="own_queries",
    )(queries, keys, values, grad_attended, lse)

    (grad_hidden,) = pl.pallas_call(
        lambda *refs: halo_kernel(scale, *refs),
        grid=(steps,),
        in_specs=[
            whole((payload, node_rows)),
            whole((payload, node_rows)),
            blocks(HALO, 0),
            blocks(HALO, 2),
            blocks(node_rows, 1),
            blocks(node_rows, 1),
            blocks(node_rows),
            blocks(node_rows),
            blocks(node_rows),
            columns(0),
            columns(1),
            columns(2),
            mixed_block,
            own_block,
            whole((node_rows, width)),
            whole((node_rows, 1)),
            whole((1, width)),
            whole((payload, node_rows)),
            whole((width, LANES)),
        ],
        out_specs=[own_block],
        out_shape=[shape((1, node_rows, width), b16)],
        scratch_shapes=[
            pltpu.VMEM((2 * HALO, LANES), b16),
            pltpu.VMEM((2, HEADS, 2 * HALO), f32),
            pltpu.VMEM((node_rows, width), f32),
        ],
        compiler_params=params,
        name="neighbour_queries",
    )(
        halo_low, halo_high, queries, queries, keys, values, grad_query, key_part, value_part,
        full, full, full, full, hidden, forcing, inverse_rms, norm_gain[None], halo, decode,
    )
    return (grad_hidden, grad_out_proj, loss)


def solution(mesh):
    placed = (
        P("ens", "node", None),
        P("node", None),
        P(),
        P("ens", None),
        P("ens", None),
        P("ens", None),
        P("ens", None),
        P(),
        P(None, "node"),
        P("node"),
    )
    return jax.shard_map(
        per_device,
        mesh=mesh,
        in_specs=placed,
        out_specs=(P("ens", "node", None), P("ens", None), P()),
        check_vma=False,
    )
```

```python
import math

import jax
import jax.numpy as jnp
from jax import lax
from jax.experimental import pallas as pl
from jax.experimental.pallas import tpu as pltpu
from jax.sharding import PartitionSpec as P

HEADS = 16
HALO = 128
LANES = 128
STEP = 256
VROWS = 112
SIDE = 4
RING_Z = 8
RING_Y = 8
HOPS = (0, SIDE - 1, 1, 2)


ALPHA = 0.95
KAPPA = 0.25
EPS_NORM = 1e-05
FAR = -1e30

f32 = jnp.float32
b16 = jnp.bfloat16


def nn(a, b):
    return lax.dot_general(a, b, (((1,), (0,)), ((), ())), preferred_element_type=f32)


def nt(a, b):
    return lax.dot_general(a, b, (((1,), (1,)), ((), ())), preferred_element_type=f32)


def tn(a, b):
    return lax.dot_general(a, b, (((0,), (0,)), ((), ())), preferred_element_type=f32)


def whole(shape):
    return pl.BlockSpec(shape, lambda i: (0,) * len(shape))


def head_masks(value):
    lane = lax.broadcasted_iota(jnp.int32, (1, LANES), 1)
    first = jnp.where(lane < LANES // 2, value, 0.0).astype(b16)
    second = jnp.where(lane < LANES // 2, 0.0, value).astype(b16)
    return first, second


def window_mask(rows, span):
    offset = lax.broadcasted_iota(jnp.int32, (rows, span), 1) - lax.broadcasted_iota(
        jnp.int32, (rows, span), 0
    )
    return (offset >= 0) & (offset <= 2 * HALO)


def split_bf16(value, pieces):
    out = []
    for _ in range(pieces):
        piece = value.astype(b16)
        out.append(piece)
        value = value - piece.astype(f32)
    return out


def forward_kernel(scale, place, low, own, high, hidden, forcing, decode, *refs):
    pieces, refs = refs[: 2 * len(HOPS)], refs[2 * len(HOPS) :]
    queries, keys, values, attended, lse, pred, full, normed, total, weights, load, store = refs
    step = pl.program_id(0)
    rows = own.shape[0]
    span = rows + 2 * HALO
    x, z, core = place[0], place[1], place[2]
    side = len(HOPS)
    block = pieces[0].shape[0] // side

    def loads():
        copies = []
        for mine in (True, False):
            which = core if mine else 1 - core
            for outer, far in enumerate(HOPS):
                piece = pieces[outer if mine else side + outer]
                for inner, near in enumerate(HOPS):
                    along_x = jnp.where(which == 0, near, far)
                    along_z = jnp.where(which == 0, far, near)
                    chip = lax.rem(x + along_x, side) * side + lax.rem(z + along_z, side)
                    copies.append(
                        pltpu.make_async_copy(
                            piece.at[pl.ds(inner * block, block)],
                            weights.at[pl.ds((chip * 2 + which) * block, block)],
                            load.at[(0 if mine else side * side) + outer * side + inner],
                        )
                    )
        return copies

    @pl.when(step == 0)
    def _():
        copies = loads()
        for copy in copies:
            copy.start()
        for copy in copies:
            copy.wait()
        pltpu.make_async_copy(weights, full, store.at[0]).start()

    @pl.when(step == 0)
    def _():
        normed[:HALO] = low[...]
        normed[HALO : HALO + rows] = own[...]
        normed[HALO + rows :] = high[...]
        total[...] = nn(hidden[0], decode[...]) + nn(forcing[...], decode[...])

    field = normed[...]
    width = own.shape[1]
    at = step * STEP
    for index, out in enumerate((queries, keys, values)):
        cols = pl.ds(pl.multiple_of(index * width + at, STEP), STEP)
        out[...] = nn(field, weights[:, cols]).astype(b16)
    mixed = weights[pl.ds(pl.multiple_of(at, STEP), STEP), 3 * width :]
    window = window_mask(rows, span)
    masks = head_masks(scale)
    lower = lax.broadcasted_iota(jnp.int32, (rows, LANES), 1) < LANES // 2
    for pair in range(STEP // LANES):
        cols = slice(pair * LANES, (pair + 1) * LANES)
        query = queries[HALO : HALO + rows, cols]
        key = keys[:, cols]
        value = values[:, cols]
        outs, stats = [], []
        for mask in masks:
            scores = jnp.where(window, nt(query * mask, key), FAR)
            top = jnp.max(scores, -1, keepdims=True)
            expo = jnp.exp(scores - top)
            norm = jnp.sum(expo, -1, keepdims=True)
            probs = (expo * (1.0 / norm)).astype(b16)
            outs.append(nn(probs, value))
            stats.append(top + jnp.log(norm))
        attended[:, cols] = jnp.where(lower, outs[0], outs[1]).astype(b16)
        lse[:, cols] = jnp.where(lower, stats[0], stats[1])
    total[...] += nn(attended[...], mixed)

    @pl.when(step == pl.num_programs(0) - 1)
    def _():
        pltpu.make_async_copy(weights, full, store.at[0]).wait()
        pred[...] = total[...].T[:VROWS].astype(b16)


def loss_kernel(
    coeff, variables, others, theirs, pred, targets, weight, attended, mixed, lse,
    gram, halo, grad_attended,
):
    own = pred[...].astype(f32)
    rows = attended.shape[0]
    width = attended.shape[1]

    def member(index, carry):
        pair_abs, pair_slope = carry
        for part in (others, theirs):
            delta = own - part[index].astype(f32)
            square = delta * delta + KAPPA * KAPPA
            inverse = lax.rsqrt(square)
            pair_abs = pair_abs + (square * inverse - KAPPA)
            pair_slope = pair_slope + delta * inverse
        return pair_abs, pair_slope

    zero = jnp.zeros((VROWS, LANES), f32)
    pair_abs, pair_slope = lax.fori_loop(0, others.shape[0], member, (zero, zero), unroll=2)
    delta = own - targets[...].astype(f32)
    square = delta * delta + KAPPA * KAPPA
    inverse = lax.rsqrt(square)
    real = lax.broadcasted_iota(jnp.int32, (VROWS, LANES), 0) < variables
    scale = weight[...]
    entries = jnp.where(real, scale * (square * inverse - KAPPA - coeff * pair_abs), 0.0)
    loss = jnp.sum(jnp.sum(entries, 0, keepdims=True), 1, keepdims=True)
    grad = jnp.where(real, scale * (delta * inverse - 2.0 * coeff * pair_slope), 0.0)
    grad_b = grad.astype(b16)
    halo[:VROWS] = grad_b
    grad_full = jnp.concatenate([grad, jnp.zeros((LANES - VROWS, LANES), f32)], 0)
    grad_t = grad_full.T.astype(b16)
    parts = nn(grad_full.astype(b16), attended[...])
    parts = parts.T
    column = lax.broadcasted_iota(jnp.int32, (width, LANES), 1)
    for index, piece in enumerate(split_bf16(loss, 3)):
        parts = jnp.where(column == variables + index, piece.astype(f32), parts)
    gram[...] = parts.astype(b16)
    grad_att = nt(grad_t, mixed[...]).astype(b16)
    grad_attended[...] = grad_att
    size = width // HEADS
    head = lax.broadcasted_iota(jnp.int32, (HEADS, width), 0)
    feature = lax.broadcasted_iota(jnp.int32, (HEADS, width), 1)
    inside = jnp.where((feature >= head * size) & (feature < (head + 1) * size), 1.0, 0.0)
    chosen = jnp.where(feature == head * size, 1.0, 0.0).astype(b16)
    inside = inside.astype(b16)
    product = grad_att.astype(f32) * attended[...].astype(f32)
    row_delta = sum(nt(inside, piece) for piece in split_bf16(product, 2))
    row_lse = sum(nt(chosen, piece) for piece in split_bf16(lse[...], 3))
    at = VROWS
    for piece in split_bf16(row_delta, 2) + split_bf16(row_lse, 3):
        halo[at : at + HEADS] = piece
        at += HEADS


def own_kernel(scale, query, keys, values, grad_att, lse, grad_query, grad_key, grad_value):
    rows = query.shape[0]
    span = keys.shape[0]
    window = window_mask(rows, span)
    scaled = head_masks(scale)
    plain = head_masks(1.0)
    center = slice(HALO, HALO + rows)
    for pair in range(STEP // LANES):
        cols = slice(pair * LANES, (pair + 1) * LANES)
        q, k, v, g = query[:, cols], keys[:, cols], values[:, cols], grad_att[:, cols]
        stats = lse[:, cols]
        d_query = d_key = d_value = None
        for half in range(2):
            q_half = q * scaled[half]
            g_half = g * plain[half]
            at = half * (LANES // 2)
            probs = jnp.where(window, jnp.exp(nt(q_half, k) - stats[:, at : at + 1]), 0.0)
            d_probs = nt(g_half, v)
            delta = jnp.sum(probs * d_probs, -1, keepdims=True)
            d_scores = (probs * (d_probs - delta)).astype(b16)
            probs = probs.astype(b16)
            dq = nn(d_scores, k * scaled[half])
            dk = tn(d_scores[:, center], q_half)
            dv = tn(probs[:, center], g_half)
            d_query = dq if d_query is None else d_query + dq
            d_key = dk if d_key is None else d_key + dk
            d_value = dv if d_value is None else d_value + dv
        grad_query[:, cols] = d_query.astype(b16)
        grad_key[:, cols] = d_key
        grad_value[:, cols] = d_value


def halo_kernel(
    scale, low, high, query_low, query_high, keys, values, grad_query, key_part, value_part,
    wq, wk, wv, mixed, hidden, forcing, inverse_rms, gain, halo, decode,
    grad_hidden, grad_t, stats, total,
):
    step = pl.program_id(0)
    rows = keys.shape[0]

    @pl.when(step == 0)
    def _():
        zero = jnp.zeros((LANES - VROWS, LANES), b16)
        for side, part in enumerate((low, high)):
            grad = jnp.concatenate([part[:VROWS], zero], 0)
            grad_t[side * HALO : (side + 1) * HALO] = grad.astype(f32).T.astype(b16)
            at = slice(side * HALO, (side + 1) * HALO)
            pieces = [
                part[VROWS + HEADS * n : VROWS + HEADS * (n + 1)].astype(f32) for n in range(5)
            ]
            stats[0, :, at] = pieces[0] + pieces[1]
            stats[1, :, at] = pieces[2] + pieces[3] + pieces[4]
        total[...] = jnp.zeros_like(total)

    key_at = lax.broadcasted_iota(jnp.int32, (rows, 2 * HALO), 0)
    query_at = lax.broadcasted_iota(jnp.int32, (rows, 2 * HALO), 1)
    window = ((query_at < HALO) & (query_at >= key_at)) | (
        (query_at >= HALO) & (query_at - HALO <= key_at)
    )
    scaled = head_masks(scale)
    plain = head_masks(1.0)
    grad_att = nt(grad_t[...], mixed[...]).astype(b16)
    per_step = 2 * (STEP // LANES)
    d_keys, d_values = [], []
    for pair in range(STEP // LANES):
        cols = slice(pair * LANES, (pair + 1) * LANES)
        q = jnp.concatenate([query_low[:, cols], query_high[:, cols]], 0)
        k, v, g = keys[:, cols], values[:, cols], grad_att[:, cols]
        d_key = key_part[:, cols]
        d_value = value_part[:, cols]
        for half in range(2):
            row = step * per_step + 2 * pair + half
            delta = stats[0, pl.ds(row, 1), :]
            lse = stats[1, pl.ds(row, 1), :]
            probs = jnp.where(window, jnp.exp(nt(k * scaled[half], q) - lse), 0.0)
            d_probs = nt(v * plain[half], g)
            d_scores = (probs * (d_probs - delta)).astype(b16)
            d_key = d_key + nn(d_scores, q * scaled[half])
            d_value = d_value + nn(probs.astype(b16), g * plain[half])
        d_keys.append(d_key.astype(b16))
        d_values.append(d_value.astype(b16))
    total[...] += (
        nt(grad_query[...], wq[...])
        + nt(jnp.concatenate(d_keys, 1), wk[...])
        + nt(jnp.concatenate(d_values, 1), wv[...])
    )

    @pl.when(step == pl.num_programs(0) - 1)
    def _():
        zero = jnp.zeros((LANES - VROWS, LANES), b16)
        own = jnp.concatenate([halo[:VROWS], zero], 0).astype(f32).T.astype(b16)
        grad_resid = nt(own, decode[...])
        xfield = hidden[0].astype(f32) + forcing[...].astype(f32)
        inverse = inverse_rms[...]
        grad = gain[...] * total[...]
        mean = jnp.mean(xfield * grad, -1, keepdims=True)
        result = grad_resid + inverse * grad - xfield * (inverse * inverse * inverse * mean)
        grad_hidden[0] = result.astype(b16)


def shifted(value, axis, steps):
    count = lax.axis_size(axis)
    pairs = [(source, (source + steps) % count) for source in range(count)]
    return lax.ppermute(value, axis, pairs)


def permute(value, moves):
    pairs = []
    for x in range(SIDE):
        for z in range(RING_Z):
            for y in range(RING_Y):
                for core in range(2):
                    dx, dz, dc = moves[core]
                    at = (x, z, core)
                    to = ((x + dx) % SIDE, (z + dz) % RING_Z, core ^ dc)
                    pairs.append(
                        tuple(
                            ((px * SIDE + pz % SIDE) * 2 + pc) * 2 * RING_Y + pz // SIDE * RING_Y + y
                            for px, pz, pc in (at, to)
                        )
                    )
    return lax.ppermute(value, ("ens", "node"), pairs)


def ring(value, along):
    out = [value]
    for hop in (1, -1, -2):
        moves = [(hop, 0, 0) if axis == 0 else (0, hop, 0) for axis in along]
        out.append(permute(value, moves))
    return out


def swapped(value):
    return permute(value, [(0, 0, 1)] * 2)


def gathered(packed):
    return ring(jnp.concatenate(ring(packed, (0, 1)), 0), (1, 0))


def everyone(value):
    value = value[None]
    for phase in range(2):
        groups = []
        for core in range(2):
            for fixed in range(SIDE):
                chips = [
                    step * SIDE + fixed if core == phase else fixed * SIDE + step
                    for step in range(SIDE)
                ]
                groups.append([2 * chip + core for chip in chips])
        spread = jnp.broadcast_to(value[None], (SIDE,) + value.shape)
        spread = spread.reshape((-1,) + value.shape[1:])
        value = lax.all_to_all(spread, "ens", 0, 0, tiled=True, axis_index_groups=groups)
    return value


def per_device(
    hidden, forcing, norm_gain, w_query, w_key, w_value, w_out, w_decode, targets, area_weight
):
    node_rows = hidden.shape[1]
    width = hidden.shape[2]
    head_size = width // HEADS
    span = node_rows + 2 * HALO
    scale = 1.0 / math.sqrt(head_size)
    members = lax.axis_size("ens")
    shards = lax.axis_size("node")
    rows = w_query.shape[0]
    variables = w_decode.shape[1]
    steps = width // STEP
    shape = jax.ShapeDtypeStruct

    def params(mebibytes):
        return pltpu.CompilerParams(
            dimension_semantics=("arbitrary",), vmem_limit_bytes=mebibytes * 1024 * 1024
        )

    def cost(us):
        return pl.CostEstimate(
            flops=us * 10**9, transcendentals=0, bytes_accessed=us * 3 * 10**6
        )
    decode = jnp.pad(w_decode, ((0, 0), (0, LANES - variables)))
    mixed = jnp.dot(w_out, decode, preferred_element_type=f32).astype(b16)
    position = lax.axis_index("ens")
    core = position % 2
    place = jnp.stack([position // (2 * SIDE), position // 2 % SIDE, core]).astype(jnp.int32)
    mine = gathered(jnp.concatenate([w_query, w_key, w_value, mixed], 1))
    xfield = hidden[0].astype(f32) + forcing.astype(f32)
    inverse_rms = lax.rsqrt(jnp.mean(xfield * xfield, -1, keepdims=True) + EPS_NORM)
    normed = (xfield * inverse_rms * norm_gain).astype(b16)
    low = shifted(normed, "node", 1)
    high = shifted(normed, "node", -1)
    mine[-1], low, high = lax.optimization_barrier((mine[-1], low, high))
    pieces = mine + [swapped(piece) for piece in mine]

    def columns(at):
        return pl.BlockSpec((width, STEP), lambda i: (0, at * steps + i))

    def blocks(height, at=0):
        return pl.BlockSpec((height, STEP), lambda i: (at, i))

    mixed_at = 3 * width // LANES
    packed_width = 3 * width + LANES
    mixed_block = pl.BlockSpec((STEP, LANES), lambda i: (i, mixed_at))
    anywhere = pl.BlockSpec(memory_space=pl.ANY)
    own_block = whole((1, node_rows, width))
    queries, keys, values, attended, lse, pred, full = pl.pallas_call(
        lambda *refs: forward_kernel(scale, *refs),
        grid=(steps,),
        in_specs=[
            pl.BlockSpec(memory_space=pltpu.SMEM),
            whole((HALO, width)),
            whole((node_rows, width)),
            whole((HALO, width)),
            own_block,
            whole((node_rows, width)),
            whole((width, LANES)),
        ]
        + [anywhere] * len(pieces),
        out_specs=[
            blocks(span),
            blocks(span),
            blocks(span),
            blocks(node_rows),
            blocks(node_rows),
            whole((VROWS, node_rows)),
            anywhere,
        ],
        out_shape=[
            shape((span, width), b16),
            shape((span, width), b16),
            shape((span, width), b16),
            shape((node_rows, width), b16),
            shape((node_rows, width), f32),
            shape((VROWS, node_rows), b16),
            shape((width, packed_width), b16),
        ],
        scratch_shapes=[
            pltpu.VMEM((span, width), b16),
            pltpu.VMEM((node_rows, LANES), f32),
            pltpu.VMEM((width, packed_width), b16),
            pltpu.SemaphoreType.DMA((len(pieces) * SIDE,)),
            pltpu.SemaphoreType.DMA((1,)),
        ],
        compiler_params=params(24),
        cost_estimate=cost(12),
        name="forward",
    )(place, low, normed, high, hidden, forcing, decode, *pieces)

    others = everyone(pred)
    theirs = swapped(others)
    eps = (1.0 - ALPHA) / members
    coeff = (1.0 - eps) / (2.0 * (members - 1))
    truth = jnp.pad(targets, ((0, VROWS - variables), (0, 0)))
    payload = VROWS + 5 * HEADS
    gram, halo, grad_attended = pl.pallas_call(
        lambda *refs: loss_kernel(coeff, variables, *refs),
        grid=(1,),
        in_specs=[
            whole(others.shape),
            whole(others.shape),
            whole((VROWS, node_rows)),
            whole((VROWS, node_rows)),
            whole((1, node_rows)),
            whole((node_rows, width)),
            pl.BlockSpec((width, LANES), lambda i: (0, mixed_at)),
            whole((node_rows, width)),
        ],
        out_specs=[
            whole((width, LANES)),
            whole((payload, node_rows)),
            whole((node_rows, width)),
        ],
        out_shape=[
            shape((width, LANES), b16),
            shape((payload, node_rows), b16),
            shape((node_rows, width), b16),
        ],
        compiler_params=params(12),
        cost_estimate=cost(3),
        name="crps",
    )(others, theirs, pred, truth, area_weight[None], attended, full, lse)

    halo_low = shifted(halo, "node", 1)
    halo_high = shifted(halo, "node", -1)
    parts = lax.all_to_all(gram.reshape(members, rows, LANES), "ens", 0, 0, tiled=True)
    part = jnp.sum(parts.astype(f32), 0)
    parts = lax.all_to_all(
        jnp.broadcast_to(part[None], (shards,) + part.shape), "node", 0, 0, tiled=True
    )
    total = jnp.sum(parts, 0)
    grad_out_proj = lax.dot_general(
        total[:, :variables],
        w_decode.astype(f32),
        (((1,), (1,)), ((), ())),
        preferred_element_type=f32,
    )
    loss = jnp.sum(total[0, variables : variables + 3]) / (members * node_rows * shards * variables)

    grad_query, key_part, value_part = pl.pallas_call(
        lambda *refs: own_kernel(scale, *refs),
        grid=(steps,),
        in_specs=[
            blocks(node_rows, HALO // node_rows),
            blocks(span),
            blocks(span),
            blocks(node_rows),
            blocks(node_rows),
        ],
        out_specs=[blocks(node_rows)] * 3,
        out_shape=[
            shape((node_rows, width), b16),
            shape((node_rows, width), f32),
            shape((node_rows, width), f32),
        ],
        compiler_params=params(12),
        cost_estimate=cost(6),
        name="own_queries",
    )(queries, keys, values, grad_attended, lse)

    (grad_hidden,) = pl.pallas_call(
        lambda *refs: halo_kernel(scale, *refs),
        grid=(steps,),
        in_specs=[
            whole((payload, node_rows)),
            whole((payload, node_rows)),
            blocks(HALO, 0),
            blocks(HALO, 2),
            blocks(node_rows, 1),
            blocks(node_rows, 1),
            blocks(node_rows),
            blocks(node_rows),
            blocks(node_rows),
            columns(0),
            columns(1),
            columns(2),
            mixed_block,
            own_block,
            whole((node_rows, width)),
            whole((node_rows, 1)),
            whole((1, width)),
            whole((payload, node_rows)),
            whole((width, LANES)),
        ],
        out_specs=[own_block],
        out_shape=[shape((1, node_rows, width), b16)],
        scratch_shapes=[
            pltpu.VMEM((2 * HALO, LANES), b16),
            pltpu.VMEM((2, HEADS, 2 * HALO), f32),
            pltpu.VMEM((node_rows, width), f32),
        ],
        compiler_params=params(16),
        cost_estimate=cost(9),
        name="neighbour_queries",
    )(
        halo_low, halo_high, queries, queries, keys, values, grad_query, key_part, value_part,
        full, full, full, full, hidden, forcing, inverse_rms, norm_gain[None], halo, decode,
    )
    return (grad_hidden, grad_out_proj, loss)


def solution(mesh):
    placed = (
        P("ens", "node", None),
        P("node", None),
        P(),
        P("ens", None),
        P("ens", None),
        P("ens", None),
        P("ens", None),
        P(),
        P(None, "node"),
        P("node"),
    )
    return jax.shard_map(
        per_device,
        mesh=mesh,
        in_specs=placed,
        out_specs=(P("ens", "node", None), P("ens", None), P()),
        check_vma=False,
    )
```

```python
import math

import jax
import jax.numpy as jnp
from jax import lax
from jax.experimental import pallas as pl
from jax.experimental.pallas import tpu as pltpu
from jax.sharding import PartitionSpec as P

HEADS = 16
HALO = 128
LANES = 128
STEP = 256
VROWS = 112
SIDE = 4
RING_Z = 8
RING_Y = 8
HOPS = (0, SIDE - 1, 1, 2)


ALPHA = 0.95
KAPPA = 0.25
EPS_NORM = 1e-05
FAR = -1e30

f32 = jnp.float32
b16 = jnp.bfloat16


def nn(a, b):
    return lax.dot_general(a, b, (((1,), (0,)), ((), ())), preferred_element_type=f32)


def nt(a, b):
    return lax.dot_general(a, b, (((1,), (1,)), ((), ())), preferred_element_type=f32)


def tn(a, b):
    return lax.dot_general(a, b, (((0,), (0,)), ((), ())), preferred_element_type=f32)


def whole(shape):
    return pl.BlockSpec(shape, lambda i: (0,) * len(shape))


def head_masks(value):
    lane = lax.broadcasted_iota(jnp.int32, (1, LANES), 1)
    first = jnp.where(lane < LANES // 2, value, 0.0).astype(b16)
    second = jnp.where(lane < LANES // 2, 0.0, value).astype(b16)
    return first, second


def window_mask(rows, span):
    offset = lax.broadcasted_iota(jnp.int32, (rows, span), 1) - lax.broadcasted_iota(
        jnp.int32, (rows, span), 0
    )
    return (offset >= 0) & (offset <= 2 * HALO)


def split_bf16(value, pieces):
    out = []
    for _ in range(pieces):
        piece = value.astype(b16)
        out.append(piece)
        value = value - piece.astype(f32)
    return out


def forward_kernel(scale, place, low, own, high, hidden, forcing, decode, *refs):
    pieces, refs = refs[: 2 * len(HOPS)], refs[2 * len(HOPS) :]
    queries, keys, values, attended, lse, pred, full, normed, total, weights, load, store = refs
    step = pl.program_id(0)
    rows = own.shape[0]
    span = rows + 2 * HALO
    x, z, core = place[0], place[1], place[2]
    side = len(HOPS)
    block = pieces[0].shape[0] // side

    def loads():
        copies = []
        for mine in (True, False):
            which = core if mine else 1 - core
            for outer, far in enumerate(HOPS):
                piece = pieces[outer if mine else side + outer]
                for inner, near in enumerate(HOPS):
                    along_x = jnp.where(which == 0, near, far)
                    along_z = jnp.where(which == 0, far, near)
                    chip = lax.rem(x + along_x, side) * side + lax.rem(z + along_z, side)
                    copies.append(
                        pltpu.make_async_copy(
                            piece.at[pl.ds(inner * block, block)],
                            weights.at[pl.ds((chip * 2 + which) * block, block)],
                            load.at[(0 if mine else side * side) + outer * side + inner],
                        )
                    )
        return copies

    @pl.when(step == 0)
    def _():
        copies = loads()
        for copy in copies:
            copy.start()
        for copy in copies:
            copy.wait()
        pltpu.make_async_copy(weights, full, store.at[0]).start()

    @pl.when(step == 0)
    def _():
        normed[:HALO] = low[...]
        normed[HALO : HALO + rows] = own[...]
        normed[HALO + rows :] = high[...]
        total[...] = nn(hidden[0], decode[...]) + nn(forcing[...], decode[...])

    field = normed[...]
    width = own.shape[1]
    at = step * STEP
    for index, out in enumerate((queries, keys, values)):
        cols = pl.ds(pl.multiple_of(index * width + at, STEP), STEP)
        out[...] = nn(field, weights[:, cols]).astype(b16)
    mixed = weights[pl.ds(pl.multiple_of(at, STEP), STEP), 3 * width :]
    window = window_mask(rows, span)
    masks = head_masks(scale)
    lower = lax.broadcasted_iota(jnp.int32, (rows, LANES), 1) < LANES // 2
    for pair in range(STEP // LANES):
        cols = slice(pair * LANES, (pair + 1) * LANES)
        query = queries[HALO : HALO + rows, cols]
        key = keys[:, cols]
        value = values[:, cols]
        outs, stats = [], []
        for mask in masks:
            scores = jnp.where(window, nt(query * mask, key), FAR)
            top = jnp.max(scores, -1, keepdims=True)
            expo = jnp.exp(scores - top)
            norm = jnp.sum(expo, -1, keepdims=True)
            probs = (expo * (1.0 / norm)).astype(b16)
            outs.append(nn(probs, value))
            stats.append(top + jnp.log(norm))
        attended[:, cols] = jnp.where(lower, outs[0], outs[1]).astype(b16)
        lse[:, cols] = jnp.where(lower, stats[0], stats[1])
    total[...] += nn(attended[...], mixed)

    @pl.when(step == pl.num_programs(0) - 1)
    def _():
        pltpu.make_async_copy(weights, full, store.at[0]).wait()
        pred[...] = total[...].T[:VROWS].astype(b16)


def loss_kernel(
    coeff, variables, others, theirs, pred, targets, weight, attended, mixed, lse,
    gram, halo, grad_attended,
):
    own = pred[...].astype(f32)
    rows = attended.shape[0]
    width = attended.shape[1]

    def member(index, carry):
        pair_abs, pair_slope = carry
        for part in (others, theirs):
            delta = own - part[index].astype(f32)
            square = delta * delta + KAPPA * KAPPA
            inverse = lax.rsqrt(square)
            pair_abs = pair_abs + (square * inverse - KAPPA)
            pair_slope = pair_slope + delta * inverse
        return pair_abs, pair_slope

    zero = jnp.zeros((VROWS, LANES), f32)
    pair_abs, pair_slope = lax.fori_loop(0, others.shape[0], member, (zero, zero), unroll=2)
    delta = own - targets[...].astype(f32)
    square = delta * delta + KAPPA * KAPPA
    inverse = lax.rsqrt(square)
    real = lax.broadcasted_iota(jnp.int32, (VROWS, LANES), 0) < variables
    scale = weight[...]
    entries = jnp.where(real, scale * (square * inverse - KAPPA - coeff * pair_abs), 0.0)
    loss = jnp.sum(jnp.sum(entries, 0, keepdims=True), 1, keepdims=True)
    grad = jnp.where(real, scale * (delta * inverse - 2.0 * coeff * pair_slope), 0.0)
    grad_b = grad.astype(b16)
    halo[:VROWS] = grad_b
    grad_full = jnp.concatenate([grad, jnp.zeros((LANES - VROWS, LANES), f32)], 0)
    grad_t = grad_full.T.astype(b16)
    parts = nn(grad_full.astype(b16), attended[...])
    parts = parts.T
    column = lax.broadcasted_iota(jnp.int32, (width, LANES), 1)
    for index, piece in enumerate(split_bf16(loss, 3)):
        parts = jnp.where(column == variables + index, piece.astype(f32), parts)
    gram[...] = parts.astype(b16)
    grad_att = nt(grad_t, mixed[...]).astype(b16)
    grad_attended[...] = grad_att
    size = width // HEADS
    head = lax.broadcasted_iota(jnp.int32, (HEADS, width), 0)
    feature = lax.broadcasted_iota(jnp.int32, (HEADS, width), 1)
    inside = jnp.where((feature >= head * size) & (feature < (head + 1) * size), 1.0, 0.0)
    chosen = jnp.where(feature == head * size, 1.0, 0.0).astype(b16)
    inside = inside.astype(b16)
    product = grad_att.astype(f32) * attended[...].astype(f32)
    row_delta = sum(nt(inside, piece) for piece in split_bf16(product, 2))
    row_lse = sum(nt(chosen, piece) for piece in split_bf16(lse[...], 3))
    at = VROWS
    for piece in split_bf16(row_delta, 2) + split_bf16(row_lse, 3):
        halo[at : at + HEADS] = piece
        at += HEADS


def own_kernel(scale, query, keys, values, grad_att, lse, grad_query, grad_key, grad_value):
    rows = query.shape[0]
    span = keys.shape[0]
    window = window_mask(rows, span)
    scaled = head_masks(scale)
    plain = head_masks(1.0)
    center = slice(HALO, HALO + rows)
    for pair in range(STEP // LANES):
        cols = slice(pair * LANES, (pair + 1) * LANES)
        q, k, v, g = query[:, cols], keys[:, cols], values[:, cols], grad_att[:, cols]
        stats = lse[:, cols]
        d_query = d_key = d_value = None
        for half in range(2):
            q_half = q * scaled[half]
            g_half = g * plain[half]
            at = half * (LANES // 2)
            probs = jnp.where(window, jnp.exp(nt(q_half, k) - stats[:, at : at + 1]), 0.0)
            d_probs = nt(g_half, v)
            delta = jnp.sum(probs * d_probs, -1, keepdims=True)
            d_scores = (probs * (d_probs - delta)).astype(b16)
            probs = probs.astype(b16)
            dq = nn(d_scores, k * scaled[half])
            dk = tn(d_scores[:, center], q_half)
            dv = tn(probs[:, center], g_half)
            d_query = dq if d_query is None else d_query + dq
            d_key = dk if d_key is None else d_key + dk
            d_value = dv if d_value is None else d_value + dv
        grad_query[:, cols] = d_query.astype(b16)
        grad_key[:, cols] = d_key
        grad_value[:, cols] = d_value


def halo_kernel(
    scale, low, high, query_low, query_high, keys, values, grad_query, key_part, value_part,
    wq, wk, wv, mixed, hidden, forcing, inverse_rms, gain, halo, decode,
    grad_hidden, grad_t, stats, total,
):
    step = pl.program_id(0)
    rows = keys.shape[0]

    @pl.when(step == 0)
    def _():
        zero = jnp.zeros((LANES - VROWS, LANES), b16)
        for side, part in enumerate((low, high)):
            grad = jnp.concatenate([part[:VROWS], zero], 0)
            grad_t[side * HALO : (side + 1) * HALO] = grad.astype(f32).T.astype(b16)
            at = slice(side * HALO, (side + 1) * HALO)
            pieces = [
                part[VROWS + HEADS * n : VROWS + HEADS * (n + 1)].astype(f32) for n in range(5)
            ]
            stats[0, :, at] = pieces[0] + pieces[1]
            stats[1, :, at] = pieces[2] + pieces[3] + pieces[4]
        total[...] = jnp.zeros_like(total)

    key_at = lax.broadcasted_iota(jnp.int32, (rows, 2 * HALO), 0)
    query_at = lax.broadcasted_iota(jnp.int32, (rows, 2 * HALO), 1)
    window = ((query_at < HALO) & (query_at >= key_at)) | (
        (query_at >= HALO) & (query_at - HALO <= key_at)
    )
    scaled = head_masks(scale)
    plain = head_masks(1.0)
    grad_att = nt(grad_t[...], mixed[...]).astype(b16)
    per_step = 2 * (STEP // LANES)
    d_keys, d_values = [], []
    for pair in range(STEP // LANES):
        cols = slice(pair * LANES, (pair + 1) * LANES)
        q = jnp.concatenate([query_low[:, cols], query_high[:, cols]], 0)
        k, v, g = keys[:, cols], values[:, cols], grad_att[:, cols]
        d_key = key_part[:, cols]
        d_value = value_part[:, cols]
        for half in range(2):
            row = step * per_step + 2 * pair + half
            delta = stats[0, pl.ds(row, 1), :]
            lse = stats[1, pl.ds(row, 1), :]
            probs = jnp.where(window, jnp.exp(nt(k * scaled[half], q) - lse), 0.0)
            d_probs = nt(v * plain[half], g)
            d_scores = (probs * (d_probs - delta)).astype(b16)
            d_key = d_key + nn(d_scores, q * scaled[half])
            d_value = d_value + nn(probs.astype(b16), g * plain[half])
        d_keys.append(d_key.astype(b16))
        d_values.append(d_value.astype(b16))
    total[...] += (
        nt(grad_query[...], wq[...])
        + nt(jnp.concatenate(d_keys, 1), wk[...])
        + nt(jnp.concatenate(d_values, 1), wv[...])
    )

    @pl.when(step == pl.num_programs(0) - 1)
    def _():
        zero = jnp.zeros((LANES - VROWS, LANES), b16)
        own = jnp.concatenate([halo[:VROWS], zero], 0).astype(f32).T.astype(b16)
        grad_resid = nt(own, decode[...])
        xfield = hidden[0].astype(f32) + forcing[...].astype(f32)
        inverse = inverse_rms[...]
        grad = gain[...] * total[...]
        mean = jnp.mean(xfield * grad, -1, keepdims=True)
        result = grad_resid + inverse * grad - xfield * (inverse * inverse * inverse * mean)
        grad_hidden[0] = result.astype(b16)


def shifted(value, axis, steps):
    count = lax.axis_size(axis)
    pairs = [(source, (source + steps) % count) for source in range(count)]
    return lax.ppermute(value, axis, pairs)


def permute(value, moves):
    pairs = []
    for x in range(SIDE):
        for z in range(RING_Z):
            for y in range(RING_Y):
                for core in range(2):
                    dx, dz, dc = moves[core]
                    dz = -dz if dz == -2 and z % 2 == 0 else dz
                    dx = -dx if dx == -2 and x % 2 == 0 else dx
                    at = (x, z, core)
                    to = ((x + dx) % SIDE, (z + dz) % RING_Z, core ^ dc)
                    pairs.append(
                        tuple(
                            ((px * SIDE + pz % SIDE) * 2 + pc) * 2 * RING_Y + pz // SIDE * RING_Y + y
                            for px, pz, pc in (at, to)
                        )
                    )
    return lax.ppermute(value, ("ens", "node"), pairs)


def ring(value, along):
    out = [value]
    for hop in (1, -1, -2):
        moves = [(hop, 0, 0) if axis == 0 else (0, hop, 0) for axis in along]
        out.append(permute(value, moves))
    return out


def swapped(value):
    return permute(value, [(0, 0, 1)] * 2)


def gathered(row):
    return ring(row, (1, 0))


def everyone(value):
    value = value[None]
    for phase in range(2):
        groups = []
        for core in range(2):
            for fixed in range(SIDE):
                chips = [
                    step * SIDE + fixed if core == phase else fixed * SIDE + step
                    for step in range(SIDE)
                ]
                groups.append([2 * chip + core for chip in chips])
        spread = jnp.broadcast_to(value[None], (SIDE,) + value.shape)
        spread = spread.reshape((-1,) + value.shape[1:])
        value = lax.all_to_all(spread, "ens", 0, 0, tiled=True, axis_index_groups=groups)
    return value


def per_device(
    hidden, forcing, norm_gain, w_query, w_key, w_value, w_out, w_decode, targets, area_weight
):
    node_rows = hidden.shape[1]
    width = hidden.shape[2]
    head_size = width // HEADS
    span = node_rows + 2 * HALO
    scale = 1.0 / math.sqrt(head_size)
    members = lax.axis_size("ens")
    shards = lax.axis_size("node")
    rows = w_query.shape[0]
    variables = w_decode.shape[1]
    steps = width // STEP
    shape = jax.ShapeDtypeStruct

    def params(mebibytes):
        return pltpu.CompilerParams(
            dimension_semantics=("arbitrary",), vmem_limit_bytes=mebibytes * 1024 * 1024
        )

    def cost(us):
        return pl.CostEstimate(
            flops=us * 10**9, transcendentals=0, bytes_accessed=us * 3 * 10**6
        )
    decode = jnp.pad(w_decode, ((0, 0), (0, LANES - variables)))
    mixed = jnp.dot(w_out, decode, preferred_element_type=f32).astype(b16)
    position = lax.axis_index("ens")
    core = position % 2
    place = jnp.stack([position // (2 * SIDE), position // 2 % SIDE, core]).astype(jnp.int32)
    row = ring(jnp.concatenate([w_query, w_key, w_value, mixed], 1), (0, 1))
    xfield = hidden[0].astype(f32) + forcing.astype(f32)
    inverse_rms = lax.rsqrt(jnp.mean(xfield * xfield, -1, keepdims=True) + EPS_NORM)
    normed = (xfield * inverse_rms * norm_gain).astype(b16)
    low = shifted(normed, "node", 1)
    high = shifted(normed, "node", -1)
    row = jnp.concatenate(row, 0)
    row, low, high = lax.optimization_barrier((row, low, high))
    mine = gathered(row)
    pieces = mine + [swapped(piece) for piece in mine]

    def columns(at):
        return pl.BlockSpec((width, STEP), lambda i: (0, at * steps + i))

    def blocks(height, at=0):
        return pl.BlockSpec((height, STEP), lambda i: (at, i))

    mixed_at = 3 * width // LANES
    packed_width = 3 * width + LANES
    mixed_block = pl.BlockSpec((STEP, LANES), lambda i: (i, mixed_at))
    anywhere = pl.BlockSpec(memory_space=pl.ANY)
    own_block = whole((1, node_rows, width))
    queries, keys, values, attended, lse, pred, full = pl.pallas_call(
        lambda *refs: forward_kernel(scale, *refs),
        grid=(steps,),
        in_specs=[
            pl.BlockSpec(memory_space=pltpu.SMEM),
            whole((HALO, width)),
            whole((node_rows, width)),
            whole((HALO, width)),
            own_block,
            whole((node_rows, width)),
            whole((width, LANES)),
        ]
        + [anywhere] * len(pieces),
        out_specs=[
            blocks(span),
            blocks(span),
            blocks(span),
            blocks(node_rows),
            blocks(node_rows),
            whole((VROWS, node_rows)),
            anywhere,
        ],
        out_shape=[
            pltpu.HBM((span, width), b16),
            pltpu.HBM((span, width), b16),
            pltpu.HBM((span, width), b16),
            pltpu.HBM((node_rows, width), b16),
            pltpu.HBM((node_rows, width), f32),
            pltpu.HBM((VROWS, node_rows), b16),
            pltpu.HBM((width, packed_width), b16),
        ],
        scratch_shapes=[
            pltpu.VMEM((span, width), b16),
            pltpu.VMEM((node_rows, LANES), f32),
            pltpu.VMEM((width, packed_width), b16),
            pltpu.SemaphoreType.DMA((len(pieces) * SIDE,)),
            pltpu.SemaphoreType.DMA((1,)),
        ],
        compiler_params=params(24),
        cost_estimate=cost(12),
        name="forward",
    )(place, low, normed, high, hidden, forcing, decode, *pieces)

    others = everyone(pred)
    theirs = swapped(others)
    eps = (1.0 - ALPHA) / members
    coeff = (1.0 - eps) / (2.0 * (members - 1))
    truth = jnp.pad(targets, ((0, VROWS - variables), (0, 0)))
    payload = VROWS + 5 * HEADS
    gram, halo, grad_attended = pl.pallas_call(
        lambda *refs: loss_kernel(coeff, variables, *refs),
        grid=(1,),
        in_specs=[
            whole(others.shape),
            whole(others.shape),
            whole((VROWS, node_rows)),
            whole((VROWS, node_rows)),
            whole((1, node_rows)),
            whole((node_rows, width)),
            pl.BlockSpec((width, LANES), lambda i: (0, mixed_at)),
            whole((node_rows, width)),
        ],
        out_specs=[
            whole((width, LANES)),
            whole((payload, node_rows)),
            whole((node_rows, width)),
        ],
        out_shape=[
            shape((width, LANES), b16),
            shape((payload, node_rows), b16),
            shape((node_rows, width), b16),
        ],
        compiler_params=params(12),
        cost_estimate=cost(3),
        name="crps",
    )(others, theirs, pred, truth, area_weight[None], attended, full, lse)

    halo_low = shifted(halo, "node", 1)
    halo_high = shifted(halo, "node", -1)
    parts = lax.all_to_all(gram.reshape(members, rows, LANES), "ens", 0, 0, tiled=True)
    part = jnp.sum(parts.astype(f32), 0)
    parts = lax.all_to_all(
        jnp.broadcast_to(part[None], (shards,) + part.shape), "node", 0, 0, tiled=True
    )
    total = jnp.sum(parts, 0)
    grad_out_proj = lax.dot_general(
        total[:, :variables],
        w_decode.astype(f32),
        (((1,), (1,)), ((), ())),
        preferred_element_type=f32,
    )
    loss = jnp.sum(total[0, variables : variables + 3]) / (members * node_rows * shards * variables)

    grad_query, key_part, value_part = pl.pallas_call(
        lambda *refs: own_kernel(scale, *refs),
        grid=(steps,),
        in_specs=[
            blocks(node_rows, HALO // node_rows),
            blocks(span),
            blocks(span),
            blocks(node_rows),
            blocks(node_rows),
        ],
        out_specs=[blocks(node_rows)] * 3,
        out_shape=[
            pltpu.HBM((node_rows, width), b16),
            pltpu.HBM((node_rows, width), f32),
            pltpu.HBM((node_rows, width), f32),
        ],
        compiler_params=params(12),
        cost_estimate=cost(6),
        name="own_queries",
    )(queries, keys, values, grad_attended, lse)

    (grad_hidden,) = pl.pallas_call(
        lambda *refs: halo_kernel(scale, *refs),
        grid=(steps,),
        in_specs=[
            whole((payload, node_rows)),
            whole((payload, node_rows)),
            blocks(HALO, 0),
            blocks(HALO, 2),
            blocks(node_rows, 1),
            blocks(node_rows, 1),
            blocks(node_rows),
            blocks(node_rows),
            blocks(node_rows),
            columns(0),
            columns(1),
            columns(2),
            mixed_block,
            own_block,
            whole((node_rows, width)),
            whole((node_rows, 1)),
            whole((1, width)),
            whole((payload, node_rows)),
            whole((width, LANES)),
        ],
        out_specs=[own_block],
        out_shape=[shape((1, node_rows, width), b16)],
        scratch_shapes=[
            pltpu.VMEM((2 * HALO, LANES), b16),
            pltpu.VMEM((2, HEADS, 2 * HALO), f32),
            pltpu.VMEM((node_rows, width), f32),
        ],
        compiler_params=params(16),
        cost_estimate=cost(9),
        name="neighbour_queries",
    )(
        halo_low, halo_high, queries, queries, keys, values, grad_query, key_part, value_part,
        full, full, full, full, hidden, forcing, inverse_rms, norm_gain[None], halo, decode,
    )
    return (grad_hidden, grad_out_proj, loss)


def solution(mesh):
    placed = (
        P("ens", "node", None),
        P("node", None),
        P(),
        P("ens", None),
        P("ens", None),
        P("ens", None),
        P("ens", None),
        P(),
        P(None, "node"),
        P("node"),
    )
    return jax.shard_map(
        per_device,
        mesh=mesh,
        in_specs=placed,
        out_specs=(P("ens", "node", None), P("ens", None), P()),
        check_vma=False,
    )
```

```python
import math

import jax
import jax.numpy as jnp
from jax import lax
from jax.experimental import pallas as pl
from jax.experimental.pallas import tpu as pltpu
from jax.sharding import PartitionSpec as P

HEADS = 16
HALO = 128
LANES = 128
STEP = 256
VROWS = 112
SIDE = 4
RING_Z = 8
RING_Y = 8
HOPS = (0, SIDE - 1, 1, 2)


ALPHA = 0.95
KAPPA = 0.25
EPS_NORM = 1e-05
FAR = -1e30

f32 = jnp.float32
b16 = jnp.bfloat16


def nn(a, b):
    return lax.dot_general(a, b, (((1,), (0,)), ((), ())), preferred_element_type=f32)


def nt(a, b):
    return lax.dot_general(a, b, (((1,), (1,)), ((), ())), preferred_element_type=f32)


def tn(a, b):
    return lax.dot_general(a, b, (((0,), (0,)), ((), ())), preferred_element_type=f32)


def whole(shape):
    return pl.BlockSpec(shape, lambda i: (0,) * len(shape))


def head_masks(value):
    lane = lax.broadcasted_iota(jnp.int32, (1, LANES), 1)
    first = jnp.where(lane < LANES // 2, value, 0.0).astype(b16)
    second = jnp.where(lane < LANES // 2, 0.0, value).astype(b16)
    return first, second


def window_mask(rows, span):
    offset = lax.broadcasted_iota(jnp.int32, (rows, span), 1) - lax.broadcasted_iota(
        jnp.int32, (rows, span), 0
    )
    return (offset >= 0) & (offset <= 2 * HALO)


def split_bf16(value, pieces):
    out = []
    for _ in range(pieces):
        piece = value.astype(b16)
        out.append(piece)
        value = value - piece.astype(f32)
    return out


def forward_kernel(scale, place, low, own, high, hidden, forcing, decode, *refs):
    pieces, refs = refs[: 2 * len(HOPS)], refs[2 * len(HOPS) :]
    (
        queries_out, keys_out, values_out, attended, lse_out, pred, mixed, full,
        queries, keys, values, lse, normed, weights, store,
    ) = refs
    rows, width = own.shape
    span = rows + 2 * HALO
    x, z, core = place[0], place[1], place[2]
    side = len(HOPS)
    block = pieces[0].shape[0] // side
    for mine in (True, False):
        which = core if mine else 1 - core
        for outer, far in enumerate(HOPS):
            piece = pieces[outer if mine else side + outer]
            for inner, near in enumerate(HOPS):
                along_x = jnp.where(which == 0, near, far)
                along_z = jnp.where(which == 0, far, near)
                chip = lax.rem(x + along_x, side) * side + lax.rem(z + along_z, side)
                at = pl.multiple_of((chip * 2 + which) * block, block)
                weights[pl.ds(at, block), :] = piece[inner * block : (inner + 1) * block, :]
    stores = [pltpu.make_async_copy(weights, full, store.at[0])]
    stores[0].start()
    mixed[...] = weights[:, 3 * width :]
    normed[:HALO] = low[...]
    normed[HALO : HALO + rows] = own[...]
    normed[HALO + rows :] = high[...]
    total = nn(hidden[0], decode[...]) + nn(forcing[...], decode[...])
    window = window_mask(rows, span)
    masks = head_masks(scale)
    lower = lax.broadcasted_iota(jnp.int32, (rows, LANES), 1) < LANES // 2
    pairs = STEP // LANES
    for at in range(0, width, STEP):
        cols = slice(at, at + STEP)
        field = normed[...]
        projected = [
            nn(field, weights[:, index * width + at : index * width + at + STEP]).astype(b16)
            for index in range(3)
        ]
        query, key, value = projected
        for part, scratch, out in zip(
            projected, (queries, keys, values), (queries_out, keys_out, values_out), strict=True
        ):
            scratch[:, cols] = part
            stores.append(
                pltpu.make_async_copy(scratch.at[:, cols], out.at[:, cols], store.at[len(stores)])
            )
            stores[-1].start()
        scores = []
        for pair in range(pairs):
            lanes = slice(pair * LANES, (pair + 1) * LANES)
            for mask in masks:
                scores.append(nt(query[HALO : HALO + rows, lanes] * mask, key[:, lanes]))
        scores = [jnp.where(window, score, FAR) for score in scores]
        tops = [jnp.max(score, -1, keepdims=True) for score in scores]
        expos = [jnp.exp(score - top) for score, top in zip(scores, tops, strict=True)]
        norms = [jnp.sum(expo, -1, keepdims=True) for expo in expos]
        probs = [(expo * (1.0 / norm)).astype(b16) for expo, norm in zip(expos, norms, strict=True)]
        outs = [
            nn(prob, value[:, index // 2 * LANES : (index // 2 + 1) * LANES])
            for index, prob in enumerate(probs)
        ]
        stats = [top + jnp.log(norm) for top, norm in zip(tops, norms, strict=True)]
        result = jnp.concatenate(
            [jnp.where(lower, outs[2 * n], outs[2 * n + 1]).astype(b16) for n in range(pairs)], 1
        )
        attended[:, cols] = result
        lse[:, cols] = jnp.concatenate(
            [jnp.where(lower, stats[2 * n], stats[2 * n + 1]) for n in range(pairs)], 1
        )
        stores.append(
            pltpu.make_async_copy(lse.at[:, cols], lse_out.at[:, cols], store.at[len(stores)])
        )
        stores[-1].start()
        total = total + nn(result, mixed[cols, :])
    pred[...] = total.T[:VROWS].astype(b16)
    for copy in stores:
        copy.wait()


def loss_kernel(
    coeff, variables, others, theirs, pred, targets, weight, attended, mixed, lse,
    gram, halo,
):
    own = pred[...].astype(f32)
    rows = attended.shape[0]
    width = attended.shape[1]

    def member(index, carry):
        pair_abs, pair_slope = carry
        for part in (others, theirs):
            delta = own - part[index].astype(f32)
            square = delta * delta + KAPPA * KAPPA
            inverse = lax.rsqrt(square)
            pair_abs = pair_abs + (square * inverse - KAPPA)
            pair_slope = pair_slope + delta * inverse
        return pair_abs, pair_slope

    zero = jnp.zeros((VROWS, LANES), f32)
    pair_abs, pair_slope = lax.fori_loop(0, others.shape[0], member, (zero, zero), unroll=2)
    delta = own - targets[...].astype(f32)
    square = delta * delta + KAPPA * KAPPA
    inverse = lax.rsqrt(square)
    real = lax.broadcasted_iota(jnp.int32, (VROWS, LANES), 0) < variables
    scale = weight[...]
    entries = jnp.where(real, scale * (square * inverse - KAPPA - coeff * pair_abs), 0.0)
    loss = jnp.sum(jnp.sum(entries, 0, keepdims=True), 1, keepdims=True)
    grad = jnp.where(real, scale * (delta * inverse - 2.0 * coeff * pair_slope), 0.0)
    grad_b = grad.astype(b16)
    halo[:VROWS] = grad_b
    grad_full = jnp.concatenate([grad, jnp.zeros((LANES - VROWS, LANES), f32)], 0)
    grad_t = grad_full.T.astype(b16)
    parts = nn(grad_full.astype(b16), attended[...])
    parts = parts.T
    column = lax.broadcasted_iota(jnp.int32, (width, LANES), 1)
    for index, piece in enumerate(split_bf16(loss, 3)):
        parts = jnp.where(column == variables + index, piece.astype(f32), parts)
    gram[...] = parts.astype(b16)
    grad_att = nt(grad_t, mixed[...]).astype(b16)
    size = width // HEADS
    head = lax.broadcasted_iota(jnp.int32, (HEADS, width), 0)
    feature = lax.broadcasted_iota(jnp.int32, (HEADS, width), 1)
    inside = jnp.where((feature >= head * size) & (feature < (head + 1) * size), 1.0, 0.0)
    chosen = jnp.where(feature == head * size, 1.0, 0.0).astype(b16)
    inside = inside.astype(b16)
    product = grad_att.astype(f32) * attended[...].astype(f32)
    row_delta = sum(nt(inside, piece) for piece in split_bf16(product, 2))
    row_lse = sum(nt(chosen, piece) for piece in split_bf16(lse[...], 3))
    at = VROWS
    for piece in split_bf16(row_delta, 2) + split_bf16(row_lse, 3):
        halo[at : at + HEADS] = piece
        at += HEADS


def backward_kernel(
    scale, low, own, high, hidden, forcing, inverse_rms, gain, decode, mixed,
    queries_in, keys_in, values_in, lse_in, full,
    grad_hidden, queries, keys, values, lse, weights, grad_t, stats, load,
):
    rows, width = lse.shape
    span = keys.shape[0]
    loads = []

    def fetch(source, target):
        loads.append(pltpu.make_async_copy(source, target, load.at[len(loads)]))
        loads[-1].start()

    fetch(queries_in, queries)
    fetch(keys_in, keys)
    fetch(values_in, values)
    fetch(lse_in, lse)
    for at in range(0, width, STEP):
        for index in range(3):
            cols = slice(index * width + at, index * width + at + STEP)
            fetch(full.at[:, cols], weights.at[:, cols])

    zero = jnp.zeros((LANES - VROWS, LANES), b16)
    for side, part in enumerate((own, low, high)):
        grad = jnp.concatenate([part[:VROWS], zero], 0)
        grad_t[side * rows : (side + 1) * rows] = grad.astype(f32).T.astype(b16)
    for side, part in enumerate((low, high)):
        at = slice(side * HALO, (side + 1) * HALO)
        pieces = [part[VROWS + HEADS * n : VROWS + HEADS * (n + 1)].astype(f32) for n in range(5)]
        stats[0, :, at] = pieces[0] + pieces[1]
        stats[1, :, at] = pieces[2] + pieces[3] + pieces[4]
    grad_resid = nt(grad_t[:rows], decode[...])

    window = window_mask(rows, span)
    key_at = lax.broadcasted_iota(jnp.int32, (rows, 2 * HALO), 0)
    query_at = lax.broadcasted_iota(jnp.int32, (rows, 2 * HALO), 1)
    reach = ((query_at < HALO) & (query_at >= key_at)) | (
        (query_at >= HALO) & (query_at - HALO <= key_at)
    )
    scaled = head_masks(scale)
    plain = head_masks(1.0)
    center = slice(HALO, HALO + rows)
    halves = [(pair, half) for pair in range(STEP // LANES) for half in range(2)]
    total = jnp.zeros((rows, width), f32)
    for copy in loads[:4]:
        copy.wait()
    for at in range(0, width, STEP):
        step = at // STEP
        grad_att = nt(grad_t[...], mixed[at : at + STEP, :]).astype(b16)
        lanes = [slice(at + pair * LANES, at + (pair + 1) * LANES) for pair in range(STEP // LANES)]
        query = [queries[center, cols] for cols in lanes]
        key = [keys[:, cols] for cols in lanes]
        value = [values[:, cols] for cols in lanes]
        far_query = [
            jnp.concatenate([queries[:HALO, cols], queries[HALO + rows :, cols]], 0)
            for cols in lanes
        ]
        grad = [grad_att[:rows, n * LANES : (n + 1) * LANES] for n in range(len(lanes))]
        far_grad = [grad_att[rows:, n * LANES : (n + 1) * LANES] for n in range(len(lanes))]
        scores = [nt(query[p] * scaled[h], key[p]) for p, h in halves]
        d_probs = [nt(grad[p] * plain[h], value[p]) for p, h in halves]
        probs = []
        for (p, h), score in zip(halves, scores, strict=True):
            start = lanes[p].start + h * (LANES // 2)
            probs.append(jnp.where(window, jnp.exp(score - lse[:, start : start + 1]), 0.0))
        deltas = [
            jnp.sum(prob * d_prob, -1, keepdims=True)
            for prob, d_prob in zip(probs, d_probs, strict=True)
        ]
        d_scores = [
            (prob * (d_prob - delta)).astype(b16)
            for prob, d_prob, delta in zip(probs, d_probs, deltas, strict=True)
        ]
        probs = [prob.astype(b16) for prob in probs]
        far_scores = [nt(key[p][center] * scaled[h], far_query[p]) for p, h in halves]
        far_d_probs = [nt(value[p][center] * plain[h], far_grad[p]) for p, h in halves]
        far_probs, far_d_scores = [], []
        for (p, h), score, d_prob in zip(halves, far_scores, far_d_probs, strict=True):
            row = 2 * (step * len(lanes) + p) + h
            prob = jnp.where(reach, jnp.exp(score - stats[1, row : row + 1, :]), 0.0)
            far_d_scores.append((prob * (d_prob - stats[0, row : row + 1, :])).astype(b16))
            far_probs.append(prob.astype(b16))
        d_query, d_key, d_value = [], [], []
        for p in range(len(lanes)):
            first, second = 2 * p, 2 * p + 1
            d_query.append(
                nn(d_scores[first], key[p] * scaled[0]) + nn(d_scores[second], key[p] * scaled[1])
            )
            d_key.append(
                tn(d_scores[first][:, center], query[p] * scaled[0])
                + tn(d_scores[second][:, center], query[p] * scaled[1])
                + nn(far_d_scores[first], far_query[p] * scaled[0])
                + nn(far_d_scores[second], far_query[p] * scaled[1])
            )
            d_value.append(
                tn(probs[first][:, center], grad[p] * plain[0])
                + tn(probs[second][:, center], grad[p] * plain[1])
                + nn(far_probs[first], far_grad[p] * plain[0])
                + nn(far_probs[second], far_grad[p] * plain[1])
            )
        for index, part in enumerate((d_query, d_key, d_value)):
            loads[4 + 3 * step + index].wait()
            part = jnp.concatenate(part, 1).astype(b16)
            cols = slice(index * width + at, index * width + at + STEP)
            total = total + nt(part, weights[:, cols])
    xfield = hidden[0].astype(f32) + forcing[...].astype(f32)
    inverse = inverse_rms[...]
    grad = gain[...] * total
    mean = jnp.mean(xfield * grad, -1, keepdims=True)
    result = grad_resid + inverse * grad - xfield * (inverse * inverse * inverse * mean)
    grad_hidden[0] = result.astype(b16)


def shifted(value, axis, steps):
    count = lax.axis_size(axis)
    pairs = [(source, (source + steps) % count) for source in range(count)]
    return lax.ppermute(value, axis, pairs)


def permute(value, moves):
    pairs = []
    for x in range(SIDE):
        for z in range(RING_Z):
            for y in range(RING_Y):
                for core in range(2):
                    dx, dz, dc = moves[core]
                    dz = -dz if dz == -2 and z % 2 == 0 else dz
                    dx = -dx if dx == -2 and x % 2 == 0 else dx
                    at = (x, z, core)
                    to = ((x + dx) % SIDE, (z + dz) % RING_Z, core ^ dc)
                    pairs.append(
                        tuple(
                            ((px * SIDE + pz % SIDE) * 2 + pc) * 2 * RING_Y + pz // SIDE * RING_Y + y
                            for px, pz, pc in (at, to)
                        )
                    )
    return lax.ppermute(value, ("ens", "node"), pairs)


def ring(value, along, before=()):
    out = [value]
    for hop in (1, -1, -2):
        if hop == -2 and before:
            value, *before = lax.optimization_barrier((value, *before))
        moves = [(hop, 0, 0) if axis == 0 else (0, hop, 0) for axis in along]
        out.append(permute(value, moves))
    return out + list(before)


def swapped(value):
    return permute(value, [(0, 0, 1)] * 2)


def everyone(value):
    value = value[None]
    for phase in range(2):
        groups = []
        for core in range(2):
            for fixed in range(SIDE):
                chips = [
                    step * SIDE + fixed if core == phase else fixed * SIDE + step
                    for step in range(SIDE)
                ]
                groups.append([2 * chip + core for chip in chips])
        spread = jnp.broadcast_to(value[None], (SIDE,) + value.shape)
        spread = spread.reshape((-1,) + value.shape[1:])
        value = lax.all_to_all(spread, "ens", 0, 0, tiled=True, axis_index_groups=groups)
    return value


def per_device(
    hidden, forcing, norm_gain, w_query, w_key, w_value, w_out, w_decode, targets, area_weight
):
    node_rows = hidden.shape[1]
    width = hidden.shape[2]
    head_size = width // HEADS
    span = node_rows + 2 * HALO
    scale = 1.0 / math.sqrt(head_size)
    members = lax.axis_size("ens")
    shards = lax.axis_size("node")
    rows = w_query.shape[0]
    variables = w_decode.shape[1]
    steps = width // STEP
    shape = jax.ShapeDtypeStruct

    def params(mebibytes):
        return pltpu.CompilerParams(vmem_limit_bytes=mebibytes * 1024 * 1024)

    def cost(us):
        return pl.CostEstimate(
            flops=us * 10**9, transcendentals=0, bytes_accessed=us * 3 * 10**6
        )
    decode = jnp.pad(w_decode, ((0, 0), (0, LANES - variables)))
    mixed = jnp.dot(w_out, decode, preferred_element_type=f32).astype(b16)
    position = lax.axis_index("ens")
    core = position % 2
    place = jnp.stack([position // (2 * SIDE), position // 2 % SIDE, core]).astype(jnp.int32)
    row = ring(jnp.concatenate([w_query, w_key, w_value, mixed], 1), (0, 1))
    xfield = hidden[0].astype(f32) + forcing.astype(f32)
    inverse_rms = lax.rsqrt(jnp.mean(xfield * xfield, -1, keepdims=True) + EPS_NORM)
    normed = (xfield * inverse_rms * norm_gain).astype(b16)
    low = shifted(normed, "node", 1)
    high = shifted(normed, "node", -1)
    *mine, low, high = ring(jnp.concatenate(row, 0), (1, 0), (low, high))
    pieces = mine + [swapped(piece) for piece in mine]

    packed_width = 3 * width + LANES
    in_vmem = pl.BlockSpec(memory_space=pltpu.VMEM)
    in_hbm = pl.BlockSpec(memory_space=pltpu.HBM)

    def held(value):
        return pltpu.with_memory_space_constraint(value, pltpu.HBM)

    queries, keys, values, attended, lse, pred, mixed, full = pl.pallas_call(
        lambda *refs: forward_kernel(scale, *refs),
        in_specs=[pl.BlockSpec(memory_space=pltpu.SMEM)] + [in_vmem] * (6 + len(pieces)),
        out_specs=[in_hbm, in_hbm, in_hbm, in_vmem, in_hbm, in_vmem, in_vmem, in_hbm],
        out_shape=[
            pltpu.HBM((span, width), b16),
            pltpu.HBM((span, width), b16),
            pltpu.HBM((span, width), b16),
            shape((node_rows, width), b16),
            pltpu.HBM((node_rows, width), f32),
            shape((VROWS, node_rows), b16),
            shape((width, LANES), b16),
            pltpu.HBM((width, packed_width), b16),
        ],
        scratch_shapes=[
            pltpu.VMEM((span, width), b16),
            pltpu.VMEM((span, width), b16),
            pltpu.VMEM((span, width), b16),
            pltpu.VMEM((node_rows, width), f32),
            pltpu.VMEM((span, width), b16),
            pltpu.VMEM((width, packed_width), b16),
            pltpu.SemaphoreType.DMA((1 + 4 * steps,)),
        ],
        compiler_params=params(24),
        cost_estimate=cost(9),
        name="forward",
    )(place, low, normed, high, hidden, forcing, decode, *pieces)

    others = everyone(pred)
    theirs = swapped(others)
    eps = (1.0 - ALPHA) / members
    coeff = (1.0 - eps) / (2.0 * (members - 1))
    truth = jnp.pad(targets, ((0, VROWS - variables), (0, 0)))
    payload = VROWS + 5 * HEADS
    gram, halo = pl.pallas_call(
        lambda *refs: loss_kernel(coeff, variables, *refs),
        grid=(1,),
        in_specs=[
            whole(others.shape),
            whole(others.shape),
            whole((VROWS, node_rows)),
            whole((VROWS, node_rows)),
            whole((1, node_rows)),
            whole((node_rows, width)),
            whole((width, LANES)),
            whole((node_rows, width)),
        ],
        out_specs=[
            whole((width, LANES)),
            whole((payload, node_rows)),
        ],
        out_shape=[
            shape((width, LANES), b16),
            shape((payload, node_rows), b16),
        ],
        compiler_params=params(12),
        cost_estimate=cost(3),
        name="crps",
    )(others, theirs, pred, truth, area_weight[None], attended, mixed, lse)

    halo_low = shifted(halo, "node", 1)
    halo_high = shifted(halo, "node", -1)
    parts = lax.all_to_all(gram.reshape(members, rows, LANES), "ens", 0, 0, tiled=True)
    part = jnp.sum(parts.astype(f32), 0)
    parts = lax.all_to_all(
        jnp.broadcast_to(part[None], (shards,) + part.shape), "node", 0, 0, tiled=True
    )
    total = jnp.sum(parts, 0)
    grad_out_proj = lax.dot_general(
        total[:, :variables],
        w_decode.astype(f32),
        (((1,), (1,)), ((), ())),
        preferred_element_type=f32,
    )
    loss = jnp.sum(total[0, variables : variables + 3]) / (members * node_rows * shards * variables)

    grad_hidden = pl.pallas_call(
        lambda *refs: backward_kernel(scale, *refs),
        in_specs=[in_vmem] * 9 + [in_hbm] * 5,
        out_specs=in_vmem,
        out_shape=shape((1, node_rows, width), b16),
        scratch_shapes=[
            pltpu.VMEM((span, width), b16),
            pltpu.VMEM((span, width), b16),
            pltpu.VMEM((span, width), b16),
            pltpu.VMEM((node_rows, width), f32),
            pltpu.VMEM((width, 3 * width), b16),
            pltpu.VMEM((span, LANES), b16),
            pltpu.VMEM((2, HEADS, 2 * HALO), f32),
            pltpu.SemaphoreType.DMA((4 + 3 * steps,)),
        ],
        compiler_params=params(24),
        cost_estimate=cost(12),
        name="backward",
    )(
        halo_low, halo, halo_high, hidden, forcing, inverse_rms, norm_gain[None], decode, mixed,
        *[held(part) for part in (queries, keys, values, lse, full)],
    )
    return (grad_hidden, grad_out_proj, loss)


def solution(mesh):
    placed = (
        P("ens", "node", None),
        P("node", None),
        P(),
        P("ens", None),
        P("ens", None),
        P("ens", None),
        P("ens", None),
        P(),
        P(None, "node"),
        P("node"),
    )
    return jax.shard_map(
        per_device,
        mesh=mesh,
        in_specs=placed,
        out_specs=(P("ens", "node", None), P("ens", None), P()),
        check_vma=False,
    )
```

```python
import math

import jax
import jax.numpy as jnp
from jax import lax
from jax.experimental import pallas as pl
from jax.experimental.pallas import tpu as pltpu
from jax.sharding import PartitionSpec as P

HEADS = 16
HALO = 128
LANES = 128
STEP = 256
VROWS = 112
SIDE = 4
RING_Z = 8
RING_Y = 8
HOPS = (0, SIDE - 1, 1, 2)


ALPHA = 0.95
KAPPA = 0.25
EPS_NORM = 1e-05
FAR = -1e30

f32 = jnp.float32
b16 = jnp.bfloat16


def nn(a, b):
    return lax.dot_general(a, b, (((1,), (0,)), ((), ())), preferred_element_type=f32)


def nt(a, b):
    return lax.dot_general(a, b, (((1,), (1,)), ((), ())), preferred_element_type=f32)


def tn(a, b):
    return lax.dot_general(a, b, (((0,), (0,)), ((), ())), preferred_element_type=f32)


def whole(shape):
    return pl.BlockSpec(shape, lambda i: (0,) * len(shape))


def head_masks(value):
    lane = lax.broadcasted_iota(jnp.int32, (1, LANES), 1)
    first = jnp.where(lane < LANES // 2, value, 0.0).astype(b16)
    second = jnp.where(lane < LANES // 2, 0.0, value).astype(b16)
    return first, second


def window_mask(rows, span):
    offset = lax.broadcasted_iota(jnp.int32, (rows, span), 1) - lax.broadcasted_iota(
        jnp.int32, (rows, span), 0
    )
    return (offset >= 0) & (offset <= 2 * HALO)


def split_bf16(value, pieces):
    out = []
    for _ in range(pieces):
        piece = value.astype(b16)
        out.append(piece)
        value = value - piece.astype(f32)
    return out


def forward_kernel(scale, place, own, other, hidden, forcing, decode, *refs):
    pieces, refs = refs[: len(HOPS)], refs[len(HOPS) :]
    (
        queries_out, keys_out, values_out, attended, lse, pred, mixed, full,
        queries, keys, values, weights, store,
    ) = refs
    span = own.shape[0]
    rows = span - 2 * HALO
    width = attended.shape[2]
    x, z, core = place[0], place[1], place[2]
    side = len(HOPS)
    block = pieces[0].shape[0] // side
    for outer, far in enumerate(HOPS):
        for inner, near in enumerate(HOPS):
            along_x = jnp.where(core == 0, near, far)
            along_z = jnp.where(core == 0, far, near)
            chip = lax.rem(x + along_x, side) * side + lax.rem(z + along_z, side)
            at = pl.multiple_of(chip * block, block)
            weights[pl.ds(at, block), :] = pieces[outer][inner * block : (inner + 1) * block, :]
    stores = [pltpu.make_async_copy(weights, full, store.at[0])]
    stores[0].start()
    mixed[...] = weights[pl.ds(pl.multiple_of(core * width, width), width), 3 * width :]
    window = window_mask(rows, span)
    masks = head_masks(scale)
    lower = lax.broadcasted_iota(jnp.int32, (rows, LANES), 1) < LANES // 2
    pairs = STEP // LANES
    for member, field_ref in enumerate((own, other)):
        if member == 0:
            total = nn(hidden[0], decode[...]) + nn(forcing[...], decode[...])
        else:
            total = jnp.zeros((rows, LANES), f32)
        for at in range(0, width, STEP):
            cols = slice(at, at + STEP)
            field = field_ref[...]
            projected = [
                nn(field, weights[:, index * width + at : index * width + at + STEP]).astype(b16)
                for index in range(3)
            ]
            query, key, value = projected
            for part, scratch, out in zip(
                projected, (queries, keys, values), (queries_out, keys_out, values_out), strict=True
            ):
                scratch[member, :, cols] = part
                stores.append(
                    pltpu.make_async_copy(
                        scratch.at[member, :, cols],
                        out.at[member, :, cols],
                        store.at[len(stores)],
                    )
                )
                stores[-1].start()
            scores = []
            for pair in range(pairs):
                lanes = slice(pair * LANES, (pair + 1) * LANES)
                for mask in masks:
                    scores.append(nt(query[HALO : HALO + rows, lanes] * mask, key[:, lanes]))
            scores = [jnp.where(window, score, FAR) for score in scores]
            tops = [jnp.max(score, -1, keepdims=True) for score in scores]
            expos = [jnp.exp(score - top) for score, top in zip(scores, tops, strict=True)]
            norms = [jnp.sum(expo, -1, keepdims=True) for expo in expos]
            probs = [
                (expo * (1.0 / norm)).astype(b16) for expo, norm in zip(expos, norms, strict=True)
            ]
            outs = [
                nn(prob, value[:, index // 2 * LANES : (index // 2 + 1) * LANES])
                for index, prob in enumerate(probs)
            ]
            stats = [top + jnp.log(norm) for top, norm in zip(tops, norms, strict=True)]
            result = jnp.concatenate(
                [jnp.where(lower, outs[2 * n], outs[2 * n + 1]).astype(b16) for n in range(pairs)],
                1,
            )
            attended[member, :, cols] = result
            lse[member, :, cols] = jnp.concatenate(
                [jnp.where(lower, stats[2 * n], stats[2 * n + 1]) for n in range(pairs)], 1
            )
            total = total + nn(result, mixed[cols, :])
        pred[member] = total.T[:VROWS]
    for copy in stores:
        copy.wait()


def loss_kernel(
    coeff, variables, place, others, theirs, preds, targets, weight, attended, mixed, lse,
    gram, halo,
):
    rows, width = attended.shape[1:]
    heads = HEADS // 2
    truth = targets[...].astype(f32)
    scale = weight[...]
    real = lax.broadcasted_iota(jnp.int32, (VROWS, LANES), 0) < variables
    size = width // heads
    head = lax.broadcasted_iota(jnp.int32, (heads, width), 0)
    feature = lax.broadcasted_iota(jnp.int32, (heads, width), 1)
    inside = jnp.where((feature >= head * size) & (feature < (head + 1) * size), 1.0, 0.0)
    chosen = jnp.where(feature == head * size, 1.0, 0.0).astype(b16)
    inside = inside.astype(b16)
    own, other = preds[0].astype(f32), preds[1].astype(f32)

    def member(index, carry):
        pair_abs, slope_own, slope_other = carry
        for part in (others, theirs):
            value = part[index].astype(f32)
            delta = own - value
            square = delta * delta + KAPPA * KAPPA
            inverse = lax.rsqrt(square)
            pair_abs = pair_abs + (square * inverse - KAPPA)
            slope_own = slope_own + delta * inverse
            delta = other - value
            slope_other = slope_other + delta * lax.rsqrt(delta * delta + KAPPA * KAPPA)
        return pair_abs, slope_own, slope_other

    zero = jnp.zeros((VROWS, LANES), f32)
    pair_abs, *slopes = lax.fori_loop(0, others.shape[0], member, (zero, zero, zero), unroll=2)
    parts = jnp.zeros((LANES, width), f32)
    row_delta, row_lse = [], []
    for index, value in enumerate((own, other)):
        delta = value - truth
        square = delta * delta + KAPPA * KAPPA
        inverse = lax.rsqrt(square)
        if index == 0:
            entries = scale * (square * inverse - KAPPA - coeff * pair_abs)
            entries = jnp.where(real, entries, 0.0)
            loss = jnp.sum(jnp.sum(entries, 0, keepdims=True), 1, keepdims=True)
        grad = jnp.where(real, scale * (delta * inverse - 2.0 * coeff * slopes[index]), 0.0)
        halo[index * VROWS : (index + 1) * VROWS] = grad.astype(b16)
        grad_full = jnp.concatenate([grad, jnp.zeros((LANES - VROWS, LANES), f32)], 0)
        grad_t = grad_full.T.astype(b16)
        parts = parts + nn(grad_full.astype(b16), attended[index])
        grad_att = nt(grad_t, mixed[...]).astype(b16)
        product = grad_att.astype(f32) * attended[index].astype(f32)
        row_delta.append(sum(nt(inside, piece) for piece in split_bf16(product, 2)))
        row_lse.append(sum(nt(chosen, piece) for piece in split_bf16(lse[index], 3)))
    at = 2 * VROWS
    for pieces in (
        split_bf16(jnp.concatenate(row_delta, 0), 2),
        split_bf16(jnp.concatenate(row_lse, 0), 3),
    ):
        for piece in pieces:
            halo[at : at + HEADS] = piece
            at += HEADS
    column = lax.broadcasted_iota(jnp.int32, (width, LANES), 1)
    parts = parts.T
    blank = jnp.zeros((width, LANES), f32)
    for index, piece in enumerate(split_bf16(loss, 3)):
        parts = jnp.where(column == variables + index, piece.astype(f32), parts)
        blank = jnp.where(column == variables + index, piece.astype(f32), blank)
    core = place[2]
    gram[pl.ds(pl.multiple_of(core * width, width), width), :] = parts.astype(b16)
    gram[pl.ds(pl.multiple_of((1 - core) * width, width), width), :] = blank.astype(b16)


def middle_kernel(variables, parts, spread):
    total = parts[0].astype(f32)
    for index in range(1, parts.shape[0]):
        total = total + parts[index].astype(f32)
    column = lax.broadcasted_iota(jnp.int32, total.shape, 1)
    spare = (column >= variables) & (column < variables + 3)
    loss = jnp.sum(jnp.where(spare, total, 0.0), 1, keepdims=True)
    for index, piece in enumerate(split_bf16(loss, 3)):
        total = jnp.where(column == variables + index, piece.astype(f32), total)
    total = total.astype(b16)
    for index in range(spread.shape[0]):
        spread[index] = total


def backward_kernel(
    scale, low, own, high, mixed, queries_in, keys_in, values_in, lse_in, full,
    total_own, total_other, queries, keys, values, lse, weights, grad_t, stats, load,
):
    rows, width = lse.shape[1:]
    span = keys.shape[1]
    loads = []

    def fetch(source, target):
        loads.append(pltpu.make_async_copy(source, target, load.at[len(loads)]))
        loads[-1].start()

    fetch(queries_in, queries)
    fetch(keys_in, keys)
    fetch(values_in, values)
    fetch(lse_in, lse)
    for at in range(0, width, STEP):
        for index in range(3):
            cols = slice(index * width + at, index * width + at + STEP)
            fetch(full.at[:, cols], weights.at[:, cols])

    zero = jnp.zeros((LANES - VROWS, LANES), b16)
    for member in range(2):
        for side, part in enumerate((own, low, high)):
            grad = jnp.concatenate([part[member * VROWS : (member + 1) * VROWS], zero], 0)
            grad_t[member, side * rows : (side + 1) * rows] = grad.astype(f32).T.astype(b16)
    first_stat = 2 * VROWS
    for side, part in enumerate((low, high)):
        at = slice(side * HALO, (side + 1) * HALO)
        pieces = [
            part[first_stat + HEADS * n : first_stat + HEADS * (n + 1)].astype(f32)
            for n in range(5)
        ]
        stats[0, :, at] = pieces[0] + pieces[1]
        stats[1, :, at] = pieces[2] + pieces[3] + pieces[4]

    window = window_mask(rows, span)
    key_at = lax.broadcasted_iota(jnp.int32, (rows, 2 * HALO), 0)
    query_at = lax.broadcasted_iota(jnp.int32, (rows, 2 * HALO), 1)
    reach = ((query_at < HALO) & (query_at >= key_at)) | (
        (query_at >= HALO) & (query_at - HALO <= key_at)
    )
    scaled = head_masks(scale)
    plain = head_masks(1.0)
    center = slice(HALO, HALO + rows)
    halves = [(pair, half) for pair in range(STEP // LANES) for half in range(2)]
    for copy in loads[:4]:
        copy.wait()
    for member in (1, 0):
        total = jnp.zeros((rows, weights.shape[0]), f32)
        for at in range(0, width, STEP):
            step = at // STEP
            grad_att = nt(grad_t[member], mixed[at : at + STEP, :]).astype(b16)
            lanes = [
                slice(at + pair * LANES, at + (pair + 1) * LANES) for pair in range(STEP // LANES)
            ]
            query = [queries[member, center, cols] for cols in lanes]
            key = [keys[member, :, cols] for cols in lanes]
            value = [values[member, :, cols] for cols in lanes]
            far_query = [
                jnp.concatenate(
                    [queries[member, :HALO, cols], queries[member, HALO + rows :, cols]], 0
                )
                for cols in lanes
            ]
            grad = [grad_att[:rows, n * LANES : (n + 1) * LANES] for n in range(len(lanes))]
            far_grad = [grad_att[rows:, n * LANES : (n + 1) * LANES] for n in range(len(lanes))]
            scores = [nt(query[p] * scaled[h], key[p]) for p, h in halves]
            d_probs = [nt(grad[p] * plain[h], value[p]) for p, h in halves]
            probs = []
            for (p, h), score in zip(halves, scores, strict=True):
                start = lanes[p].start + h * (LANES // 2)
                probs.append(
                    jnp.where(window, jnp.exp(score - lse[member, :, start : start + 1]), 0.0)
                )
            deltas = [
                jnp.sum(prob * d_prob, -1, keepdims=True)
                for prob, d_prob in zip(probs, d_probs, strict=True)
            ]
            d_scores = [
                (prob * (d_prob - delta)).astype(b16)
                for prob, d_prob, delta in zip(probs, d_probs, deltas, strict=True)
            ]
            probs = [prob.astype(b16) for prob in probs]
            far_scores = [nt(key[p][center] * scaled[h], far_query[p]) for p, h in halves]
            far_d_probs = [nt(value[p][center] * plain[h], far_grad[p]) for p, h in halves]
            far_probs, far_d_scores = [], []
            for (p, h), score, d_prob in zip(halves, far_scores, far_d_probs, strict=True):
                row = member * (HEADS // 2) + 2 * (step * len(lanes) + p) + h
                prob = jnp.where(reach, jnp.exp(score - stats[1, row : row + 1, :]), 0.0)
                far_d_scores.append((prob * (d_prob - stats[0, row : row + 1, :])).astype(b16))
                far_probs.append(prob.astype(b16))
            d_query, d_key, d_value = [], [], []
            for p in range(len(lanes)):
                first, second = 2 * p, 2 * p + 1
                d_query.append(
                    nn(d_scores[first], key[p] * scaled[0])
                    + nn(d_scores[second], key[p] * scaled[1])
                )
                d_key.append(
                    tn(d_scores[first][:, center], query[p] * scaled[0])
                    + tn(d_scores[second][:, center], query[p] * scaled[1])
                    + nn(far_d_scores[first], far_query[p] * scaled[0])
                    + nn(far_d_scores[second], far_query[p] * scaled[1])
                )
                d_value.append(
                    tn(probs[first][:, center], grad[p] * plain[0])
                    + tn(probs[second][:, center], grad[p] * plain[1])
                    + nn(far_probs[first], far_grad[p] * plain[0])
                    + nn(far_probs[second], far_grad[p] * plain[1])
                )
            for index, part in enumerate((d_query, d_key, d_value)):
                if member == 1:
                    loads[4 + 3 * step + index].wait()
                part = jnp.concatenate(part, 1).astype(b16)
                cols = slice(index * width + at, index * width + at + STEP)
                total = total + nt(part, weights[:, cols])
        if member == 1:
            total_other[...] = total.astype(b16)
        else:
            total_own[...] = total


def final_kernel(
    own, hidden, forcing, inverse_rms, gain, decode, total_own, from_partner, grad_hidden
):
    zero = jnp.zeros((LANES - VROWS, LANES), b16)
    grad_t = jnp.concatenate([own[:VROWS], zero], 0).astype(f32).T.astype(b16)
    grad_resid = nt(grad_t, decode[...])
    xfield = hidden[0].astype(f32) + forcing[...].astype(f32)
    inverse = inverse_rms[...]
    grad = gain[...] * (total_own[...] + from_partner[...].astype(f32))
    mean = jnp.mean(xfield * grad, -1, keepdims=True)
    result = grad_resid + inverse * grad - xfield * (inverse * inverse * inverse * mean)
    grad_hidden[0] = result.astype(b16)


def shifted(value, axis, steps):
    count = lax.axis_size(axis)
    pairs = [(source, (source + steps) % count) for source in range(count)]
    return lax.ppermute(value, axis, pairs)


def permute(value, moves):
    pairs = []
    for x in range(SIDE):
        for z in range(RING_Z):
            for y in range(RING_Y):
                for core in range(2):
                    dx, dz, dc = moves[core]
                    dz = -dz if dz == -2 and z % 2 == 0 else dz
                    dx = -dx if dx == -2 and x % 2 == 0 else dx
                    at = (x, z, core)
                    to = ((x + dx) % SIDE, (z + dz) % RING_Z, core ^ dc)
                    pairs.append(
                        tuple(
                            ((px * SIDE + pz % SIDE) * 2 + pc) * 2 * RING_Y + pz // SIDE * RING_Y + y
                            for px, pz, pc in (at, to)
                        )
                    )
    return lax.ppermute(value, ("ens", "node"), pairs)


def ring(value, along, before=()):
    out = [value]
    for hop in (1, -1, -2):
        if hop == -2 and before:
            value, *before = lax.optimization_barrier((value, *before))
        moves = [(hop, 0, 0) if axis == 0 else (0, hop, 0) for axis in along]
        out.append(permute(value, moves))
    return out + list(before)


def swapped(value):
    return permute(value, [(0, 0, 1)] * 2)


def everyone(value):
    value = value[None]
    for phase in range(2):
        groups = []
        for core in range(2):
            for fixed in range(SIDE):
                chips = [
                    step * SIDE + fixed if core == phase else fixed * SIDE + step
                    for step in range(SIDE)
                ]
                groups.append([2 * chip + core for chip in chips])
        spread = jnp.broadcast_to(value[None], (SIDE,) + value.shape)
        spread = spread.reshape((-1,) + value.shape[1:])
        value = lax.all_to_all(spread, "ens", 0, 0, tiled=True, axis_index_groups=groups)
    return value


def per_device(
    hidden, forcing, norm_gain, w_query, w_key, w_value, w_out, w_decode, targets, area_weight
):
    node_rows = hidden.shape[1]
    width = hidden.shape[2]
    head_size = width // HEADS
    span = node_rows + 2 * HALO
    scale = 1.0 / math.sqrt(head_size)
    members = lax.axis_size("ens")
    shards = lax.axis_size("node")
    rows = w_query.shape[0]
    variables = w_decode.shape[1]
    steps = width // STEP
    shape = jax.ShapeDtypeStruct

    def params(mebibytes):
        return pltpu.CompilerParams(vmem_limit_bytes=mebibytes * 1024 * 1024)

    def cost(us):
        return pl.CostEstimate(
            flops=us * 10**9, transcendentals=0, bytes_accessed=us * 3 * 10**6
        )
    decode = jnp.pad(w_decode, ((0, 0), (0, LANES - variables)))
    mixed = jnp.dot(w_out, decode, preferred_element_type=f32).astype(b16)
    position = lax.axis_index("ens")
    core = position % 2
    place = jnp.stack([position // (2 * SIDE), position // 2 % SIDE, core]).astype(jnp.int32)
    half = width // 2
    both = [
        jnp.concatenate([w[:, at : at + half] for w in (w_query, w_key, w_value)] + [mixed], 1)
        for at in (0, half)
    ]
    keep = jnp.where(core == 0, both[0], both[1])
    partner = swapped(jnp.where(core == 0, both[1], both[0]))
    block = jnp.where(
        core == 0,
        jnp.concatenate([keep, partner], 0),
        jnp.concatenate([partner, keep], 0),
    )
    row = ring(block, (0, 1))
    xfield = hidden[0].astype(f32) + forcing.astype(f32)
    inverse_rms = lax.rsqrt(jnp.mean(xfield * xfield, -1, keepdims=True) + EPS_NORM)
    normed = (xfield * inverse_rms * norm_gain).astype(b16)
    low = shifted(normed, "node", 1)
    high = shifted(normed, "node", -1)
    *pieces, low, high = ring(jnp.concatenate(row, 0), (1, 0), (low, high))
    field = jnp.concatenate([low, normed, high], 0)
    other_field = swapped(field)
    packed_width = 3 * half + LANES

    in_vmem = pl.BlockSpec(memory_space=pltpu.VMEM)
    in_hbm = pl.BlockSpec(memory_space=pltpu.HBM)

    def held(value):
        return pltpu.with_memory_space_constraint(value, pltpu.HBM)

    in_smem = pl.BlockSpec(memory_space=pltpu.SMEM)
    queries, keys, values, attended, lse, partial, mixed, full = pl.pallas_call(
        lambda *refs: forward_kernel(scale, *refs),
        in_specs=[in_smem] + [in_vmem] * (5 + len(pieces)),
        out_specs=[in_hbm, in_hbm, in_hbm, in_vmem, in_vmem, in_vmem, in_vmem, in_hbm],
        out_shape=[
            pltpu.HBM((2, span, half), b16),
            pltpu.HBM((2, span, half), b16),
            pltpu.HBM((2, span, half), b16),
            shape((2, node_rows, half), b16),
            shape((2, node_rows, half), f32),
            shape((2, VROWS, node_rows), f32),
            shape((half, LANES), b16),
            pltpu.HBM((width, packed_width), b16),
        ],
        scratch_shapes=[
            pltpu.VMEM((2, span, half), b16),
            pltpu.VMEM((2, span, half), b16),
            pltpu.VMEM((2, span, half), b16),
            pltpu.VMEM((width, packed_width), b16),
            pltpu.SemaphoreType.DMA((1 + 3 * steps,)),
        ],
        compiler_params=params(24),
        cost_estimate=cost(8),
        name="forward",
    )(place, field, other_field, hidden, forcing, decode, *pieces)
    preds = (partial + swapped(partial)[::-1]).astype(b16)

    others = everyone(preds[0])
    theirs = swapped(others)
    eps = (1.0 - ALPHA) / members
    coeff = (1.0 - eps) / (2.0 * (members - 1))
    truth = jnp.pad(targets, ((0, VROWS - variables), (0, 0)))
    payload = 2 * VROWS + 5 * HEADS
    gram, halo = pl.pallas_call(
        lambda *refs: loss_kernel(coeff, variables, *refs),
        in_specs=[in_smem] + [in_vmem] * 8,
        out_specs=[in_vmem] * 2,
        out_shape=[shape((width, LANES), b16), shape((payload, node_rows), b16)],
        compiler_params=params(12),
        cost_estimate=cost(3),
        name="crps",
    )(place, others, theirs, preds, truth, area_weight[None], attended, mixed, lse)

    halo_low = shifted(halo, "node", 1)
    halo_high = shifted(halo, "node", -1)
    parts = lax.all_to_all(gram.reshape(members, rows, LANES), "ens", 0, 0, tiled=True)
    spread = pl.pallas_call(
        lambda *refs: middle_kernel(variables, *refs),
        in_specs=[in_vmem],
        out_specs=in_vmem,
        out_shape=shape((shards, rows, LANES), b16),
        compiler_params=params(8),
        cost_estimate=cost(1),
        name="middle",
    )(parts)
    parts = lax.all_to_all(spread, "node", 0, 0, tiled=True)
    total = jnp.sum(parts.astype(f32), 0)
    grad_out_proj = lax.dot_general(
        total[:, :variables],
        w_decode.astype(f32),
        (((1,), (1,)), ((), ())),
        preferred_element_type=f32,
    )
    loss = jnp.sum(total[0, variables : variables + 3]) / (members * node_rows * shards * variables)

    total_own, total_other = pl.pallas_call(
        lambda *refs: backward_kernel(scale, *refs),
        in_specs=[in_vmem] * 4 + [in_hbm] * 5,
        out_specs=[in_vmem] * 2,
        out_shape=[shape((node_rows, width), f32), shape((node_rows, width), b16)],
        scratch_shapes=[
            pltpu.VMEM((2, span, half), b16),
            pltpu.VMEM((2, span, half), b16),
            pltpu.VMEM((2, span, half), b16),
            pltpu.VMEM((2, node_rows, half), f32),
            pltpu.VMEM((width, 3 * half), b16),
            pltpu.VMEM((2, span, LANES), b16),
            pltpu.VMEM((2, HEADS, 2 * HALO), f32),
            pltpu.SemaphoreType.DMA((4 + 3 * steps // 2,)),
        ],
        compiler_params=params(24),
        cost_estimate=cost(10),
        name="backward",
    )(halo_low, halo, halo_high, mixed, *[held(part) for part in (queries, keys, values, lse, full)])
    grad_hidden = pl.pallas_call(
        final_kernel,
        in_specs=[in_vmem] * 8,
        out_specs=in_vmem,
        out_shape=shape((1, node_rows, width), b16),
        compiler_params=params(12),
        cost_estimate=cost(2),
        name="final",
    )(
        halo, hidden, forcing, inverse_rms, norm_gain[None], decode, total_own,
        swapped(total_other),
    )
    return (grad_hidden, grad_out_proj, loss)


def solution(mesh):
    placed = (
        P("ens", "node", None),
        P("node", None),
        P(),
        P("ens", None),
        P("ens", None),
        P("ens", None),
        P("ens", None),
        P(),
        P(None, "node"),
        P("node"),
    )
    return jax.shard_map(
        per_device,
        mesh=mesh,
        in_specs=placed,
        out_specs=(P("ens", "node", None), P("ens", None), P()),
        check_vma=False,
    )
```

```python
import math

import jax
import jax.numpy as jnp
from jax import lax
from jax.experimental import pallas as pl
from jax.experimental.pallas import tpu as pltpu
from jax.sharding import PartitionSpec as P

HEADS = 16
HALO = 128
LANES = 128
STEP = 256
VROWS = 112
SIDE = 4
RING_Z = 8
RING_Y = 8
HOPS = (0, SIDE - 1, 1, 2)


ALPHA = 0.95
KAPPA = 0.25
EPS_NORM = 1e-05
FAR = -1e30

f32 = jnp.float32
b16 = jnp.bfloat16


def nn(a, b):
    return lax.dot_general(a, b, (((1,), (0,)), ((), ())), preferred_element_type=f32)


def nt(a, b):
    return lax.dot_general(a, b, (((1,), (1,)), ((), ())), preferred_element_type=f32)


def tn(a, b):
    return lax.dot_general(a, b, (((0,), (0,)), ((), ())), preferred_element_type=f32)


def whole(shape):
    return pl.BlockSpec(shape, lambda i: (0,) * len(shape))


def head_masks(value):
    lane = lax.broadcasted_iota(jnp.int32, (1, LANES), 1)
    first = jnp.where(lane < LANES // 2, value, 0.0).astype(b16)
    second = jnp.where(lane < LANES // 2, 0.0, value).astype(b16)
    return first, second


def window_mask(rows, span):
    offset = lax.broadcasted_iota(jnp.int32, (rows, span), 1) - lax.broadcasted_iota(
        jnp.int32, (rows, span), 0
    )
    return (offset >= 0) & (offset <= 2 * HALO)


def split_bf16(value, pieces):
    out = []
    for _ in range(pieces):
        piece = value.astype(b16)
        out.append(piece)
        value = value - piece.astype(f32)
    return out


def forward_kernel(scale, place, own, other, hidden, forcing, decode, *refs):
    pieces, refs = refs[: len(HOPS)], refs[len(HOPS) :]
    (
        queries_out, keys_out, values_out, attended, lse, pred, mixed, full,
        queries, keys, values, weights, store,
    ) = refs
    span = own.shape[0]
    rows = span - 2 * HALO
    width = attended.shape[2]
    x, z, core = place[0], place[1], place[2]
    side = len(HOPS)
    block = pieces[0].shape[0] // side
    for outer, far in enumerate(HOPS):
        for inner, near in enumerate(HOPS):
            along_x = jnp.where(core == 0, near, far)
            along_z = jnp.where(core == 0, far, near)
            chip = lax.rem(x + along_x, side) * side + lax.rem(z + along_z, side)
            at = pl.multiple_of(chip * block, block)
            weights[pl.ds(at, block), :] = pieces[outer][inner * block : (inner + 1) * block, :]
    stores = [pltpu.make_async_copy(weights, full, store.at[0])]
    stores[0].start()
    mixed[...] = weights[pl.ds(pl.multiple_of(core * width, width), width), 3 * width :]
    window = window_mask(rows, span)
    masks = head_masks(scale)
    lower = lax.broadcasted_iota(jnp.int32, (rows, LANES), 1) < LANES // 2
    pairs = STEP // LANES
    for member, field_ref in enumerate((own, other)):
        if member == 0:
            total = nn(hidden[0], decode[...]) + nn(forcing[...], decode[...])
        else:
            total = jnp.zeros((rows, LANES), f32)
        for at in range(0, width, STEP):
            cols = slice(at, at + STEP)
            field = field_ref[...]
            projected = [
                nn(field, weights[:, index * width + at : index * width + at + STEP]).astype(b16)
                for index in range(3)
            ]
            query, key, value = projected
            for part, scratch, out in zip(
                projected, (queries, keys, values), (queries_out, keys_out, values_out), strict=True
            ):
                scratch[member, :, cols] = part
                stores.append(
                    pltpu.make_async_copy(
                        scratch.at[member, :, cols],
                        out.at[member, :, cols],
                        store.at[len(stores)],
                    )
                )
                stores[-1].start()
            scores = []
            for pair in range(pairs):
                lanes = slice(pair * LANES, (pair + 1) * LANES)
                for mask in masks:
                    scores.append(nt(query[HALO : HALO + rows, lanes] * mask, key[:, lanes]))
            scores = [jnp.where(window, score, FAR) for score in scores]
            tops = [jnp.max(score, -1, keepdims=True) for score in scores]
            expos = [jnp.exp(score - top) for score, top in zip(scores, tops, strict=True)]
            norms = [jnp.sum(expo, -1, keepdims=True) for expo in expos]
            probs = [
                (expo * (1.0 / norm)).astype(b16) for expo, norm in zip(expos, norms, strict=True)
            ]
            outs = [
                nn(prob, value[:, index // 2 * LANES : (index // 2 + 1) * LANES])
                for index, prob in enumerate(probs)
            ]
            stats = [top + jnp.log(norm) for top, norm in zip(tops, norms, strict=True)]
            result = jnp.concatenate(
                [jnp.where(lower, outs[2 * n], outs[2 * n + 1]).astype(b16) for n in range(pairs)],
                1,
            )
            attended[member, :, cols] = result
            lse[member, :, cols] = jnp.concatenate(
                [jnp.where(lower, stats[2 * n], stats[2 * n + 1]) for n in range(pairs)], 1
            )
            total = total + nn(result, mixed[cols, :])
        pred[member] = total.T[:VROWS]
    for copy in stores:
        copy.wait()


def loss_kernel(
    coeff, variables, place, others, theirs, preds, targets, weight, attended, mixed, lse,
    gram, halo,
):
    rows, width = attended.shape[1:]
    heads = HEADS // 2
    truth = targets[...].astype(f32)
    scale = weight[...]
    real = lax.broadcasted_iota(jnp.int32, (VROWS, LANES), 0) < variables
    size = width // heads
    head = lax.broadcasted_iota(jnp.int32, (heads, width), 0)
    feature = lax.broadcasted_iota(jnp.int32, (heads, width), 1)
    inside = jnp.where((feature >= head * size) & (feature < (head + 1) * size), 1.0, 0.0)
    chosen = jnp.where(feature == head * size, 1.0, 0.0).astype(b16)
    inside = inside.astype(b16)
    own, other = preds[0].astype(f32), preds[1].astype(f32)

    def member(index, carry):
        pair_abs, slope_own, slope_other = carry
        for part in (others, theirs):
            value = part[index].astype(f32)
            delta = own - value
            square = delta * delta + KAPPA * KAPPA
            inverse = lax.rsqrt(square)
            pair_abs = pair_abs + (square * inverse - KAPPA)
            slope_own = slope_own + delta * inverse
            delta = other - value
            slope_other = slope_other + delta * lax.rsqrt(delta * delta + KAPPA * KAPPA)
        return pair_abs, slope_own, slope_other

    zero = jnp.zeros((VROWS, LANES), f32)
    pair_abs, *slopes = lax.fori_loop(0, others.shape[0], member, (zero, zero, zero), unroll=2)
    parts = jnp.zeros((LANES, width), f32)
    row_delta, row_lse = [], []
    for index, value in enumerate((own, other)):
        delta = value - truth
        square = delta * delta + KAPPA * KAPPA
        inverse = lax.rsqrt(square)
        if index == 0:
            entries = scale * (square * inverse - KAPPA - coeff * pair_abs)
            entries = jnp.where(real, entries, 0.0)
            loss = jnp.sum(jnp.sum(entries, 0, keepdims=True), 1, keepdims=True)
        grad = jnp.where(real, scale * (delta * inverse - 2.0 * coeff * slopes[index]), 0.0)
        halo[index * VROWS : (index + 1) * VROWS] = grad.astype(b16)
        grad_full = jnp.concatenate([grad, jnp.zeros((LANES - VROWS, LANES), f32)], 0)
        grad_t = grad_full.T.astype(b16)
        parts = parts + nn(grad_full.astype(b16), attended[index])
        grad_att = nt(grad_t, mixed[...]).astype(b16)
        product = grad_att.astype(f32) * attended[index].astype(f32)
        row_delta.append(sum(nt(inside, piece) for piece in split_bf16(product, 2)))
        row_lse.append(sum(nt(chosen, piece) for piece in split_bf16(lse[index], 3)))
    at = 2 * VROWS
    for pieces in (
        split_bf16(jnp.concatenate(row_delta, 0), 2),
        split_bf16(jnp.concatenate(row_lse, 0), 3),
    ):
        for piece in pieces:
            halo[at : at + HEADS] = piece
            at += HEADS
    column = lax.broadcasted_iota(jnp.int32, (width, LANES), 1)
    parts = parts.T
    blank = jnp.zeros((width, LANES), f32)
    for index, piece in enumerate(split_bf16(loss, 3)):
        parts = jnp.where(column == variables + index, piece.astype(f32), parts)
        blank = jnp.where(column == variables + index, piece.astype(f32), blank)
    core = place[2]
    gram[pl.ds(pl.multiple_of(core * width, width), width), :] = parts.astype(b16)
    gram[pl.ds(pl.multiple_of((1 - core) * width, width), width), :] = blank.astype(b16)


def middle_kernel(variables, parts, spread):
    total = parts[0].astype(f32)
    for index in range(1, parts.shape[0]):
        total = total + parts[index].astype(f32)
    column = lax.broadcasted_iota(jnp.int32, total.shape, 1)
    spare = (column >= variables) & (column < variables + 3)
    loss = jnp.sum(jnp.where(spare, total, 0.0), 1, keepdims=True)
    for index, piece in enumerate(split_bf16(loss, 3)):
        total = jnp.where(column == variables + index, piece.astype(f32), total)
    total = total.astype(b16)
    for index in range(spread.shape[0]):
        spread[index] = total


def backward_kernel(
    scale, low, own, high, mixed, queries_in, keys_in, values_in, lse_in, full,
    total_own, total_other, queries, keys, values, lse, weights, grad_t, stats, load,
):
    rows, width = lse.shape[1:]
    span = keys.shape[1]
    loads = []

    def fetch(source, target):
        loads.append(pltpu.make_async_copy(source, target, load.at[len(loads)]))
        loads[-1].start()

    fetch(queries_in, queries)
    fetch(keys_in, keys)
    fetch(values_in, values)
    fetch(lse_in, lse)
    for at in range(0, width, STEP):
        for index in range(3):
            cols = slice(index * width + at, index * width + at + STEP)
            fetch(full.at[:, cols], weights.at[:, cols])

    zero = jnp.zeros((LANES - VROWS, LANES), b16)
    for member in range(2):
        for side, part in enumerate((own, low, high)):
            grad = jnp.concatenate([part[member * VROWS : (member + 1) * VROWS], zero], 0)
            grad_t[member, side * rows : (side + 1) * rows] = grad.astype(f32).T.astype(b16)
    first_stat = 2 * VROWS
    for side, part in enumerate((low, high)):
        at = slice(side * HALO, (side + 1) * HALO)
        pieces = [
            part[first_stat + HEADS * n : first_stat + HEADS * (n + 1)].astype(f32)
            for n in range(5)
        ]
        stats[0, :, at] = pieces[0] + pieces[1]
        stats[1, :, at] = pieces[2] + pieces[3] + pieces[4]

    window = window_mask(rows, span)
    key_at = lax.broadcasted_iota(jnp.int32, (rows, 2 * HALO), 0)
    query_at = lax.broadcasted_iota(jnp.int32, (rows, 2 * HALO), 1)
    reach = ((query_at < HALO) & (query_at >= key_at)) | (
        (query_at >= HALO) & (query_at - HALO <= key_at)
    )
    scaled = head_masks(scale)
    plain = head_masks(1.0)
    center = slice(HALO, HALO + rows)
    halves = [(pair, half) for pair in range(STEP // LANES) for half in range(2)]
    for copy in loads[:4]:
        copy.wait()
    for member in (1, 0):
        total = jnp.zeros((rows, weights.shape[0]), f32)
        for at in range(0, width, STEP):
            step = at // STEP
            grad_att = nt(grad_t[member], mixed[at : at + STEP, :]).astype(b16)
            lanes = [
                slice(at + pair * LANES, at + (pair + 1) * LANES) for pair in range(STEP // LANES)
            ]
            query = [queries[member, center, cols] for cols in lanes]
            key = [keys[member, :, cols] for cols in lanes]
            value = [values[member, :, cols] for cols in lanes]
            far_query = [
                jnp.concatenate(
                    [queries[member, :HALO, cols], queries[member, HALO + rows :, cols]], 0
                )
                for cols in lanes
            ]
            grad = [grad_att[:rows, n * LANES : (n + 1) * LANES] for n in range(len(lanes))]
            far_grad = [grad_att[rows:, n * LANES : (n + 1) * LANES] for n in range(len(lanes))]
            scores = [nt(query[p] * scaled[h], key[p]) for p, h in halves]
            d_probs = [nt(grad[p] * plain[h], value[p]) for p, h in halves]
            probs = []
            for (p, h), score in zip(halves, scores, strict=True):
                start = lanes[p].start + h * (LANES // 2)
                probs.append(
                    jnp.where(window, jnp.exp(score - lse[member, :, start : start + 1]), 0.0)
                )
            deltas = [
                jnp.sum(prob * d_prob, -1, keepdims=True)
                for prob, d_prob in zip(probs, d_probs, strict=True)
            ]
            d_scores = [
                (prob * (d_prob - delta)).astype(b16)
                for prob, d_prob, delta in zip(probs, d_probs, deltas, strict=True)
            ]
            probs = [prob.astype(b16) for prob in probs]
            far_scores = [nt(key[p][center] * scaled[h], far_query[p]) for p, h in halves]
            far_d_probs = [nt(value[p][center] * plain[h], far_grad[p]) for p, h in halves]
            far_probs, far_d_scores = [], []
            for (p, h), score, d_prob in zip(halves, far_scores, far_d_probs, strict=True):
                row = member * (HEADS // 2) + 2 * (step * len(lanes) + p) + h
                prob = jnp.where(reach, jnp.exp(score - stats[1, row : row + 1, :]), 0.0)
                far_d_scores.append((prob * (d_prob - stats[0, row : row + 1, :])).astype(b16))
                far_probs.append(prob.astype(b16))
            d_query, d_key, d_value = [], [], []
            for p in range(len(lanes)):
                first, second = 2 * p, 2 * p + 1
                d_query.append(
                    nn(d_scores[first], key[p] * scaled[0])
                    + nn(d_scores[second], key[p] * scaled[1])
                )
                d_key.append(
                    tn(d_scores[first][:, center], query[p] * scaled[0])
                    + tn(d_scores[second][:, center], query[p] * scaled[1])
                    + nn(far_d_scores[first], far_query[p] * scaled[0])
                    + nn(far_d_scores[second], far_query[p] * scaled[1])
                )
                d_value.append(
                    tn(probs[first][:, center], grad[p] * plain[0])
                    + tn(probs[second][:, center], grad[p] * plain[1])
                    + nn(far_probs[first], far_grad[p] * plain[0])
                    + nn(far_probs[second], far_grad[p] * plain[1])
                )
            for index, part in enumerate((d_query, d_key, d_value)):
                if member == 1:
                    loads[4 + 3 * step + index].wait()
                part = jnp.concatenate(part, 1).astype(b16)
                cols = slice(index * width + at, index * width + at + STEP)
                total = total + nt(part, weights[:, cols])
        if member == 1:
            total_other[...] = total.astype(b16)
        else:
            total_own[...] = total


def final_kernel(
    own, hidden, forcing, inverse_rms, gain, decode, total_own, from_partner, grad_hidden
):
    zero = jnp.zeros((LANES - VROWS, LANES), b16)
    grad_t = jnp.concatenate([own[:VROWS], zero], 0).astype(f32).T.astype(b16)
    grad_resid = nt(grad_t, decode[...])
    xfield = hidden[0].astype(f32) + forcing[...].astype(f32)
    inverse = inverse_rms[...]
    grad = gain[...] * (total_own[...] + from_partner[...].astype(f32))
    mean = jnp.mean(xfield * grad, -1, keepdims=True)
    result = grad_resid + inverse * grad - xfield * (inverse * inverse * inverse * mean)
    grad_hidden[0] = result.astype(b16)


def shifted(value, axis, steps):
    count = lax.axis_size(axis)
    pairs = [(source, (source + steps) % count) for source in range(count)]
    return lax.ppermute(value, axis, pairs)


def permute(value, moves):
    pairs = []
    for x in range(SIDE):
        for z in range(RING_Z):
            for y in range(RING_Y):
                for core in range(2):
                    dx, dz, dc = moves[core]
                    dz = -dz if dz == -2 and z % 2 == 0 else dz
                    dx = -dx if dx == -2 and x % 2 == 0 else dx
                    at = (x, z, core)
                    to = ((x + dx) % SIDE, (z + dz) % RING_Z, core ^ dc)
                    pairs.append(
                        tuple(
                            ((px * SIDE + pz % SIDE) * 2 + pc) * 2 * RING_Y + pz // SIDE * RING_Y + y
                            for px, pz, pc in (at, to)
                        )
                    )
    return lax.ppermute(value, ("ens", "node"), pairs)


def ring(value, along, before=()):
    blocks = {0: value}
    for hop in (-2, 1, -1):
        if hop == -1 and before:
            value, *before = lax.optimization_barrier((value, *before))
        moves = [(hop, 0, 0) if axis == 0 else (0, hop, 0) for axis in along]
        blocks[hop] = permute(value, moves)
    return [blocks[0], blocks[1], blocks[-1], blocks[-2], *before]


def swapped(value):
    return permute(value, [(0, 0, 1)] * 2)


def everyone(value):
    value = value[None]
    for phase in range(2):
        groups = []
        for core in range(2):
            for fixed in range(SIDE):
                chips = [
                    step * SIDE + fixed if core == phase else fixed * SIDE + step
                    for step in range(SIDE)
                ]
                groups.append([2 * chip + core for chip in chips])
        spread = jnp.broadcast_to(value[None], (SIDE,) + value.shape)
        spread = spread.reshape((-1,) + value.shape[1:])
        value = lax.all_to_all(spread, "ens", 0, 0, tiled=True, axis_index_groups=groups)
    return value


def per_device(
    hidden, forcing, norm_gain, w_query, w_key, w_value, w_out, w_decode, targets, area_weight
):
    node_rows = hidden.shape[1]
    width = hidden.shape[2]
    head_size = width // HEADS
    span = node_rows + 2 * HALO
    scale = 1.0 / math.sqrt(head_size)
    members = lax.axis_size("ens")
    shards = lax.axis_size("node")
    rows = w_query.shape[0]
    variables = w_decode.shape[1]
    steps = width // STEP
    shape = jax.ShapeDtypeStruct

    def params(mebibytes):
        return pltpu.CompilerParams(vmem_limit_bytes=mebibytes * 1024 * 1024)

    def cost(us):
        return pl.CostEstimate(
            flops=us * 10**9, transcendentals=0, bytes_accessed=us * 3 * 10**6
        )
    decode = jnp.pad(w_decode, ((0, 0), (0, LANES - variables)))
    mixed = jnp.dot(w_out, decode, preferred_element_type=f32).astype(b16)
    position = lax.axis_index("ens")
    core = position % 2
    place = jnp.stack([position // (2 * SIDE), position // 2 % SIDE, core]).astype(jnp.int32)
    half = width // 2
    both = [
        jnp.concatenate([w[:, at : at + half] for w in (w_query, w_key, w_value)] + [mixed], 1)
        for at in (0, half)
    ]
    keep = jnp.where(core == 0, both[0], both[1])
    partner = swapped(jnp.where(core == 0, both[1], both[0]))
    block = jnp.where(
        core == 0,
        jnp.concatenate([keep, partner], 0),
        jnp.concatenate([partner, keep], 0),
    )
    row = ring(block, (0, 1))
    xfield = hidden[0].astype(f32) + forcing.astype(f32)
    inverse_rms = lax.rsqrt(jnp.mean(xfield * xfield, -1, keepdims=True) + EPS_NORM)
    normed = (xfield * inverse_rms * norm_gain).astype(b16)
    low = shifted(normed, "node", 1)
    high = shifted(normed, "node", -1)
    *pieces, low, high = ring(jnp.concatenate(row, 0), (1, 0), (low, high))
    field = jnp.concatenate([low, normed, high], 0)
    other_field = swapped(field)
    packed_width = 3 * half + LANES

    in_vmem = pl.BlockSpec(memory_space=pltpu.VMEM)
    in_hbm = pl.BlockSpec(memory_space=pltpu.HBM)

    def held(value):
        return pltpu.with_memory_space_constraint(value, pltpu.HBM)

    in_smem = pl.BlockSpec(memory_space=pltpu.SMEM)
    queries, keys, values, attended, lse, partial, mixed, full = pl.pallas_call(
        lambda *refs: forward_kernel(scale, *refs),
        in_specs=[in_smem] + [in_vmem] * (5 + len(pieces)),
        out_specs=[in_hbm, in_hbm, in_hbm, in_vmem, in_vmem, in_vmem, in_vmem, in_hbm],
        out_shape=[
            pltpu.HBM((2, span, half), b16),
            pltpu.HBM((2, span, half), b16),
            pltpu.HBM((2, span, half), b16),
            shape((2, node_rows, half), b16),
            shape((2, node_rows, half), f32),
            shape((2, VROWS, node_rows), f32),
            shape((half, LANES), b16),
            pltpu.HBM((width, packed_width), b16),
        ],
        scratch_shapes=[
            pltpu.VMEM((2, span, half), b16),
            pltpu.VMEM((2, span, half), b16),
            pltpu.VMEM((2, span, half), b16),
            pltpu.VMEM((width, packed_width), b16),
            pltpu.SemaphoreType.DMA((1 + 3 * steps,)),
        ],
        compiler_params=params(24),
        cost_estimate=cost(8),
        name="forward",
    )(place, field, other_field, hidden, forcing, decode, *pieces)
    preds = (partial + swapped(partial)[::-1]).astype(b16)

    others = everyone(preds[0])
    theirs = swapped(others)
    eps = (1.0 - ALPHA) / members
    coeff = (1.0 - eps) / (2.0 * (members - 1))
    truth = jnp.pad(targets, ((0, VROWS - variables), (0, 0)))
    payload = 2 * VROWS + 5 * HEADS
    gram, halo = pl.pallas_call(
        lambda *refs: loss_kernel(coeff, variables, *refs),
        in_specs=[in_smem] + [in_vmem] * 8,
        out_specs=[in_vmem] * 2,
        out_shape=[shape((width, LANES), b16), shape((payload, node_rows), b16)],
        compiler_params=params(12),
        cost_estimate=cost(3),
        name="crps",
    )(place, others, theirs, preds, truth, area_weight[None], attended, mixed, lse)

    halo_low = shifted(halo, "node", 1)
    halo_high = shifted(halo, "node", -1)
    parts = lax.all_to_all(gram.reshape(members, rows, LANES), "ens", 0, 0, tiled=True)
    spread = pl.pallas_call(
        lambda *refs: middle_kernel(variables, *refs),
        in_specs=[in_vmem],
        out_specs=in_vmem,
        out_shape=shape((shards, rows, LANES), b16),
        compiler_params=params(8),
        cost_estimate=cost(1),
        name="middle",
    )(parts)
    halo, spread = lax.optimization_barrier((halo, spread))
    parts = lax.all_to_all(spread, "node", 0, 0, tiled=True)
    total = jnp.sum(parts.astype(f32), 0)
    grad_out_proj = lax.dot_general(
        total[:, :variables],
        w_decode.astype(f32),
        (((1,), (1,)), ((), ())),
        preferred_element_type=f32,
    )
    loss = jnp.sum(total[0, variables : variables + 3]) / (members * node_rows * shards * variables)

    total_own, total_other = pl.pallas_call(
        lambda *refs: backward_kernel(scale, *refs),
        in_specs=[in_vmem] * 4 + [in_hbm] * 5,
        out_specs=[in_vmem] * 2,
        out_shape=[shape((node_rows, width), f32), shape((node_rows, width), b16)],
        scratch_shapes=[
            pltpu.VMEM((2, span, half), b16),
            pltpu.VMEM((2, span, half), b16),
            pltpu.VMEM((2, span, half), b16),
            pltpu.VMEM((2, node_rows, half), f32),
            pltpu.VMEM((width, 3 * half), b16),
            pltpu.VMEM((2, span, LANES), b16),
            pltpu.VMEM((2, HEADS, 2 * HALO), f32),
            pltpu.SemaphoreType.DMA((4 + 3 * steps // 2,)),
        ],
        compiler_params=params(24),
        cost_estimate=cost(10),
        name="backward",
    )(halo_low, halo, halo_high, mixed, *[held(part) for part in (queries, keys, values, lse, full)])
    grad_hidden = pl.pallas_call(
        final_kernel,
        in_specs=[in_vmem] * 8,
        out_specs=in_vmem,
        out_shape=shape((1, node_rows, width), b16),
        compiler_params=params(12),
        cost_estimate=cost(2),
        name="final",
    )(
        halo, hidden, forcing, inverse_rms, norm_gain[None], decode, total_own,
        swapped(total_other),
    )
    return (grad_hidden, grad_out_proj, loss)


def solution(mesh):
    placed = (
        P("ens", "node", None),
        P("node", None),
        P(),
        P("ens", None),
        P("ens", None),
        P("ens", None),
        P("ens", None),
        P(),
        P(None, "node"),
        P("node"),
    )
    return jax.shard_map(
        per_device,
        mesh=mesh,
        in_specs=placed,
        out_specs=(P("ens", "node", None), P("ens", None), P()),
        check_vma=False,
    )
```

```python
import math

import jax
import jax.numpy as jnp
from jax import lax
from jax.experimental import pallas as pl
from jax.experimental.pallas import tpu as pltpu
from jax.sharding import PartitionSpec as P

HEADS = 16
HALO = 128
LANES = 128
STEP = 256
VROWS = 112
SIDE = 4
RING_Z = 8
RING_Y = 8
HOPS = (0, SIDE - 1, 1, 2)


ALPHA = 0.95
KAPPA = 0.25
EPS_NORM = 1e-05
FAR = -1e30

f32 = jnp.float32
b16 = jnp.bfloat16


def nn(a, b):
    return lax.dot_general(a, b, (((1,), (0,)), ((), ())), preferred_element_type=f32)


def nt(a, b):
    return lax.dot_general(a, b, (((1,), (1,)), ((), ())), preferred_element_type=f32)


def tn(a, b):
    return lax.dot_general(a, b, (((0,), (0,)), ((), ())), preferred_element_type=f32)


def whole(shape):
    return pl.BlockSpec(shape, lambda i: (0,) * len(shape))


def head_masks(value):
    lane = lax.broadcasted_iota(jnp.int32, (1, LANES), 1)
    first = jnp.where(lane < LANES // 2, value, 0.0).astype(b16)
    second = jnp.where(lane < LANES // 2, 0.0, value).astype(b16)
    return first, second


def window_mask(rows, span):
    offset = lax.broadcasted_iota(jnp.int32, (rows, span), 1) - lax.broadcasted_iota(
        jnp.int32, (rows, span), 0
    )
    return (offset >= 0) & (offset <= 2 * HALO)


def split_bf16(value, pieces):
    out = []
    for _ in range(pieces):
        piece = value.astype(b16)
        out.append(piece)
        value = value - piece.astype(f32)
    return out


def forward_kernel(scale, place, low, own, high, wrapped, hidden, forcing, decode_t, *refs):
    pieces, refs = refs[: 2 * len(HOPS)], refs[2 * len(HOPS) :]
    (
        queries_out, keys_out, values_out, attended, lse_out, pred, mixed, full,
        queries, keys, values, lse, normed, weights, store,
    ) = refs
    rows, width = own.shape
    span = rows + 2 * HALO
    x, z, core = place[0], place[1], place[2]
    side = len(HOPS)
    block = pieces[0].shape[0] // side
    for mine in (True, False):
        which = core if mine else 1 - core
        for outer, far in enumerate(HOPS):
            piece = pieces[outer if mine else side + outer]
            for inner, near in enumerate(HOPS):
                along_x = jnp.where(which == 0, near, far)
                along_z = jnp.where(which == 0, far, near)
                chip = lax.rem(x + along_x, side) * side + lax.rem(z + along_z, side)
                at = pl.multiple_of((chip * 2 + which) * block, block)
                weights[pl.ds(at, block), :] = piece[inner * block : (inner + 1) * block, :]
    stores = [pltpu.make_async_copy(weights, full, store.at[0])]
    stores[0].start()
    mixed[...] = weights[:, 3 * width :]
    at_y = place[3]
    normed[:HALO] = jnp.where(at_y == 0, wrapped[...], low[...])
    normed[HALO : HALO + rows] = own[...]
    normed[HALO + rows :] = jnp.where(at_y == RING_Y - 1, wrapped[...], high[...])
    total = nt(hidden[0], decode_t[...]) + nt(forcing[...], decode_t[...])
    window = window_mask(rows, span)
    masks = head_masks(scale)
    lower = lax.broadcasted_iota(jnp.int32, (rows, LANES), 1) < LANES // 2
    pairs = STEP // LANES
    for at in range(0, width, STEP):
        cols = slice(at, at + STEP)
        field = normed[...]
        projected = [
            nn(field, weights[:, index * width + at : index * width + at + STEP]).astype(b16)
            for index in range(3)
        ]
        query, key, value = projected
        for part, scratch, out in zip(
            projected, (queries, keys, values), (queries_out, keys_out, values_out), strict=True
        ):
            scratch[:, cols] = part
            stores.append(
                pltpu.make_async_copy(scratch.at[:, cols], out.at[:, cols], store.at[len(stores)])
            )
            stores[-1].start()
        scores = []
        for pair in range(pairs):
            lanes = slice(pair * LANES, (pair + 1) * LANES)
            for mask in masks:
                scores.append(nt(query[HALO : HALO + rows, lanes] * mask, key[:, lanes]))
        scores = [jnp.where(window, score, FAR) for score in scores]
        tops = [jnp.max(score, -1, keepdims=True) for score in scores]
        expos = [jnp.exp(score - top) for score, top in zip(scores, tops, strict=True)]
        norms = [jnp.sum(expo, -1, keepdims=True) for expo in expos]
        probs = [(expo * (1.0 / norm)).astype(b16) for expo, norm in zip(expos, norms, strict=True)]
        outs = [
            nn(prob, value[:, index // 2 * LANES : (index // 2 + 1) * LANES])
            for index, prob in enumerate(probs)
        ]
        stats = [top + jnp.log(norm) for top, norm in zip(tops, norms, strict=True)]
        result = jnp.concatenate(
            [jnp.where(lower, outs[2 * n], outs[2 * n + 1]).astype(b16) for n in range(pairs)], 1
        )
        attended[:, cols] = result
        lse[:, cols] = jnp.concatenate(
            [jnp.where(lower, stats[2 * n], stats[2 * n + 1]) for n in range(pairs)], 1
        )
        stores.append(
            pltpu.make_async_copy(lse.at[:, cols], lse_out.at[:, cols], store.at[len(stores)])
        )
        stores[-1].start()
        total = total + nn(result, mixed[cols, :])
    pred[...] = total.T[:VROWS].astype(b16)
    for copy in stores:
        copy.wait()


def loss_kernel(
    coeff, variables, others, theirs, pred, targets, weight, attended, mixed, lse,
    gram, halo,
):
    own = pred[...].astype(f32)
    rows = attended.shape[0]
    width = attended.shape[1]

    def member(index, carry):
        pair_abs, pair_slope = carry
        for part in (others, theirs):
            delta = own - part[index].astype(f32)
            square = delta * delta + KAPPA * KAPPA
            inverse = lax.rsqrt(square)
            pair_abs = pair_abs + (square * inverse - KAPPA)
            pair_slope = pair_slope + delta * inverse
        return pair_abs, pair_slope

    zero = jnp.zeros((VROWS, LANES), f32)
    pair_abs, pair_slope = lax.fori_loop(0, others.shape[0], member, (zero, zero), unroll=2)
    delta = own - targets[...].astype(f32)
    square = delta * delta + KAPPA * KAPPA
    inverse = lax.rsqrt(square)
    real = lax.broadcasted_iota(jnp.int32, (VROWS, LANES), 0) < variables
    scale = weight[...]
    entries = jnp.where(real, scale * (square * inverse - KAPPA - coeff * pair_abs), 0.0)
    loss = jnp.sum(jnp.sum(entries, 0, keepdims=True), 1, keepdims=True)
    grad = jnp.where(real, scale * (delta * inverse - 2.0 * coeff * pair_slope), 0.0)
    grad_b = grad.astype(b16)
    halo[:VROWS] = grad_b
    grad_full = jnp.concatenate([grad, jnp.zeros((LANES - VROWS, LANES), f32)], 0)
    grad_t = grad_full.T.astype(b16)
    parts = nn(grad_full.astype(b16), attended[...])
    parts = parts.T
    column = lax.broadcasted_iota(jnp.int32, (width, LANES), 1)
    for index, piece in enumerate(split_bf16(loss, 3)):
        parts = jnp.where(column == variables + index, piece.astype(f32), parts)
    gram[...] = parts.astype(b16)
    grad_att = nt(grad_t, mixed[...]).astype(b16)
    size = width // HEADS
    head = lax.broadcasted_iota(jnp.int32, (HEADS, width), 0)
    feature = lax.broadcasted_iota(jnp.int32, (HEADS, width), 1)
    inside = jnp.where((feature >= head * size) & (feature < (head + 1) * size), 1.0, 0.0)
    chosen = jnp.where(feature == head * size, 1.0, 0.0).astype(b16)
    inside = inside.astype(b16)
    product = grad_att.astype(f32) * attended[...].astype(f32)
    row_delta = sum(nt(inside, piece) for piece in split_bf16(product, 2))
    row_lse = sum(nt(chosen, piece) for piece in split_bf16(lse[...], 3))
    at = VROWS
    for piece in split_bf16(row_delta, 2) + split_bf16(row_lse, 3):
        halo[at : at + HEADS] = piece
        at += HEADS


def middle_kernel(variables, parts, spread):
    total = parts[0].astype(f32)
    for index in range(1, parts.shape[0]):
        total = total + parts[index].astype(f32)
    column = lax.broadcasted_iota(jnp.int32, total.shape, 1)
    spare = (column >= variables) & (column < variables + 3)
    loss = jnp.sum(jnp.where(spare, total, 0.0), 1, keepdims=True)
    for index, piece in enumerate(split_bf16(loss, 3)):
        total = jnp.where(column == variables + index, piece.astype(f32), total)
    total = total.astype(b16)
    for index in range(spread.shape[0]):
        spread[index] = total


def last_kernel(variables, factor, parts, decode_t, grad_out, loss):
    total = parts[0].astype(f32)
    for index in range(1, parts.shape[0]):
        total = total + parts[index].astype(f32)
    column = lax.broadcasted_iota(jnp.int32, total.shape, 1)
    spare = (column >= variables) & (column < variables + 3)
    first = jnp.sum(jnp.where(spare, total, 0.0), 1, keepdims=True)[:1]
    loss[...] = jnp.broadcast_to(first * factor, loss.shape)
    real = jnp.where(column < variables, total, 0.0)
    grad_out[...] = sum(nn(piece, decode_t[...]) for piece in split_bf16(real, 2))


def backward_kernel(
    scale, place, low_part, own, high_part, wrapped, hidden, forcing, inverse_rms, gain, decode_t, mixed,
    queries_in, keys_in, values_in, lse_in, full,
    grad_hidden, queries, keys, values, lse, weights, grad_t, stats, load,
):
    rows, width = lse.shape
    span = keys.shape[0]
    loads = []

    def fetch(source, target):
        loads.append(pltpu.make_async_copy(source, target, load.at[len(loads)]))
        loads[-1].start()

    fetch(queries_in, queries)
    fetch(keys_in, keys)
    fetch(values_in, values)
    fetch(lse_in, lse)
    for at in range(0, width, STEP):
        for index in range(3):
            cols = slice(index * width + at, index * width + at + STEP)
            fetch(full.at[:, cols], weights.at[:, cols])

    at_y = place[3]
    low = jnp.where(at_y == 0, wrapped[...], low_part[...])
    high = jnp.where(at_y == RING_Y - 1, wrapped[...], high_part[...])
    zero = jnp.zeros((LANES - VROWS, LANES), b16)
    for side, part in enumerate((own[...], low, high)):
        grad = jnp.concatenate([part[:VROWS], zero], 0)
        grad_t[side * rows : (side + 1) * rows] = grad.astype(f32).T.astype(b16)
    for side, part in enumerate((low, high)):
        at = slice(side * HALO, (side + 1) * HALO)
        pieces = [part[VROWS + HEADS * n : VROWS + HEADS * (n + 1)].astype(f32) for n in range(5)]
        stats[0, :, at] = pieces[0] + pieces[1]
        stats[1, :, at] = pieces[2] + pieces[3] + pieces[4]
    grad_resid = nn(grad_t[:rows], decode_t[...])

    window = window_mask(rows, span)
    key_at = lax.broadcasted_iota(jnp.int32, (rows, 2 * HALO), 0)
    query_at = lax.broadcasted_iota(jnp.int32, (rows, 2 * HALO), 1)
    reach = ((query_at < HALO) & (query_at >= key_at)) | (
        (query_at >= HALO) & (query_at - HALO <= key_at)
    )
    scaled = head_masks(scale)
    plain = head_masks(1.0)
    center = slice(HALO, HALO + rows)
    halves = [(pair, half) for pair in range(STEP // LANES) for half in range(2)]
    total = jnp.zeros((rows, width), f32)
    for copy in loads[:4]:
        copy.wait()
    for at in range(0, width, STEP):
        step = at // STEP
        grad_att = nt(grad_t[...], mixed[at : at + STEP, :]).astype(b16)
        lanes = [slice(at + pair * LANES, at + (pair + 1) * LANES) for pair in range(STEP // LANES)]
        query = [queries[center, cols] for cols in lanes]
        key = [keys[:, cols] for cols in lanes]
        value = [values[:, cols] for cols in lanes]
        far_query = [
            jnp.concatenate([queries[:HALO, cols], queries[HALO + rows :, cols]], 0)
            for cols in lanes
        ]
        grad = [grad_att[:rows, n * LANES : (n + 1) * LANES] for n in range(len(lanes))]
        far_grad = [grad_att[rows:, n * LANES : (n + 1) * LANES] for n in range(len(lanes))]
        scores = [nt(query[p] * scaled[h], key[p]) for p, h in halves]
        d_probs = [nt(grad[p] * plain[h], value[p]) for p, h in halves]
        probs = []
        for (p, h), score in zip(halves, scores, strict=True):
            start = lanes[p].start + h * (LANES // 2)
            probs.append(jnp.where(window, jnp.exp(score - lse[:, start : start + 1]), 0.0))
        deltas = [
            jnp.sum(prob * d_prob, -1, keepdims=True)
            for prob, d_prob in zip(probs, d_probs, strict=True)
        ]
        d_scores = [
            (prob * (d_prob - delta)).astype(b16)
            for prob, d_prob, delta in zip(probs, d_probs, deltas, strict=True)
        ]
        probs = [prob.astype(b16) for prob in probs]
        far_scores = [nt(key[p][center] * scaled[h], far_query[p]) for p, h in halves]
        far_d_probs = [nt(value[p][center] * plain[h], far_grad[p]) for p, h in halves]
        far_probs, far_d_scores = [], []
        for (p, h), score, d_prob in zip(halves, far_scores, far_d_probs, strict=True):
            row = 2 * (step * len(lanes) + p) + h
            prob = jnp.where(reach, jnp.exp(score - stats[1, row : row + 1, :]), 0.0)
            far_d_scores.append((prob * (d_prob - stats[0, row : row + 1, :])).astype(b16))
            far_probs.append(prob.astype(b16))
        d_query, d_key, d_value = [], [], []
        for p in range(len(lanes)):
            first, second = 2 * p, 2 * p + 1
            d_query.append(
                nn(d_scores[first], key[p] * scaled[0]) + nn(d_scores[second], key[p] * scaled[1])
            )
            d_key.append(
                tn(d_scores[first][:, center], query[p] * scaled[0])
                + tn(d_scores[second][:, center], query[p] * scaled[1])
                + nn(far_d_scores[first], far_query[p] * scaled[0])
                + nn(far_d_scores[second], far_query[p] * scaled[1])
            )
            d_value.append(
                tn(probs[first][:, center], grad[p] * plain[0])
                + tn(probs[second][:, center], grad[p] * plain[1])
                + nn(far_probs[first], far_grad[p] * plain[0])
                + nn(far_probs[second], far_grad[p] * plain[1])
            )
        for index, part in enumerate((d_query, d_key, d_value)):
            loads[4 + 3 * step + index].wait()
            part = jnp.concatenate(part, 1).astype(b16)
            cols = slice(index * width + at, index * width + at + STEP)
            total = total + nt(part, weights[:, cols])
    xfield = hidden[0].astype(f32) + forcing[...].astype(f32)
    inverse = inverse_rms[...]
    grad = gain[...] * total
    mean = jnp.mean(xfield * grad, -1, keepdims=True)
    result = grad_resid + inverse * grad - xfield * (inverse * inverse * inverse * mean)
    grad_hidden[0] = result.astype(b16)


def halos(value):
    up = [(n, n + 1) for n in range(2 * RING_Y) if n % RING_Y < RING_Y - 1]
    turn = [(RING_Y - 1, RING_Y), (2 * RING_Y - 1, 0)]
    low = lax.ppermute(value, "node", up)
    high = lax.ppermute(value, "node", [(b, a) for a, b in up])
    wrapped = lax.ppermute(value, "node", turn + [(b, a) for a, b in turn])
    return low, high, wrapped


def permute(value, moves):
    pairs = []
    for x in range(SIDE):
        for z in range(RING_Z):
            for y in range(RING_Y):
                for core in range(2):
                    dx, dz, dc = moves[core]
                    dz = -dz if dz == -2 and z % 2 == 0 else dz
                    dx = -dx if dx == -2 and x % 2 == 0 else dx
                    at = (x, z, core)
                    to = ((x + dx) % SIDE, (z + dz) % RING_Z, core ^ dc)
                    pairs.append(
                        tuple(
                            ((px * SIDE + pz % SIDE) * 2 + pc) * 2 * RING_Y + pz // SIDE * RING_Y + y
                            for px, pz, pc in (at, to)
                        )
                    )
    return lax.ppermute(value, ("ens", "node"), pairs)


def ring(value, along, before=()):
    out = [value]
    for hop in (1, -1, -2):
        if hop == -2 and before:
            value, *before = lax.optimization_barrier((value, *before))
        moves = [(hop, 0, 0) if axis == 0 else (0, hop, 0) for axis in along]
        out.append(permute(value, moves))
    return out + list(before)


def swapped(value):
    return permute(value, [(0, 0, 1)] * 2)


def everyone(value):
    value = value[None]
    chips = [[x * SIDE + z for z in range(SIDE)] for x in range(SIDE)]
    for lines in (chips, list(zip(*chips, strict=True))):
        groups = [[2 * chip + core for chip in line] for core in range(2) for line in lines]
        spread = jnp.broadcast_to(value[None], (SIDE,) + value.shape)
        spread = spread.reshape((-1,) + value.shape[1:])
        value = lax.all_to_all(spread, "ens", 0, 0, tiled=True, axis_index_groups=groups)
    return value


def per_device(
    hidden, forcing, norm_gain, w_query, w_key, w_value, w_out, w_decode, targets, area_weight
):
    node_rows = hidden.shape[1]
    width = hidden.shape[2]
    head_size = width // HEADS
    span = node_rows + 2 * HALO
    scale = 1.0 / math.sqrt(head_size)
    members = lax.axis_size("ens")
    shards = lax.axis_size("node")
    rows = w_query.shape[0]
    variables = w_decode.shape[1]
    steps = width // STEP
    shape = jax.ShapeDtypeStruct

    def params(mebibytes):
        return pltpu.CompilerParams(vmem_limit_bytes=mebibytes * 1024 * 1024)

    def cost(us):
        return pl.CostEstimate(
            flops=us * 10**9, transcendentals=0, bytes_accessed=us * 3 * 10**6
        )
    decode_t = jnp.pad(w_decode.T, ((0, LANES - variables), (0, 0)))
    mixed = nt(w_out, decode_t).astype(b16)
    position = lax.axis_index("ens")
    core = position % 2
    at_y = lax.axis_index("node") % RING_Y
    place = jnp.stack([position // (2 * SIDE), position // 2 % SIDE, core, at_y])
    place = place.astype(jnp.int32)
    packed = jnp.concatenate([w_query, w_key, w_value, mixed], 1)
    xfield = hidden[0].astype(f32) + forcing.astype(f32)
    inverse_rms = lax.rsqrt(jnp.mean(xfield * xfield, -1, keepdims=True) + EPS_NORM)
    normed = (xfield * inverse_rms * norm_gain).astype(b16)
    low, high, wrapped = halos(normed)
    row = ring(packed, (0, 1))
    *mine, low, high, wrapped = ring(jnp.concatenate(row, 0), (1, 0), (low, high, wrapped))
    pieces = mine + [swapped(piece) for piece in mine]

    packed_width = 3 * width + LANES
    in_smem = pl.BlockSpec(memory_space=pltpu.SMEM)
    in_vmem = pl.BlockSpec(memory_space=pltpu.VMEM)
    in_hbm = pl.BlockSpec(memory_space=pltpu.HBM)

    def held(value):
        return pltpu.with_memory_space_constraint(value, pltpu.HBM)

    queries, keys, values, attended, lse, pred, mixed, full = pl.pallas_call(
        lambda *refs: forward_kernel(scale, *refs),
        in_specs=[in_smem] + [in_vmem] * (7 + len(pieces)),
        out_specs=[in_hbm, in_hbm, in_hbm, in_vmem, in_hbm, in_vmem, in_vmem, in_hbm],
        out_shape=[
            pltpu.HBM((span, width), b16),
            pltpu.HBM((span, width), b16),
            pltpu.HBM((span, width), b16),
            shape((node_rows, width), b16),
            pltpu.HBM((node_rows, width), f32),
            shape((VROWS, node_rows), b16),
            shape((width, LANES), b16),
            pltpu.HBM((width, packed_width), b16),
        ],
        scratch_shapes=[
            pltpu.VMEM((span, width), b16),
            pltpu.VMEM((span, width), b16),
            pltpu.VMEM((span, width), b16),
            pltpu.VMEM((node_rows, width), f32),
            pltpu.VMEM((span, width), b16),
            pltpu.VMEM((width, packed_width), b16),
            pltpu.SemaphoreType.DMA((1 + 4 * steps,)),
        ],
        compiler_params=params(24),
        cost_estimate=cost(9),
        name="forward",
    )(place, low, normed, high, wrapped, hidden, forcing, decode_t, *pieces)

    others = everyone(pred)
    theirs = swapped(others)
    eps = (1.0 - ALPHA) / members
    coeff = (1.0 - eps) / (2.0 * (members - 1))
    truth = jnp.pad(targets, ((0, VROWS - variables), (0, 0)))
    payload = VROWS + 5 * HEADS
    gram, halo = pl.pallas_call(
        lambda *refs: loss_kernel(coeff, variables, *refs),
        grid=(1,),
        in_specs=[
            whole(others.shape),
            whole(others.shape),
            whole((VROWS, node_rows)),
            whole((VROWS, node_rows)),
            whole((1, node_rows)),
            whole((node_rows, width)),
            whole((width, LANES)),
            whole((node_rows, width)),
        ],
        out_specs=[
            whole((width, LANES)),
            whole((payload, node_rows)),
        ],
        out_shape=[
            shape((width, LANES), b16),
            shape((payload, node_rows), b16),
        ],
        compiler_params=params(12),
        cost_estimate=cost(3),
        name="crps",
    )(others, theirs, pred, truth, area_weight[None], attended, mixed, lse)

    halo_low, halo_high, halo_wrapped = halos(halo)
    parts = lax.all_to_all(gram.reshape(members, rows, LANES), "ens", 0, 0, tiled=True)
    spread = pl.pallas_call(
        lambda *refs: middle_kernel(variables, *refs),
        in_specs=[in_vmem],
        out_specs=in_vmem,
        out_shape=shape((shards, rows, LANES), b16),
        compiler_params=params(8),
        cost_estimate=cost(1),
        name="middle",
    )(parts)
    halo, spread = lax.optimization_barrier((halo, spread))
    parts = lax.all_to_all(spread, "node", 0, 0, tiled=True)
    factor = 1.0 / (members * node_rows * shards * variables)
    grad_out_proj, loss = pl.pallas_call(
        lambda *refs: last_kernel(variables, factor, *refs),
        in_specs=[in_vmem] * 2,
        out_specs=[in_vmem] * 2,
        out_shape=[shape((rows, width), f32), shape((1, LANES), f32)],
        compiler_params=params(8),
        cost_estimate=cost(1),
        name="last",
    )(parts, decode_t)

    grad_hidden = pl.pallas_call(
        lambda *refs: backward_kernel(scale, *refs),
        in_specs=[in_smem] + [in_vmem] * 10 + [in_hbm] * 5,
        out_specs=in_vmem,
        out_shape=shape((1, node_rows, width), b16),
        scratch_shapes=[
            pltpu.VMEM((span, width), b16),
            pltpu.VMEM((span, width), b16),
            pltpu.VMEM((span, width), b16),
            pltpu.VMEM((node_rows, width), f32),
            pltpu.VMEM((width, 3 * width), b16),
            pltpu.VMEM((span, LANES), b16),
            pltpu.VMEM((2, HEADS, 2 * HALO), f32),
            pltpu.SemaphoreType.DMA((4 + 3 * steps,)),
        ],
        compiler_params=params(24),
        cost_estimate=cost(12),
        name="backward",
    )(
        place, halo_low, halo, halo_high, halo_wrapped, hidden, forcing, inverse_rms,
        norm_gain[None], decode_t, mixed,
        *[held(part) for part in (queries, keys, values, lse, full)],
    )
    return (grad_hidden, grad_out_proj, loss[0, 0])


def solution(mesh):
    placed = (
        P("ens", "node", None),
        P("node", None),
        P(),
        P("ens", None),
        P("ens", None),
        P("ens", None),
        P("ens", None),
        P(),
        P(None, "node"),
        P("node"),
    )
    return jax.shard_map(
        per_device,
        mesh=mesh,
        in_specs=placed,
        out_specs=(P("ens", "node", None), P("ens", None), P()),
        check_vma=False,
    )
```

```python
import math

import jax
import jax.numpy as jnp
from jax import lax
from jax.experimental import pallas as pl
from jax.experimental.pallas import tpu as pltpu
from jax.sharding import PartitionSpec as P

HEADS = 16
HALO = 128
LANES = 128
STEP = 256
VROWS = 112
SIDE = 4
RING_Z = 8
RING_Y = 8
HOPS = (0, SIDE - 1, 1, 2)


ALPHA = 0.95
KAPPA = 0.25
EPS_NORM = 1e-05
FAR = -1e30

f32 = jnp.float32
b16 = jnp.bfloat16


def nn(a, b):
    return lax.dot_general(a, b, (((1,), (0,)), ((), ())), preferred_element_type=f32)


def nt(a, b):
    return lax.dot_general(a, b, (((1,), (1,)), ((), ())), preferred_element_type=f32)


def tn(a, b):
    return lax.dot_general(a, b, (((0,), (0,)), ((), ())), preferred_element_type=f32)


def whole(shape):
    return pl.BlockSpec(shape, lambda i: (0,) * len(shape))


def head_masks(value):
    lane = lax.broadcasted_iota(jnp.int32, (1, LANES), 1)
    first = jnp.where(lane < LANES // 2, value, 0.0).astype(b16)
    second = jnp.where(lane < LANES // 2, 0.0, value).astype(b16)
    return first, second


def window_mask(rows, span):
    offset = lax.broadcasted_iota(jnp.int32, (rows, span), 1) - lax.broadcasted_iota(
        jnp.int32, (rows, span), 0
    )
    return (offset >= 0) & (offset <= 2 * HALO)


def split_bf16(value, pieces):
    out = []
    for _ in range(pieces):
        piece = value.astype(b16)
        out.append(piece)
        value = value - piece.astype(f32)
    return out


def forward_kernel(scale, place, near, own, far, hidden, forcing, decode_t, *refs):
    pieces, refs = refs[: 2 * len(HOPS)], refs[2 * len(HOPS) :]
    (
        queries_out, keys_out, values_out, attended, lse_out, pred, mixed, full,
        queries, keys, values, lse, normed, weights, store,
    ) = refs
    rows, width = own.shape
    span = rows + 2 * HALO
    x, z, core = place[0], place[1], place[2]
    side = len(HOPS)
    block = pieces[0].shape[0] // side
    for mine in (True, False):
        which = core if mine else 1 - core
        for outer, second in enumerate(HOPS):
            piece = pieces[outer if mine else side + outer]
            for inner, first in enumerate(HOPS):
                along_x = jnp.where(which == 0, first, second)
                along_z = jnp.where(which == 0, second, first)
                chip = lax.rem(x + along_x, side) * side + lax.rem(z + along_z, side)
                at = pl.multiple_of((chip * 2 + which) * block, block)
                weights[pl.ds(at, block), :] = piece[inner * block : (inner + 1) * block, :]
    stores = [pltpu.make_async_copy(weights, full, store.at[0])]
    stores[0].start()
    mixed[...] = weights[:, 3 * width :]
    even = place[3] == 0
    normed[:HALO] = jnp.where(even, near[...], far[...])
    normed[HALO : HALO + rows] = own[...]
    normed[HALO + rows :] = jnp.where(even, far[...], near[...])
    total = nt(hidden[0], decode_t[...]) + nt(forcing[...], decode_t[...])
    window = window_mask(rows, span)
    masks = head_masks(scale)
    lower = lax.broadcasted_iota(jnp.int32, (rows, LANES), 1) < LANES // 2
    pairs = STEP // LANES
    for at in range(0, width, STEP):
        cols = slice(at, at + STEP)
        field = normed[...]
        projected = [
            nn(field, weights[:, index * width + at : index * width + at + STEP]).astype(b16)
            for index in range(3)
        ]
        query, key, value = projected
        for part, scratch, out in zip(
            projected, (queries, keys, values), (queries_out, keys_out, values_out), strict=True
        ):
            scratch[:, cols] = part
            stores.append(
                pltpu.make_async_copy(scratch.at[:, cols], out.at[:, cols], store.at[len(stores)])
            )
            stores[-1].start()
        scores = []
        for pair in range(pairs):
            lanes = slice(pair * LANES, (pair + 1) * LANES)
            for mask in masks:
                scores.append(nt(query[HALO : HALO + rows, lanes] * mask, key[:, lanes]))
        scores = [jnp.where(window, score, FAR) for score in scores]
        tops = [jnp.max(score, -1, keepdims=True) for score in scores]
        expos = [jnp.exp(score - top) for score, top in zip(scores, tops, strict=True)]
        norms = [jnp.sum(expo, -1, keepdims=True) for expo in expos]
        probs = [(expo * (1.0 / norm)).astype(b16) for expo, norm in zip(expos, norms, strict=True)]
        outs = [
            nn(prob, value[:, index // 2 * LANES : (index // 2 + 1) * LANES])
            for index, prob in enumerate(probs)
        ]
        stats = [top + jnp.log(norm) for top, norm in zip(tops, norms, strict=True)]
        result = jnp.concatenate(
            [jnp.where(lower, outs[2 * n], outs[2 * n + 1]).astype(b16) for n in range(pairs)], 1
        )
        attended[:, cols] = result
        lse[:, cols] = jnp.concatenate(
            [jnp.where(lower, stats[2 * n], stats[2 * n + 1]) for n in range(pairs)], 1
        )
        stores.append(
            pltpu.make_async_copy(lse.at[:, cols], lse_out.at[:, cols], store.at[len(stores)])
        )
        stores[-1].start()
        total = total + nn(result, mixed[cols, :])
    pred[...] = total.T[:VROWS].astype(b16)
    for copy in stores:
        copy.wait()


def loss_kernel(
    coeff, variables, others, theirs, pred, targets, weight, attended, mixed, lse,
    gram, halo,
):
    own = pred[...].astype(f32)
    rows = attended.shape[0]
    width = attended.shape[1]

    def member(index, carry):
        pair_abs, pair_slope = carry
        for part in (others, theirs):
            delta = own - part[index].astype(f32)
            square = delta * delta + KAPPA * KAPPA
            inverse = lax.rsqrt(square)
            pair_abs = pair_abs + (square * inverse - KAPPA)
            pair_slope = pair_slope + delta * inverse
        return pair_abs, pair_slope

    zero = jnp.zeros((VROWS, LANES), f32)
    pair_abs, pair_slope = lax.fori_loop(0, others.shape[0], member, (zero, zero), unroll=2)
    delta = own - targets[...].astype(f32)
    square = delta * delta + KAPPA * KAPPA
    inverse = lax.rsqrt(square)
    real = lax.broadcasted_iota(jnp.int32, (VROWS, LANES), 0) < variables
    scale = weight[...]
    entries = jnp.where(real, scale * (square * inverse - KAPPA - coeff * pair_abs), 0.0)
    loss = jnp.sum(jnp.sum(entries, 0, keepdims=True), 1, keepdims=True)
    grad = jnp.where(real, scale * (delta * inverse - 2.0 * coeff * pair_slope), 0.0)
    grad_b = grad.astype(b16)
    halo[:VROWS] = grad_b
    grad_full = jnp.concatenate([grad, jnp.zeros((LANES - VROWS, LANES), f32)], 0)
    grad_t = grad_full.T.astype(b16)
    parts = nn(grad_full.astype(b16), attended[...])
    parts = parts.T
    column = lax.broadcasted_iota(jnp.int32, (width, LANES), 1)
    for index, piece in enumerate(split_bf16(loss, 3)):
        parts = jnp.where(column == variables + index, piece.astype(f32), parts)
    gram[...] = parts.astype(b16)
    grad_att = nt(grad_t, mixed[...]).astype(b16)
    size = width // HEADS
    head = lax.broadcasted_iota(jnp.int32, (HEADS, width), 0)
    feature = lax.broadcasted_iota(jnp.int32, (HEADS, width), 1)
    inside = jnp.where((feature >= head * size) & (feature < (head + 1) * size), 1.0, 0.0)
    chosen = jnp.where(feature == head * size, 1.0, 0.0).astype(b16)
    inside = inside.astype(b16)
    product = grad_att.astype(f32) * attended[...].astype(f32)
    row_delta = sum(nt(inside, piece) for piece in split_bf16(product, 2))
    row_lse = sum(nt(chosen, piece) for piece in split_bf16(lse[...], 3))
    at = VROWS
    for piece in split_bf16(row_delta, 2) + split_bf16(row_lse, 3):
        halo[at : at + HEADS] = piece
        at += HEADS


def middle_kernel(variables, parts, spread):
    total = parts[0].astype(f32)
    for index in range(1, parts.shape[0]):
        total = total + parts[index].astype(f32)
    column = lax.broadcasted_iota(jnp.int32, total.shape, 1)
    spare = (column >= variables) & (column < variables + 3)
    loss = jnp.sum(jnp.where(spare, total, 0.0), 1, keepdims=True)
    for index, piece in enumerate(split_bf16(loss, 3)):
        total = jnp.where(column == variables + index, piece.astype(f32), total)
    total = total.astype(b16)
    for index in range(spread.shape[0]):
        spread[index] = total


def last_kernel(variables, factor, parts, decode_t, grad_out, loss):
    total = parts[0].astype(f32)
    for index in range(1, parts.shape[0]):
        total = total + parts[index].astype(f32)
    column = lax.broadcasted_iota(jnp.int32, total.shape, 1)
    spare = (column >= variables) & (column < variables + 3)
    first = jnp.sum(jnp.where(spare, total, 0.0), 1, keepdims=True)[:1]
    loss[...] = jnp.broadcast_to(first * factor, loss.shape)
    real = jnp.where(column < variables, total, 0.0)
    grad_out[...] = sum(nn(piece, decode_t[...]) for piece in split_bf16(real, 2))


def backward_kernel(
    scale, place, near, own, far, hidden, forcing, inverse_rms, gain, decode_t, mixed,
    queries_in, keys_in, values_in, lse_in, full,
    grad_hidden, queries, keys, values, lse, weights, grad_t, stats, load,
):
    rows, width = lse.shape
    span = keys.shape[0]
    loads = []

    def fetch(source, target):
        loads.append(pltpu.make_async_copy(source, target, load.at[len(loads)]))
        loads[-1].start()

    fetch(queries_in, queries)
    fetch(keys_in, keys)
    fetch(values_in, values)
    fetch(lse_in, lse)
    for at in range(0, width, STEP):
        for index in range(3):
            cols = slice(index * width + at, index * width + at + STEP)
            fetch(full.at[:, cols], weights.at[:, cols])

    even = place[3] == 0
    low = jnp.where(even, near[...], far[...])
    high = jnp.where(even, far[...], near[...])
    zero = jnp.zeros((LANES - VROWS, LANES), b16)
    for side, part in enumerate((own[...], low, high)):
        grad = jnp.concatenate([part[:VROWS], zero], 0)
        grad_t[side * rows : (side + 1) * rows] = grad.astype(f32).T.astype(b16)
    for side, part in enumerate((low, high)):
        at = slice(side * HALO, (side + 1) * HALO)
        pieces = [part[VROWS + HEADS * n : VROWS + HEADS * (n + 1)].astype(f32) for n in range(5)]
        stats[0, :, at] = pieces[0] + pieces[1]
        stats[1, :, at] = pieces[2] + pieces[3] + pieces[4]
    grad_resid = nn(grad_t[:rows], decode_t[...])

    window = window_mask(rows, span)
    key_at = lax.broadcasted_iota(jnp.int32, (rows, 2 * HALO), 0)
    query_at = lax.broadcasted_iota(jnp.int32, (rows, 2 * HALO), 1)
    reach = ((query_at < HALO) & (query_at >= key_at)) | (
        (query_at >= HALO) & (query_at - HALO <= key_at)
    )
    scaled = head_masks(scale)
    plain = head_masks(1.0)
    center = slice(HALO, HALO + rows)
    halves = [(pair, half) for pair in range(STEP // LANES) for half in range(2)]
    total = jnp.zeros((rows, width), f32)
    for copy in loads[:4]:
        copy.wait()
    for at in range(0, width, STEP):
        step = at // STEP
        grad_att = nt(grad_t[...], mixed[at : at + STEP, :]).astype(b16)
        lanes = [slice(at + pair * LANES, at + (pair + 1) * LANES) for pair in range(STEP // LANES)]
        query = [queries[center, cols] for cols in lanes]
        key = [keys[:, cols] for cols in lanes]
        value = [values[:, cols] for cols in lanes]
        far_query = [
            jnp.concatenate([queries[:HALO, cols], queries[HALO + rows :, cols]], 0)
            for cols in lanes
        ]
        grad = [grad_att[:rows, n * LANES : (n + 1) * LANES] for n in range(len(lanes))]
        far_grad = [grad_att[rows:, n * LANES : (n + 1) * LANES] for n in range(len(lanes))]
        scores = [nt(query[p] * scaled[h], key[p]) for p, h in halves]
        d_probs = [nt(grad[p] * plain[h], value[p]) for p, h in halves]
        probs = []
        for (p, h), score in zip(halves, scores, strict=True):
            start = lanes[p].start + h * (LANES // 2)
            probs.append(jnp.where(window, jnp.exp(score - lse[:, start : start + 1]), 0.0))
        deltas = [
            jnp.sum(prob * d_prob, -1, keepdims=True)
            for prob, d_prob in zip(probs, d_probs, strict=True)
        ]
        d_scores = [
            (prob * (d_prob - delta)).astype(b16)
            for prob, d_prob, delta in zip(probs, d_probs, deltas, strict=True)
        ]
        probs = [prob.astype(b16) for prob in probs]
        far_scores = [nt(key[p][center] * scaled[h], far_query[p]) for p, h in halves]
        far_d_probs = [nt(value[p][center] * plain[h], far_grad[p]) for p, h in halves]
        far_probs, far_d_scores = [], []
        for (p, h), score, d_prob in zip(halves, far_scores, far_d_probs, strict=True):
            row = 2 * (step * len(lanes) + p) + h
            prob = jnp.where(reach, jnp.exp(score - stats[1, row : row + 1, :]), 0.0)
            far_d_scores.append((prob * (d_prob - stats[0, row : row + 1, :])).astype(b16))
            far_probs.append(prob.astype(b16))
        d_query, d_key, d_value = [], [], []
        for p in range(len(lanes)):
            first, second = 2 * p, 2 * p + 1
            d_query.append(
                nn(d_scores[first], key[p] * scaled[0]) + nn(d_scores[second], key[p] * scaled[1])
            )
            d_key.append(
                tn(d_scores[first][:, center], query[p] * scaled[0])
                + tn(d_scores[second][:, center], query[p] * scaled[1])
                + nn(far_d_scores[first], far_query[p] * scaled[0])
                + nn(far_d_scores[second], far_query[p] * scaled[1])
            )
            d_value.append(
                tn(probs[first][:, center], grad[p] * plain[0])
                + tn(probs[second][:, center], grad[p] * plain[1])
                + nn(far_probs[first], far_grad[p] * plain[0])
                + nn(far_probs[second], far_grad[p] * plain[1])
            )
        for index, part in enumerate((d_query, d_key, d_value)):
            loads[4 + 3 * step + index].wait()
            part = jnp.concatenate(part, 1).astype(b16)
            cols = slice(index * width + at, index * width + at + STEP)
            total = total + nt(part, weights[:, cols])
    xfield = hidden[0].astype(f32) + forcing[...].astype(f32)
    inverse = inverse_rms[...]
    grad = gain[...] * total
    mean = jnp.mean(xfield * grad, -1, keepdims=True)
    result = grad_resid + inverse * grad - xfield * (inverse * inverse * inverse * mean)
    grad_hidden[0] = result.astype(b16)


def halos(value):
    count = 2 * RING_Y
    return tuple(
        lax.ppermute(value, "node", [(n, (n + (1 if n % 2 == odd else -1)) % count) for n in range(count)])
        for odd in (1, 0)
    )


def permute(value, moves):
    pairs = []
    for x in range(SIDE):
        for z in range(RING_Z):
            for y in range(RING_Y):
                for core in range(2):
                    dx, dz, dc = moves[core]
                    dz = -dz if dz == -2 and z % 2 == 0 else dz
                    dx = -dx if dx == -2 and x % 2 == 0 else dx
                    at = (x, z, core)
                    to = ((x + dx) % SIDE, (z + dz) % RING_Z, core ^ dc)
                    pairs.append(
                        tuple(
                            ((px * SIDE + pz % SIDE) * 2 + pc) * 2 * RING_Y + pz // SIDE * RING_Y + y
                            for px, pz, pc in (at, to)
                        )
                    )
    return lax.ppermute(value, ("ens", "node"), pairs)


def ring(value, along, before=()):
    out = [value]
    for hop in (1, -1, -2):
        if hop == -2 and before:
            value, *before = lax.optimization_barrier((value, *before))
        moves = [(hop, 0, 0) if axis == 0 else (0, hop, 0) for axis in along]
        out.append(permute(value, moves))
    return out + list(before)


def swapped(value):
    return permute(value, [(0, 0, 1)] * 2)


def everyone(value):
    value = value[None]
    chips = [[x * SIDE + z for z in range(SIDE)] for x in range(SIDE)]
    for lines in (chips, list(zip(*chips, strict=True))):
        groups = [[2 * chip + core for chip in line] for core in range(2) for line in lines]
        spread = jnp.broadcast_to(value[None], (SIDE,) + value.shape)
        spread = spread.reshape((-1,) + value.shape[1:])
        value = lax.all_to_all(spread, "ens", 0, 0, tiled=True, axis_index_groups=groups)
    return value


def per_device(
    hidden, forcing, norm_gain, w_query, w_key, w_value, w_out, w_decode, targets, area_weight
):
    node_rows = hidden.shape[1]
    width = hidden.shape[2]
    head_size = width // HEADS
    span = node_rows + 2 * HALO
    scale = 1.0 / math.sqrt(head_size)
    members = lax.axis_size("ens")
    shards = lax.axis_size("node")
    rows = w_query.shape[0]
    variables = w_decode.shape[1]
    steps = width // STEP
    shape = jax.ShapeDtypeStruct

    def params(mebibytes):
        return pltpu.CompilerParams(vmem_limit_bytes=mebibytes * 1024 * 1024)

    def cost(us):
        return pl.CostEstimate(
            flops=us * 10**9, transcendentals=0, bytes_accessed=us * 3 * 10**6
        )
    decode_t = jnp.pad(w_decode.T, ((0, LANES - variables), (0, 0)))
    mixed = nt(w_out, decode_t).astype(b16)
    position = lax.axis_index("ens")
    core = position % 2
    parity = lax.axis_index("node") % 2
    place = jnp.stack([position // (2 * SIDE), position // 2 % SIDE, core, parity])
    place = place.astype(jnp.int32)
    packed = jnp.concatenate([w_query, w_key, w_value, mixed], 1)
    xfield = hidden[0].astype(f32) + forcing.astype(f32)
    inverse_rms = lax.rsqrt(jnp.mean(xfield * xfield, -1, keepdims=True) + EPS_NORM)
    normed = (xfield * inverse_rms * norm_gain).astype(b16)
    near, far = halos(normed)
    row = ring(packed, (0, 1))
    *mine, near, far = ring(jnp.concatenate(row, 0), (1, 0), (near, far))
    pieces = mine + [swapped(piece) for piece in mine]

    packed_width = 3 * width + LANES
    in_smem = pl.BlockSpec(memory_space=pltpu.SMEM)
    in_vmem = pl.BlockSpec(memory_space=pltpu.VMEM)
    in_hbm = pl.BlockSpec(memory_space=pltpu.HBM)

    def held(value):
        return pltpu.with_memory_space_constraint(value, pltpu.HBM)

    queries, keys, values, attended, lse, pred, mixed, full = pl.pallas_call(
        lambda *refs: forward_kernel(scale, *refs),
        in_specs=[in_smem] + [in_vmem] * (6 + len(pieces)),
        out_specs=[in_hbm, in_hbm, in_hbm, in_vmem, in_hbm, in_vmem, in_vmem, in_hbm],
        out_shape=[
            pltpu.HBM((span, width), b16),
            pltpu.HBM((span, width), b16),
            pltpu.HBM((span, width), b16),
            shape((node_rows, width), b16),
            pltpu.HBM((node_rows, width), f32),
            shape((VROWS, node_rows), b16),
            shape((width, LANES), b16),
            pltpu.HBM((width, packed_width), b16),
        ],
        scratch_shapes=[
            pltpu.VMEM((span, width), b16),
            pltpu.VMEM((span, width), b16),
            pltpu.VMEM((span, width), b16),
            pltpu.VMEM((node_rows, width), f32),
            pltpu.VMEM((span, width), b16),
            pltpu.VMEM((width, packed_width), b16),
            pltpu.SemaphoreType.DMA((1 + 4 * steps,)),
        ],
        compiler_params=params(24),
        cost_estimate=cost(9),
        name="forward",
    )(place, near, normed, far, hidden, forcing, decode_t, *pieces)

    others = everyone(pred)
    theirs = swapped(others)
    eps = (1.0 - ALPHA) / members
    coeff = (1.0 - eps) / (2.0 * (members - 1))
    truth = jnp.pad(targets, ((0, VROWS - variables), (0, 0)))
    payload = VROWS + 5 * HEADS
    gram, halo = pl.pallas_call(
        lambda *refs: loss_kernel(coeff, variables, *refs),
        grid=(1,),
        in_specs=[
            whole(others.shape),
            whole(others.shape),
            whole((VROWS, node_rows)),
            whole((VROWS, node_rows)),
            whole((1, node_rows)),
            whole((node_rows, width)),
            whole((width, LANES)),
            whole((node_rows, width)),
        ],
        out_specs=[
            whole((width, LANES)),
            whole((payload, node_rows)),
        ],
        out_shape=[
            shape((width, LANES), b16),
            shape((payload, node_rows), b16),
        ],
        compiler_params=params(12),
        cost_estimate=cost(3),
        name="crps",
    )(others, theirs, pred, truth, area_weight[None], attended, mixed, lse)

    halo_near, halo_far = halos(halo)
    parts = lax.all_to_all(gram.reshape(members, rows, LANES), "ens", 0, 0, tiled=True)
    spread = pl.pallas_call(
        lambda *refs: middle_kernel(variables, *refs),
        in_specs=[in_vmem],
        out_specs=in_vmem,
        out_shape=shape((shards, rows, LANES), b16),
        compiler_params=params(8),
        cost_estimate=cost(1),
        name="middle",
    )(parts)
    halo, spread = lax.optimization_barrier((halo, spread))
    parts = lax.all_to_all(spread, "node", 0, 0, tiled=True)
    factor = 1.0 / (members * node_rows * shards * variables)
    grad_out_proj, loss = pl.pallas_call(
        lambda *refs: last_kernel(variables, factor, *refs),
        in_specs=[in_vmem] * 2,
        out_specs=[in_vmem] * 2,
        out_shape=[shape((rows, width), f32), shape((1, LANES), f32)],
        compiler_params=params(8),
        cost_estimate=cost(1),
        name="last",
    )(parts, decode_t)

    grad_hidden = pl.pallas_call(
        lambda *refs: backward_kernel(scale, *refs),
        in_specs=[in_smem] + [in_vmem] * 9 + [in_hbm] * 5,
        out_specs=in_vmem,
        out_shape=shape((1, node_rows, width), b16),
        scratch_shapes=[
            pltpu.VMEM((span, width), b16),
            pltpu.VMEM((span, width), b16),
            pltpu.VMEM((span, width), b16),
            pltpu.VMEM((node_rows, width), f32),
            pltpu.VMEM((width, 3 * width), b16),
            pltpu.VMEM((span, LANES), b16),
            pltpu.VMEM((2, HEADS, 2 * HALO), f32),
            pltpu.SemaphoreType.DMA((4 + 3 * steps,)),
        ],
        compiler_params=params(24),
        cost_estimate=cost(12),
        name="backward",
    )(
        place, halo_near, halo, halo_far, hidden, forcing, inverse_rms,
        norm_gain[None], decode_t, mixed,
        *[held(part) for part in (queries, keys, values, lse, full)],
    )
    return (grad_hidden, grad_out_proj, loss[0, 0])


def solution(mesh):
    placed = (
        P("ens", "node", None),
        P("node", None),
        P(),
        P("ens", None),
        P("ens", None),
        P("ens", None),
        P("ens", None),
        P(),
        P(None, "node"),
        P("node"),
    )
    return jax.shard_map(
        per_device,
        mesh=mesh,
        in_specs=placed,
        out_specs=(P("ens", "node", None), P("ens", None), P()),
        check_vma=False,
    )
```

```python
import math

import jax
import jax.numpy as jnp
from jax import lax
from jax.experimental import pallas as pl
from jax.experimental.pallas import tpu as pltpu
from jax.sharding import PartitionSpec as P

HEADS = 16
HALO = 128
LANES = 128
STEP = 256
VROWS = 112
SIDE = 4
RING_Z = 8
RING_Y = 8
HOPS = (0, SIDE - 1, 1, 2)


ALPHA = 0.95
KAPPA = 0.25
EPS_NORM = 1e-05
FAR = -1e30

f32 = jnp.float32
b16 = jnp.bfloat16


def nn(a, b):
    return lax.dot_general(a, b, (((1,), (0,)), ((), ())), preferred_element_type=f32)


def nt(a, b):
    return lax.dot_general(a, b, (((1,), (1,)), ((), ())), preferred_element_type=f32)


def tn(a, b):
    return lax.dot_general(a, b, (((0,), (0,)), ((), ())), preferred_element_type=f32)


def whole(shape):
    return pl.BlockSpec(shape, lambda i: (0,) * len(shape))


def head_masks(value):
    lane = lax.broadcasted_iota(jnp.int32, (1, LANES), 1)
    first = jnp.where(lane < LANES // 2, value, 0.0).astype(b16)
    second = jnp.where(lane < LANES // 2, 0.0, value).astype(b16)
    return first, second


def window_mask(rows, span):
    offset = lax.broadcasted_iota(jnp.int32, (rows, span), 1) - lax.broadcasted_iota(
        jnp.int32, (rows, span), 0
    )
    return (offset >= 0) & (offset <= 2 * HALO)


def split_bf16(value, pieces):
    out = []
    for _ in range(pieces):
        piece = value.astype(b16)
        out.append(piece)
        value = value - piece.astype(f32)
    return out


def forward_kernel(scale, place, near, own, far, hidden, forcing, decode_t, *refs):
    pieces, refs = refs[: 2 * len(HOPS)], refs[2 * len(HOPS) :]
    (
        queries_out, keys_out, values_out, attended, lse_out, pred, mixed, full,
        queries, keys, values, lse, normed, weights, store,
    ) = refs
    rows, width = own.shape
    span = rows + 2 * HALO
    x, z, core = place[0], place[1], place[2]
    side = len(HOPS)
    block = pieces[0].shape[0] // side
    for mine in (True, False):
        which = core if mine else 1 - core
        for outer, second in enumerate(HOPS):
            piece = pieces[outer if mine else side + outer]
            for inner, first in enumerate(HOPS):
                along_x = jnp.where(which == 0, first, second)
                along_z = jnp.where(which == 0, second, first)
                chip = lax.rem(x + along_x, side) * side + lax.rem(z + along_z, side)
                at = pl.multiple_of((chip * 2 + which) * block, block)
                weights[pl.ds(at, block), :] = piece[inner * block : (inner + 1) * block, :]
    stores = [pltpu.make_async_copy(weights, full, store.at[0])]
    stores[0].start()
    mixed[...] = weights[:, 3 * width :]
    even = place[3] == 0
    normed[:HALO] = jnp.where(even, near[...], far[...])
    normed[HALO : HALO + rows] = own[...]
    normed[HALO + rows :] = jnp.where(even, far[...], near[...])
    total = nt(hidden[0], decode_t[...]) + nt(forcing[...], decode_t[...])
    window = window_mask(rows, span)
    masks = head_masks(scale)
    lower = lax.broadcasted_iota(jnp.int32, (rows, LANES), 1) < LANES // 2
    pairs = STEP // LANES
    for at in range(0, width, STEP):
        cols = slice(at, at + STEP)
        field = normed[...]
        projected = [
            nn(field, weights[:, index * width + at : index * width + at + STEP]).astype(b16)
            for index in range(3)
        ]
        query, key, value = projected
        for part, scratch, out in zip(
            projected, (queries, keys, values), (queries_out, keys_out, values_out), strict=True
        ):
            scratch[:, cols] = part
            stores.append(
                pltpu.make_async_copy(scratch.at[:, cols], out.at[:, cols], store.at[len(stores)])
            )
            stores[-1].start()
        scores = []
        for pair in range(pairs):
            lanes = slice(pair * LANES, (pair + 1) * LANES)
            for mask in masks:
                scores.append(nt(query[HALO : HALO + rows, lanes] * mask, key[:, lanes]))
        scores = [jnp.where(window, score, FAR) for score in scores]
        tops = [jnp.max(score, -1, keepdims=True) for score in scores]
        expos = [jnp.exp(score - top) for score, top in zip(scores, tops, strict=True)]
        norms = [jnp.sum(expo, -1, keepdims=True) for expo in expos]
        probs = [(expo * (1.0 / norm)).astype(b16) for expo, norm in zip(expos, norms, strict=True)]
        outs = [
            nn(prob, value[:, index // 2 * LANES : (index // 2 + 1) * LANES])
            for index, prob in enumerate(probs)
        ]
        stats = [top + jnp.log(norm) for top, norm in zip(tops, norms, strict=True)]
        result = jnp.concatenate(
            [jnp.where(lower, outs[2 * n], outs[2 * n + 1]).astype(b16) for n in range(pairs)], 1
        )
        attended[:, cols] = result
        lse[:, cols] = jnp.concatenate(
            [jnp.where(lower, stats[2 * n], stats[2 * n + 1]) for n in range(pairs)], 1
        )
        stores.append(
            pltpu.make_async_copy(lse.at[:, cols], lse_out.at[:, cols], store.at[len(stores)])
        )
        stores[-1].start()
        total = total + nn(result, mixed[cols, :])
    pred[...] = total.T[:VROWS].astype(b16)
    for copy in stores:
        copy.wait()


def loss_kernel(
    coeff, variables, others, theirs, pred, targets, weight, attended, mixed, lse,
    gram, halo,
):
    own = pred[...].astype(f32)
    rows = attended.shape[0]
    width = attended.shape[1]

    def member(index, carry):
        pair_abs, pair_slope = carry
        for part in (others, theirs):
            delta = own - part[index].astype(f32)
            square = delta * delta + KAPPA * KAPPA
            inverse = lax.rsqrt(square)
            pair_abs = pair_abs + (square * inverse - KAPPA)
            pair_slope = pair_slope + delta * inverse
        return pair_abs, pair_slope

    zero = jnp.zeros((VROWS, LANES), f32)
    pair_abs, pair_slope = lax.fori_loop(0, others.shape[0], member, (zero, zero), unroll=2)
    delta = own - targets[...].astype(f32)
    square = delta * delta + KAPPA * KAPPA
    inverse = lax.rsqrt(square)
    real = lax.broadcasted_iota(jnp.int32, (VROWS, LANES), 0) < variables
    scale = weight[...]
    entries = jnp.where(real, scale * (square * inverse - KAPPA - coeff * pair_abs), 0.0)
    loss = jnp.sum(jnp.sum(entries, 0, keepdims=True), 1, keepdims=True)
    grad = jnp.where(real, scale * (delta * inverse - 2.0 * coeff * pair_slope), 0.0)
    grad_b = grad.astype(b16)
    halo[:VROWS] = grad_b
    grad_full = jnp.concatenate([grad, jnp.zeros((LANES - VROWS, LANES), f32)], 0)
    grad_t = grad_full.T.astype(b16)
    parts = nn(grad_full.astype(b16), attended[...])
    parts = parts.T
    column = lax.broadcasted_iota(jnp.int32, (width, LANES), 1)
    for index, piece in enumerate(split_bf16(loss, 3)):
        parts = jnp.where(column == variables + index, piece.astype(f32), parts)
    gram[...] = parts.astype(b16)
    grad_att = nt(grad_t, mixed[...]).astype(b16)
    size = width // HEADS
    head = lax.broadcasted_iota(jnp.int32, (HEADS, width), 0)
    feature = lax.broadcasted_iota(jnp.int32, (HEADS, width), 1)
    inside = jnp.where((feature >= head * size) & (feature < (head + 1) * size), 1.0, 0.0)
    chosen = jnp.where(feature == head * size, 1.0, 0.0).astype(b16)
    inside = inside.astype(b16)
    product = grad_att.astype(f32) * attended[...].astype(f32)
    row_delta = sum(nt(inside, piece) for piece in split_bf16(product, 2))
    row_lse = sum(nt(chosen, piece) for piece in split_bf16(lse[...], 3))
    at = VROWS
    for piece in split_bf16(row_delta, 2) + split_bf16(row_lse, 3):
        halo[at : at + HEADS] = piece
        at += HEADS


def middle_kernel(variables, parts, spread):
    total = parts[0].astype(f32)
    for index in range(1, parts.shape[0]):
        total = total + parts[index].astype(f32)
    column = lax.broadcasted_iota(jnp.int32, total.shape, 1)
    spare = (column >= variables) & (column < variables + 3)
    loss = jnp.sum(jnp.where(spare, total, 0.0), 1, keepdims=True)
    for index, piece in enumerate(split_bf16(loss, 3)):
        total = jnp.where(column == variables + index, piece.astype(f32), total)
    total = total.astype(b16)
    for index in range(spread.shape[0]):
        spread[index] = total


def last_kernel(variables, factor, parts, decode_t, grad_out, loss):
    total = parts[0].astype(f32)
    for index in range(1, parts.shape[0]):
        total = total + parts[index].astype(f32)
    column = lax.broadcasted_iota(jnp.int32, total.shape, 1)
    spare = (column >= variables) & (column < variables + 3)
    first = jnp.sum(jnp.where(spare, total, 0.0), 1, keepdims=True)[:1]
    loss[...] = jnp.broadcast_to(first * factor, loss.shape)
    real = jnp.where(column < variables, total, 0.0)
    grad_out[...] = sum(nn(piece, decode_t[...]) for piece in split_bf16(real, 2))


def backward_kernel(
    scale, place, near, own, far, hidden, forcing, inverse_rms, gain, decode_t, mixed,
    queries_in, keys_in, values_in, lse_in, full,
    grad_hidden, queries, keys, values, lse, weights, grad_t, stats, load,
):
    rows, width = lse.shape
    span = keys.shape[0]
    loads = []

    def fetch(source, target):
        loads.append(pltpu.make_async_copy(source, target, load.at[len(loads)]))
        loads[-1].start()

    fetch(queries_in, queries)
    fetch(keys_in, keys)
    fetch(values_in, values)
    fetch(lse_in, lse)
    for at in range(0, width, STEP):
        for index in range(3):
            cols = slice(index * width + at, index * width + at + STEP)
            fetch(full.at[:, cols], weights.at[:, cols])

    even = place[3] == 0
    low = jnp.where(even, near[...], far[...])
    high = jnp.where(even, far[...], near[...])
    zero = jnp.zeros((LANES - VROWS, LANES), b16)
    for side, part in enumerate((own[...], low, high)):
        grad = jnp.concatenate([part[:VROWS], zero], 0)
        grad_t[side * rows : (side + 1) * rows] = grad.astype(f32).T.astype(b16)
    for side, part in enumerate((low, high)):
        at = slice(side * HALO, (side + 1) * HALO)
        pieces = [part[VROWS + HEADS * n : VROWS + HEADS * (n + 1)].astype(f32) for n in range(5)]
        stats[0, :, at] = pieces[0] + pieces[1]
        stats[1, :, at] = pieces[2] + pieces[3] + pieces[4]
    grad_resid = nn(grad_t[:rows], decode_t[...])

    window = window_mask(rows, span)
    key_at = lax.broadcasted_iota(jnp.int32, (rows, 2 * HALO), 0)
    query_at = lax.broadcasted_iota(jnp.int32, (rows, 2 * HALO), 1)
    reach = ((query_at < HALO) & (query_at >= key_at)) | (
        (query_at >= HALO) & (query_at - HALO <= key_at)
    )
    scaled = head_masks(scale)
    plain = head_masks(1.0)
    center = slice(HALO, HALO + rows)
    halves = [(pair, half) for pair in range(STEP // LANES) for half in range(2)]
    total = jnp.zeros((rows, width), f32)
    for copy in loads[:4]:
        copy.wait()
    for at in range(0, width, STEP):
        step = at // STEP
        grad_att = nt(grad_t[...], mixed[at : at + STEP, :]).astype(b16)
        lanes = [slice(at + pair * LANES, at + (pair + 1) * LANES) for pair in range(STEP // LANES)]
        query = [queries[center, cols] for cols in lanes]
        key = [keys[:, cols] for cols in lanes]
        value = [values[:, cols] for cols in lanes]
        far_query = [
            jnp.concatenate([queries[:HALO, cols], queries[HALO + rows :, cols]], 0)
            for cols in lanes
        ]
        grad = [grad_att[:rows, n * LANES : (n + 1) * LANES] for n in range(len(lanes))]
        far_grad = [grad_att[rows:, n * LANES : (n + 1) * LANES] for n in range(len(lanes))]
        scores = [nt(query[p] * scaled[h], key[p]) for p, h in halves]
        d_probs = [nt(grad[p] * plain[h], value[p]) for p, h in halves]
        probs = []
        for (p, h), score in zip(halves, scores, strict=True):
            start = lanes[p].start + h * (LANES // 2)
            probs.append(jnp.where(window, jnp.exp(score - lse[:, start : start + 1]), 0.0))
        deltas = [
            jnp.sum(prob * d_prob, -1, keepdims=True)
            for prob, d_prob in zip(probs, d_probs, strict=True)
        ]
        d_scores = [
            (prob * (d_prob - delta)).astype(b16)
            for prob, d_prob, delta in zip(probs, d_probs, deltas, strict=True)
        ]
        probs = [prob.astype(b16) for prob in probs]
        far_scores = [nt(key[p][center] * scaled[h], far_query[p]) for p, h in halves]
        far_d_probs = [nt(value[p][center] * plain[h], far_grad[p]) for p, h in halves]
        far_probs, far_d_scores = [], []
        for (p, h), score, d_prob in zip(halves, far_scores, far_d_probs, strict=True):
            row = 2 * (step * len(lanes) + p) + h
            prob = jnp.where(reach, jnp.exp(score - stats[1, row : row + 1, :]), 0.0)
            far_d_scores.append((prob * (d_prob - stats[0, row : row + 1, :])).astype(b16))
            far_probs.append(prob.astype(b16))
        d_query, d_key, d_value = [], [], []
        for p in range(len(lanes)):
            first, second = 2 * p, 2 * p + 1
            d_query.append(
                nn(d_scores[first], key[p] * scaled[0]) + nn(d_scores[second], key[p] * scaled[1])
            )
            d_key.append(
                tn(d_scores[first][:, center], query[p] * scaled[0])
                + tn(d_scores[second][:, center], query[p] * scaled[1])
                + nn(far_d_scores[first], far_query[p] * scaled[0])
                + nn(far_d_scores[second], far_query[p] * scaled[1])
            )
            d_value.append(
                tn(probs[first][:, center], grad[p] * plain[0])
                + tn(probs[second][:, center], grad[p] * plain[1])
                + nn(far_probs[first], far_grad[p] * plain[0])
                + nn(far_probs[second], far_grad[p] * plain[1])
            )
        for index, part in enumerate((d_query, d_key, d_value)):
            loads[4 + 3 * step + index].wait()
            part = jnp.concatenate(part, 1).astype(b16)
            cols = slice(index * width + at, index * width + at + STEP)
            total = total + nt(part, weights[:, cols])
    xfield = hidden[0].astype(f32) + forcing[...].astype(f32)
    inverse = inverse_rms[...]
    grad = gain[...] * total
    mean = jnp.mean(xfield * grad, -1, keepdims=True)
    result = grad_resid + inverse * grad - xfield * (inverse * inverse * inverse * mean)
    grad_hidden[0] = result.astype(b16)


def halos(value):
    count = 2 * RING_Y
    return tuple(
        lax.ppermute(value, "node", [(n, (n + (1 if n % 2 == odd else -1)) % count) for n in range(count)])
        for odd in (1, 0)
    )


def permute(value, moves):
    pairs = []
    for x in range(SIDE):
        for z in range(RING_Z):
            for y in range(RING_Y):
                for core in range(2):
                    dx, dz, dc = moves[core]
                    dz = -dz if dz == -2 and z % 2 == 0 else dz
                    dx = -dx if dx == -2 and x % 2 == 0 else dx
                    at = (x, z, core)
                    to = ((x + dx) % SIDE, (z + dz) % RING_Z, core ^ dc)
                    pairs.append(
                        tuple(
                            ((px * SIDE + pz % SIDE) * 2 + pc) * 2 * RING_Y + pz // SIDE * RING_Y + y
                            for px, pz, pc in (at, to)
                        )
                    )
    return lax.ppermute(value, ("ens", "node"), pairs)


def ring(value, along, before=()):
    out = [value]
    for hop in (1, -1, -2):
        if hop == -2 and before:
            value, *before = lax.optimization_barrier((value, *before))
        moves = [(hop, 0, 0) if axis == 0 else (0, hop, 0) for axis in along]
        out.append(permute(value, moves))
    return out + list(before)


def swapped(value):
    return permute(value, [(0, 0, 1)] * 2)


def everyone(value):
    value = value[None]
    chips = [[x * SIDE + z for z in range(SIDE)] for x in range(SIDE)]
    for lines in (chips, list(zip(*chips, strict=True))):
        groups = [[2 * chip + core for chip in line] for core in range(2) for line in lines]
        spread = jnp.broadcast_to(value[None], (SIDE,) + value.shape)
        spread = spread.reshape((-1,) + value.shape[1:])
        value = lax.all_to_all(spread, "ens", 0, 0, tiled=True, axis_index_groups=groups)
    return value


def per_device(
    hidden, forcing, norm_gain, w_query, w_key, w_value, w_out, w_decode, targets, area_weight
):
    node_rows = hidden.shape[1]
    width = hidden.shape[2]
    head_size = width // HEADS
    span = node_rows + 2 * HALO
    scale = 1.0 / math.sqrt(head_size)
    members = lax.axis_size("ens")
    shards = lax.axis_size("node")
    rows = w_query.shape[0]
    variables = w_decode.shape[1]
    steps = width // STEP
    shape = jax.ShapeDtypeStruct

    def params(mebibytes):
        return pltpu.CompilerParams(vmem_limit_bytes=mebibytes * 1024 * 1024)

    def cost(us):
        return pl.CostEstimate(
            flops=us * 10**9, transcendentals=0, bytes_accessed=us * 3 * 10**6
        )
    decode_t = jnp.pad(w_decode.T, ((0, LANES - variables), (0, 0)))
    mixed = nt(w_out, decode_t).astype(b16)
    position = lax.axis_index("ens")
    core = position % 2
    parity = lax.axis_index("node") % 2
    place = jnp.stack([position // (2 * SIDE), position // 2 % SIDE, core, parity])
    place = place.astype(jnp.int32)
    packed = jnp.concatenate([w_query, w_key, w_value, mixed], 1)
    xfield = hidden[0].astype(f32) + forcing.astype(f32)
    inverse_rms = lax.rsqrt(jnp.mean(xfield * xfield, -1, keepdims=True) + EPS_NORM)
    normed = (xfield * inverse_rms * norm_gain).astype(b16)
    near, far = halos(normed)
    row = ring(packed, (0, 1))
    *mine, far = ring(jnp.concatenate(row, 0), (1, 0), (far,))
    mine[3], near = lax.optimization_barrier((mine[3], near))
    pieces = mine + [swapped(piece) for piece in mine]

    packed_width = 3 * width + LANES
    in_smem = pl.BlockSpec(memory_space=pltpu.SMEM)
    in_vmem = pl.BlockSpec(memory_space=pltpu.VMEM)
    in_hbm = pl.BlockSpec(memory_space=pltpu.HBM)

    def held(value):
        return pltpu.with_memory_space_constraint(value, pltpu.HBM)

    queries, keys, values, attended, lse, pred, mixed, full = pl.pallas_call(
        lambda *refs: forward_kernel(scale, *refs),
        in_specs=[in_smem] + [in_vmem] * (6 + len(pieces)),
        out_specs=[in_hbm, in_hbm, in_hbm, in_vmem, in_hbm, in_vmem, in_vmem, in_hbm],
        out_shape=[
            pltpu.HBM((span, width), b16),
            pltpu.HBM((span, width), b16),
            pltpu.HBM((span, width), b16),
            shape((node_rows, width), b16),
            pltpu.HBM((node_rows, width), f32),
            shape((VROWS, node_rows), b16),
            shape((width, LANES), b16),
            pltpu.HBM((width, packed_width), b16),
        ],
        scratch_shapes=[
            pltpu.VMEM((span, width), b16),
            pltpu.VMEM((span, width), b16),
            pltpu.VMEM((span, width), b16),
            pltpu.VMEM((node_rows, width), f32),
            pltpu.VMEM((span, width), b16),
            pltpu.VMEM((width, packed_width), b16),
            pltpu.SemaphoreType.DMA((1 + 4 * steps,)),
        ],
        compiler_params=params(24),
        cost_estimate=cost(9),
        name="forward",
    )(place, near, normed, far, hidden, forcing, decode_t, *pieces)

    others = everyone(pred)
    theirs = swapped(others)
    eps = (1.0 - ALPHA) / members
    coeff = (1.0 - eps) / (2.0 * (members - 1))
    truth = jnp.pad(targets, ((0, VROWS - variables), (0, 0)))
    payload = VROWS + 5 * HEADS
    gram, halo = pl.pallas_call(
        lambda *refs: loss_kernel(coeff, variables, *refs),
        grid=(1,),
        in_specs=[
            whole(others.shape),
            whole(others.shape),
            whole((VROWS, node_rows)),
            whole((VROWS, node_rows)),
            whole((1, node_rows)),
            whole((node_rows, width)),
            whole((width, LANES)),
            whole((node_rows, width)),
        ],
        out_specs=[
            whole((width, LANES)),
            whole((payload, node_rows)),
        ],
        out_shape=[
            shape((width, LANES), b16),
            shape((payload, node_rows), b16),
        ],
        compiler_params=params(12),
        cost_estimate=cost(3),
        name="crps",
    )(others, theirs, pred, truth, area_weight[None], attended, mixed, lse)

    halo_near, halo_far = halos(halo)
    parts = lax.all_to_all(gram.reshape(members, rows, LANES), "ens", 0, 0, tiled=True)
    spread = pl.pallas_call(
        lambda *refs: middle_kernel(variables, *refs),
        in_specs=[in_vmem],
        out_specs=in_vmem,
        out_shape=shape((shards, rows, LANES), b16),
        compiler_params=params(8),
        cost_estimate=cost(1),
        name="middle",
    )(parts)
    halo, spread = lax.optimization_barrier((halo, spread))
    parts = lax.all_to_all(spread, "node", 0, 0, tiled=True)
    factor = 1.0 / (members * node_rows * shards * variables)
    grad_out_proj, loss = pl.pallas_call(
        lambda *refs: last_kernel(variables, factor, *refs),
        in_specs=[in_vmem] * 2,
        out_specs=[in_vmem] * 2,
        out_shape=[shape((rows, width), f32), shape((1, LANES), f32)],
        compiler_params=params(8),
        cost_estimate=cost(1),
        name="last",
    )(parts, decode_t)

    grad_hidden = pl.pallas_call(
        lambda *refs: backward_kernel(scale, *refs),
        in_specs=[in_smem] + [in_vmem] * 9 + [in_hbm] * 5,
        out_specs=in_vmem,
        out_shape=shape((1, node_rows, width), b16),
        scratch_shapes=[
            pltpu.VMEM((span, width), b16),
            pltpu.VMEM((span, width), b16),
            pltpu.VMEM((span, width), b16),
            pltpu.VMEM((node_rows, width), f32),
            pltpu.VMEM((width, 3 * width), b16),
            pltpu.VMEM((span, LANES), b16),
            pltpu.VMEM((2, HEADS, 2 * HALO), f32),
            pltpu.SemaphoreType.DMA((4 + 3 * steps,)),
        ],
        compiler_params=params(24),
        cost_estimate=cost(12),
        name="backward",
    )(
        place, halo_near, halo, halo_far, hidden, forcing, inverse_rms,
        norm_gain[None], decode_t, mixed,
        *[held(part) for part in (queries, keys, values, lse, full)],
    )
    return (grad_hidden, grad_out_proj, loss[0, 0])


def solution(mesh):
    placed = (
        P("ens", "node", None),
        P("node", None),
        P(),
        P("ens", None),
        P("ens", None),
        P("ens", None),
        P("ens", None),
        P(),
        P(None, "node"),
        P("node"),
    )
    return jax.shard_map(
        per_device,
        mesh=mesh,
        in_specs=placed,
        out_specs=(P("ens", "node", None), P("ens", None), P()),
        check_vma=False,
    )
```

```python
import math

import jax
import jax.numpy as jnp
from jax import lax
from jax.experimental import pallas as pl
from jax.experimental.pallas import tpu as pltpu
from jax.sharding import PartitionSpec as P

HEADS = 16
HALO = 128
LANES = 128
STEP = 256
VROWS = 112
SIDE = 4
RING_Z = 8
RING_Y = 8
HOPS = (0, SIDE - 1, 1, 2)


ALPHA = 0.95
KAPPA = 0.25
EPS_NORM = 1e-05
FAR = -1e30

f32 = jnp.float32
b16 = jnp.bfloat16


def nn(a, b):
    return lax.dot_general(a, b, (((1,), (0,)), ((), ())), preferred_element_type=f32)


def nt(a, b):
    return lax.dot_general(a, b, (((1,), (1,)), ((), ())), preferred_element_type=f32)


def tn(a, b):
    return lax.dot_general(a, b, (((0,), (0,)), ((), ())), preferred_element_type=f32)


def whole(shape):
    return pl.BlockSpec(shape, lambda i: (0,) * len(shape))


def head_masks(value):
    lane = lax.broadcasted_iota(jnp.int32, (1, LANES), 1)
    first = jnp.where(lane < LANES // 2, value, 0.0).astype(b16)
    second = jnp.where(lane < LANES // 2, 0.0, value).astype(b16)
    return first, second


def window_mask(rows, span):
    offset = lax.broadcasted_iota(jnp.int32, (rows, span), 1) - lax.broadcasted_iota(
        jnp.int32, (rows, span), 0
    )
    return (offset >= 0) & (offset <= 2 * HALO)


def split_bf16(value, pieces):
    out = []
    for _ in range(pieces):
        piece = value.astype(b16)
        out.append(piece)
        value = value - piece.astype(f32)
    return out


def forward_kernel(scale, place, near, own, far, hidden, forcing, decode_t, *refs):
    pieces, refs = refs[: 2 * len(HOPS)], refs[2 * len(HOPS) :]
    (
        queries_out, keys_out, values_out, attended, lse_out, pred, mixed, full,
        queries, keys, values, lse, normed, weights, store,
    ) = refs
    rows, width = own.shape
    span = rows + 2 * HALO
    x, z, core = place[0], place[1], place[2]
    side = len(HOPS)
    block = pieces[0].shape[0] // side
    for mine in (True, False):
        which = core if mine else 1 - core
        for outer, second in enumerate(HOPS):
            piece = pieces[outer if mine else side + outer]
            for inner, first in enumerate(HOPS):
                along_x = jnp.where(which == 0, first, second)
                along_z = jnp.where(which == 0, second, first)
                chip = lax.rem(x + along_x, side) * side + lax.rem(z + along_z, side)
                at = pl.multiple_of((chip * 2 + which) * block, block)
                weights[pl.ds(at, block), :] = piece[inner * block : (inner + 1) * block, :]
    stores = [pltpu.make_async_copy(weights, full, store.at[0])]
    stores[0].start()
    mixed[...] = weights[:, 3 * width :]
    even = place[3] == 0
    normed[:HALO] = jnp.where(even, near[...], far[...])
    normed[HALO : HALO + rows] = own[...]
    normed[HALO + rows :] = jnp.where(even, far[...], near[...])
    total = nt(hidden[0], decode_t[...]) + nt(forcing[...], decode_t[...])
    window = window_mask(rows, span)
    masks = head_masks(scale)
    lower = lax.broadcasted_iota(jnp.int32, (rows, LANES), 1) < LANES // 2
    pairs = STEP // LANES
    for at in range(0, width, STEP):
        cols = slice(at, at + STEP)
        field = normed[...]
        projected = [
            nn(field, weights[:, index * width + at : index * width + at + STEP]).astype(b16)
            for index in range(3)
        ]
        query, key, value = projected
        for part, scratch, out in zip(
            projected, (queries, keys, values), (queries_out, keys_out, values_out), strict=True
        ):
            scratch[:, cols] = part
            stores.append(
                pltpu.make_async_copy(scratch.at[:, cols], out.at[:, cols], store.at[len(stores)])
            )
            stores[-1].start()
        scores = []
        for pair in range(pairs):
            lanes = slice(pair * LANES, (pair + 1) * LANES)
            for mask in masks:
                scores.append(nt(query[HALO : HALO + rows, lanes] * mask, key[:, lanes]))
        scores = [jnp.where(window, score, FAR) for score in scores]
        tops = [jnp.max(score, -1, keepdims=True) for score in scores]
        expos = [jnp.exp(score - top) for score, top in zip(scores, tops, strict=True)]
        norms = [jnp.sum(expo, -1, keepdims=True) for expo in expos]
        probs = [(expo * (1.0 / norm)).astype(b16) for expo, norm in zip(expos, norms, strict=True)]
        outs = [
            nn(prob, value[:, index // 2 * LANES : (index // 2 + 1) * LANES])
            for index, prob in enumerate(probs)
        ]
        stats = [top + jnp.log(norm) for top, norm in zip(tops, norms, strict=True)]
        result = jnp.concatenate(
            [jnp.where(lower, outs[2 * n], outs[2 * n + 1]).astype(b16) for n in range(pairs)], 1
        )
        attended[:, cols] = result
        lse[:, cols] = jnp.concatenate(
            [jnp.where(lower, stats[2 * n], stats[2 * n + 1]) for n in range(pairs)], 1
        )
        stores.append(
            pltpu.make_async_copy(lse.at[:, cols], lse_out.at[:, cols], store.at[len(stores)])
        )
        stores[-1].start()
        total = total + nn(result, mixed[cols, :])
    pred[...] = total.T[:VROWS].astype(b16)
    for copy in stores:
        copy.wait()


def loss_kernel(
    coeff, variables, others, theirs, pred, targets, weight, attended, mixed, lse,
    gram, halo,
):
    own = pred[...].astype(f32)
    rows = attended.shape[0]
    width = attended.shape[1]

    def member(index, carry):
        pair_abs, pair_slope = carry
        for part in (others, theirs):
            delta = own - part[index].astype(f32)
            square = delta * delta + KAPPA * KAPPA
            inverse = lax.rsqrt(square)
            pair_abs = pair_abs + (square * inverse - KAPPA)
            pair_slope = pair_slope + delta * inverse
        return pair_abs, pair_slope

    zero = jnp.zeros((VROWS, LANES), f32)
    pair_abs, pair_slope = lax.fori_loop(0, others.shape[0], member, (zero, zero), unroll=2)
    delta = own - targets[...].astype(f32)
    square = delta * delta + KAPPA * KAPPA
    inverse = lax.rsqrt(square)
    real = lax.broadcasted_iota(jnp.int32, (VROWS, LANES), 0) < variables
    scale = weight[...]
    entries = jnp.where(real, scale * (square * inverse - KAPPA - coeff * pair_abs), 0.0)
    loss = jnp.sum(jnp.sum(entries, 0, keepdims=True), 1, keepdims=True)
    grad = jnp.where(real, scale * (delta * inverse - 2.0 * coeff * pair_slope), 0.0)
    grad_b = grad.astype(b16)
    halo[:VROWS] = grad_b
    grad_full = jnp.concatenate([grad, jnp.zeros((LANES - VROWS, LANES), f32)], 0)
    grad_t = grad_full.T.astype(b16)
    parts = nn(grad_full.astype(b16), attended[...])
    parts = parts.T
    column = lax.broadcasted_iota(jnp.int32, (width, LANES), 1)
    for index, piece in enumerate(split_bf16(loss, 3)):
        parts = jnp.where(column == variables + index, piece.astype(f32), parts)
    gram[...] = parts.astype(b16)
    grad_att = nt(grad_t, mixed[...]).astype(b16)
    size = width // HEADS
    head = lax.broadcasted_iota(jnp.int32, (HEADS, width), 0)
    feature = lax.broadcasted_iota(jnp.int32, (HEADS, width), 1)
    inside = jnp.where((feature >= head * size) & (feature < (head + 1) * size), 1.0, 0.0)
    chosen = jnp.where(feature == head * size, 1.0, 0.0).astype(b16)
    inside = inside.astype(b16)
    product = grad_att.astype(f32) * attended[...].astype(f32)
    row_delta = sum(nt(inside, piece) for piece in split_bf16(product, 2))
    row_lse = sum(nt(chosen, piece) for piece in split_bf16(lse[...], 3))
    at = VROWS
    for piece in split_bf16(row_delta, 2) + split_bf16(row_lse, 3):
        halo[at : at + HEADS] = piece
        at += HEADS


def middle_kernel(variables, parts, spread):
    total = parts[0].astype(f32)
    for index in range(1, parts.shape[0]):
        total = total + parts[index].astype(f32)
    column = lax.broadcasted_iota(jnp.int32, total.shape, 1)
    spare = (column >= variables) & (column < variables + 3)
    loss = jnp.sum(jnp.where(spare, total, 0.0), 1, keepdims=True)
    for index, piece in enumerate(split_bf16(loss, 3)):
        total = jnp.where(column == variables + index, piece.astype(f32), total)
    total = total.astype(b16)
    for index in range(spread.shape[0]):
        spread[index] = total


def last_kernel(variables, factor, parts, decode_t, grad_out, loss):
    total = parts[0].astype(f32)
    for index in range(1, parts.shape[0]):
        total = total + parts[index].astype(f32)
    column = lax.broadcasted_iota(jnp.int32, total.shape, 1)
    spare = (column >= variables) & (column < variables + 3)
    first = jnp.sum(jnp.where(spare, total, 0.0), 1, keepdims=True)[:1]
    loss[...] = jnp.broadcast_to(first * factor, loss.shape)
    real = jnp.where(column < variables, total, 0.0)
    grad_out[...] = sum(nn(piece, decode_t[...]) for piece in split_bf16(real, 2))


def backward_kernel(
    scale, place, near, own, far, hidden, forcing, inverse_rms, gain, decode_t, mixed,
    queries_in, keys_in, values_in, lse_in, full,
    grad_hidden, queries, keys, values, lse, weights, grad_t, stats, load,
):
    rows, width = lse.shape
    span = keys.shape[0]
    loads = []

    def fetch(source, target):
        loads.append(pltpu.make_async_copy(source, target, load.at[len(loads)]))
        loads[-1].start()

    fetch(queries_in, queries)
    fetch(keys_in, keys)
    fetch(values_in, values)
    fetch(lse_in, lse)
    for at in range(0, width, STEP):
        for index in range(3):
            cols = slice(index * width + at, index * width + at + STEP)
            fetch(full.at[:, cols], weights.at[:, cols])

    even = place[3] == 0
    low = jnp.where(even, near[...], far[...])
    high = jnp.where(even, far[...], near[...])
    zero = jnp.zeros((LANES - VROWS, LANES), b16)
    for side, part in enumerate((own[...], low, high)):
        grad = jnp.concatenate([part[:VROWS], zero], 0)
        grad_t[side * rows : (side + 1) * rows] = grad.astype(f32).T.astype(b16)
    for side, part in enumerate((low, high)):
        at = slice(side * HALO, (side + 1) * HALO)
        pieces = [part[VROWS + HEADS * n : VROWS + HEADS * (n + 1)].astype(f32) for n in range(5)]
        stats[0, :, at] = pieces[0] + pieces[1]
        stats[1, :, at] = pieces[2] + pieces[3] + pieces[4]
    grad_resid = nn(grad_t[:rows], decode_t[...])

    window = window_mask(rows, span)
    key_at = lax.broadcasted_iota(jnp.int32, (rows, 2 * HALO), 0)
    query_at = lax.broadcasted_iota(jnp.int32, (rows, 2 * HALO), 1)
    reach = ((query_at < HALO) & (query_at >= key_at)) | (
        (query_at >= HALO) & (query_at - HALO <= key_at)
    )
    scaled = head_masks(scale)
    plain = head_masks(1.0)
    center = slice(HALO, HALO + rows)
    halves = [(pair, half) for pair in range(STEP // LANES) for half in range(2)]
    total = jnp.zeros((rows, width), f32)
    for copy in loads[:4]:
        copy.wait()
    for at in range(0, width, STEP):
        step = at // STEP
        grad_att = nt(grad_t[...], mixed[at : at + STEP, :]).astype(b16)
        lanes = [slice(at + pair * LANES, at + (pair + 1) * LANES) for pair in range(STEP // LANES)]
        query = [queries[center, cols] for cols in lanes]
        key = [keys[:, cols] for cols in lanes]
        value = [values[:, cols] for cols in lanes]
        far_query = [
            jnp.concatenate([queries[:HALO, cols], queries[HALO + rows :, cols]], 0)
            for cols in lanes
        ]
        grad = [grad_att[:rows, n * LANES : (n + 1) * LANES] for n in range(len(lanes))]
        far_grad = [grad_att[rows:, n * LANES : (n + 1) * LANES] for n in range(len(lanes))]
        scores = [nt(query[p] * scaled[h], key[p]) for p, h in halves]
        d_probs = [nt(grad[p] * plain[h], value[p]) for p, h in halves]
        probs = []
        for (p, h), score in zip(halves, scores, strict=True):
            start = lanes[p].start + h * (LANES // 2)
            probs.append(jnp.where(window, jnp.exp(score - lse[:, start : start + 1]), 0.0))
        deltas = [
            jnp.sum(prob * d_prob, -1, keepdims=True)
            for prob, d_prob in zip(probs, d_probs, strict=True)
        ]
        d_scores = [
            (prob * (d_prob - delta)).astype(b16)
            for prob, d_prob, delta in zip(probs, d_probs, deltas, strict=True)
        ]
        probs = [prob.astype(b16) for prob in probs]
        far_scores = [nt(key[p][center] * scaled[h], far_query[p]) for p, h in halves]
        far_d_probs = [nt(value[p][center] * plain[h], far_grad[p]) for p, h in halves]
        far_probs, far_d_scores = [], []
        for (p, h), score, d_prob in zip(halves, far_scores, far_d_probs, strict=True):
            row = 2 * (step * len(lanes) + p) + h
            prob = jnp.where(reach, jnp.exp(score - stats[1, row : row + 1, :]), 0.0)
            far_d_scores.append((prob * (d_prob - stats[0, row : row + 1, :])).astype(b16))
            far_probs.append(prob.astype(b16))
        d_query, d_key, d_value = [], [], []
        for p in range(len(lanes)):
            first, second = 2 * p, 2 * p + 1
            d_query.append(
                nn(d_scores[first], key[p] * scaled[0]) + nn(d_scores[second], key[p] * scaled[1])
            )
            d_key.append(
                tn(d_scores[first][:, center], query[p] * scaled[0])
                + tn(d_scores[second][:, center], query[p] * scaled[1])
                + nn(far_d_scores[first], far_query[p] * scaled[0])
                + nn(far_d_scores[second], far_query[p] * scaled[1])
            )
            d_value.append(
                tn(probs[first][:, center], grad[p] * plain[0])
                + tn(probs[second][:, center], grad[p] * plain[1])
                + nn(far_probs[first], far_grad[p] * plain[0])
                + nn(far_probs[second], far_grad[p] * plain[1])
            )
        for index, part in enumerate((d_query, d_key, d_value)):
            loads[4 + 3 * step + index].wait()
            part = jnp.concatenate(part, 1).astype(b16)
            cols = slice(index * width + at, index * width + at + STEP)
            total = total + nt(part, weights[:, cols])
    xfield = hidden[0].astype(f32) + forcing[...].astype(f32)
    inverse = inverse_rms[...]
    grad = gain[...] * total
    mean = jnp.mean(xfield * grad, -1, keepdims=True)
    result = grad_resid + inverse * grad - xfield * (inverse * inverse * inverse * mean)
    grad_hidden[0] = result.astype(b16)


def halos(value):
    count = 2 * RING_Y
    return tuple(
        lax.ppermute(value, "node", [(n, (n + (1 if n % 2 == odd else -1)) % count) for n in range(count)])
        for odd in (1, 0)
    )


def permute(value, moves):
    pairs = []
    for x in range(SIDE):
        for z in range(RING_Z):
            for y in range(RING_Y):
                for core in range(2):
                    dx, dz, dc = moves[core]
                    dz = -dz if dz == -2 and z % 2 == 0 else dz
                    dx = -dx if dx == -2 and x % 2 == 0 else dx
                    at = (x, z, core)
                    to = ((x + dx) % SIDE, (z + dz) % RING_Z, core ^ dc)
                    pairs.append(
                        tuple(
                            ((px * SIDE + pz % SIDE) * 2 + pc) * 2 * RING_Y + pz // SIDE * RING_Y + y
                            for px, pz, pc in (at, to)
                        )
                    )
    return lax.ppermute(value, ("ens", "node"), pairs)


def ring(value, along, before=()):
    blocks = {0: value}
    for hop in (-2, 1, -1):
        if hop == -1 and before:
            value, *before = lax.optimization_barrier((value, *before))
        moves = [(hop, 0, 0) if axis == 0 else (0, hop, 0) for axis in along]
        blocks[hop] = permute(value, moves)
    return [blocks[0], blocks[1], blocks[-1], blocks[-2], *before]


def swapped(value):
    return permute(value, [(0, 0, 1)] * 2)


def everyone(value):
    value = value[None]
    chips = [[x * SIDE + z for z in range(SIDE)] for x in range(SIDE)]
    for lines in (chips, list(zip(*chips, strict=True))):
        groups = [[2 * chip + core for chip in line] for core in range(2) for line in lines]
        spread = jnp.broadcast_to(value[None], (SIDE,) + value.shape)
        spread = spread.reshape((-1,) + value.shape[1:])
        value = lax.all_to_all(spread, "ens", 0, 0, tiled=True, axis_index_groups=groups)
    return value


def per_device(
    hidden, forcing, norm_gain, w_query, w_key, w_value, w_out, w_decode, targets, area_weight
):
    node_rows = hidden.shape[1]
    width = hidden.shape[2]
    head_size = width // HEADS
    span = node_rows + 2 * HALO
    scale = 1.0 / math.sqrt(head_size)
    members = lax.axis_size("ens")
    shards = lax.axis_size("node")
    rows = w_query.shape[0]
    variables = w_decode.shape[1]
    steps = width // STEP
    shape = jax.ShapeDtypeStruct

    def params(mebibytes):
        return pltpu.CompilerParams(vmem_limit_bytes=mebibytes * 1024 * 1024)

    def cost(us):
        return pl.CostEstimate(
            flops=us * 10**9, transcendentals=0, bytes_accessed=us * 3 * 10**6
        )
    decode_t = jnp.pad(w_decode.T, ((0, LANES - variables), (0, 0)))
    mixed = nt(w_out, decode_t).astype(b16)
    position = lax.axis_index("ens")
    core = position % 2
    parity = lax.axis_index("node") % 2
    place = jnp.stack([position // (2 * SIDE), position // 2 % SIDE, core, parity])
    place = place.astype(jnp.int32)
    packed = jnp.concatenate([w_query, w_key, w_value, mixed], 1)
    xfield = hidden[0].astype(f32) + forcing.astype(f32)
    inverse_rms = lax.rsqrt(jnp.mean(xfield * xfield, -1, keepdims=True) + EPS_NORM)
    normed = (xfield * inverse_rms * norm_gain).astype(b16)
    near, far = halos(normed)
    row = ring(packed, (0, 1))
    *mine, near, far = ring(jnp.concatenate(row, 0), (1, 0), (near, far))
    pieces = mine + [swapped(piece) for piece in mine]

    packed_width = 3 * width + LANES
    in_smem = pl.BlockSpec(memory_space=pltpu.SMEM)
    in_vmem = pl.BlockSpec(memory_space=pltpu.VMEM)
    in_hbm = pl.BlockSpec(memory_space=pltpu.HBM)

    def held(value):
        return pltpu.with_memory_space_constraint(value, pltpu.HBM)

    queries, keys, values, attended, lse, pred, mixed, full = pl.pallas_call(
        lambda *refs: forward_kernel(scale, *refs),
        in_specs=[in_smem] + [in_vmem] * (6 + len(pieces)),
        out_specs=[in_hbm, in_hbm, in_hbm, in_vmem, in_hbm, in_vmem, in_vmem, in_hbm],
        out_shape=[
            pltpu.HBM((span, width), b16),
            pltpu.HBM((span, width), b16),
            pltpu.HBM((span, width), b16),
            shape((node_rows, width), b16),
            pltpu.HBM((node_rows, width), f32),
            shape((VROWS, node_rows), b16),
            shape((width, LANES), b16),
            pltpu.HBM((width, packed_width), b16),
        ],
        scratch_shapes=[
            pltpu.VMEM((span, width), b16),
            pltpu.VMEM((span, width), b16),
            pltpu.VMEM((span, width), b16),
            pltpu.VMEM((node_rows, width), f32),
            pltpu.VMEM((span, width), b16),
            pltpu.VMEM((width, packed_width), b16),
            pltpu.SemaphoreType.DMA((1 + 4 * steps,)),
        ],
        compiler_params=params(24),
        cost_estimate=cost(9),
        name="forward",
    )(place, near, normed, far, hidden, forcing, decode_t, *pieces)

    others = everyone(pred)
    theirs = swapped(others)
    eps = (1.0 - ALPHA) / members
    coeff = (1.0 - eps) / (2.0 * (members - 1))
    truth = jnp.pad(targets, ((0, VROWS - variables), (0, 0)))
    payload = VROWS + 5 * HEADS
    gram, halo = pl.pallas_call(
        lambda *refs: loss_kernel(coeff, variables, *refs),
        grid=(1,),
        in_specs=[
            whole(others.shape),
            whole(others.shape),
            whole((VROWS, node_rows)),
            whole((VROWS, node_rows)),
            whole((1, node_rows)),
            whole((node_rows, width)),
            whole((width, LANES)),
            whole((node_rows, width)),
        ],
        out_specs=[
            whole((width, LANES)),
            whole((payload, node_rows)),
        ],
        out_shape=[
            shape((width, LANES), b16),
            shape((payload, node_rows), b16),
        ],
        compiler_params=params(12),
        cost_estimate=cost(3),
        name="crps",
    )(others, theirs, pred, truth, area_weight[None], attended, mixed, lse)

    halo_near, halo_far = halos(halo)
    parts = lax.all_to_all(gram.reshape(members, rows, LANES), "ens", 0, 0, tiled=True)
    spread = pl.pallas_call(
        lambda *refs: middle_kernel(variables, *refs),
        in_specs=[in_vmem],
        out_specs=in_vmem,
        out_shape=shape((shards, rows, LANES), b16),
        compiler_params=params(8),
        cost_estimate=cost(1),
        name="middle",
    )(parts)
    halo, spread = lax.optimization_barrier((halo, spread))
    parts = lax.all_to_all(spread, "node", 0, 0, tiled=True)
    factor = 1.0 / (members * node_rows * shards * variables)
    grad_out_proj, loss = pl.pallas_call(
        lambda *refs: last_kernel(variables, factor, *refs),
        in_specs=[in_vmem] * 2,
        out_specs=[in_vmem] * 2,
        out_shape=[shape((rows, width), f32), shape((1, LANES), f32)],
        compiler_params=params(8),
        cost_estimate=cost(1),
        name="last",
    )(parts, decode_t)

    grad_hidden = pl.pallas_call(
        lambda *refs: backward_kernel(scale, *refs),
        in_specs=[in_smem] + [in_vmem] * 9 + [in_hbm] * 5,
        out_specs=in_vmem,
        out_shape=shape((1, node_rows, width), b16),
        scratch_shapes=[
            pltpu.VMEM((span, width), b16),
            pltpu.VMEM((span, width), b16),
            pltpu.VMEM((span, width), b16),
            pltpu.VMEM((node_rows, width), f32),
            pltpu.VMEM((width, 3 * width), b16),
            pltpu.VMEM((span, LANES), b16),
            pltpu.VMEM((2, HEADS, 2 * HALO), f32),
            pltpu.SemaphoreType.DMA((4 + 3 * steps,)),
        ],
        compiler_params=params(24),
        cost_estimate=cost(12),
        name="backward",
    )(
        place, halo_near, halo, halo_far, hidden, forcing, inverse_rms,
        norm_gain[None], decode_t, mixed,
        *[held(part) for part in (queries, keys, values, lse, full)],
    )
    return (grad_hidden, grad_out_proj, loss[0, 0])


def solution(mesh):
    placed = (
        P("ens", "node", None),
        P("node", None),
        P(),
        P("ens", None),
        P("ens", None),
        P("ens", None),
        P("ens", None),
        P(),
        P(None, "node"),
        P("node"),
    )
    return jax.shard_map(
        per_device,
        mesh=mesh,
        in_specs=placed,
        out_specs=(P("ens", "node", None), P("ens", None), P()),
        check_vma=False,
    )
```

```python
import math

import jax
import jax.numpy as jnp
from jax import lax
from jax.experimental import pallas as pl
from jax.experimental.pallas import tpu as pltpu
from jax.sharding import PartitionSpec as P

HEADS = 16
HALO = 128
LANES = 128
STEP = 256
VROWS = 112
SIDE = 4
RING_Z = 8
RING_Y = 8
HOPS = (0, SIDE - 1, 1, 2)


ALPHA = 0.95
KAPPA = 0.25
EPS_NORM = 1e-05
FAR = -1e30

f32 = jnp.float32
b16 = jnp.bfloat16


def nn(a, b):
    return lax.dot_general(a, b, (((1,), (0,)), ((), ())), preferred_element_type=f32)


def nt(a, b):
    return lax.dot_general(a, b, (((1,), (1,)), ((), ())), preferred_element_type=f32)


def tn(a, b):
    return lax.dot_general(a, b, (((0,), (0,)), ((), ())), preferred_element_type=f32)


def whole(shape):
    return pl.BlockSpec(shape, lambda i: (0,) * len(shape))


def head_masks(value):
    lane = lax.broadcasted_iota(jnp.int32, (1, LANES), 1)
    first = jnp.where(lane < LANES // 2, value, 0.0).astype(b16)
    second = jnp.where(lane < LANES // 2, 0.0, value).astype(b16)
    return first, second


def window_mask(rows, span):
    offset = lax.broadcasted_iota(jnp.int32, (rows, span), 1) - lax.broadcasted_iota(
        jnp.int32, (rows, span), 0
    )
    return (offset >= 0) & (offset <= 2 * HALO)


def split_bf16(value, pieces):
    out = []
    for _ in range(pieces):
        piece = value.astype(b16)
        out.append(piece)
        value = value - piece.astype(f32)
    return out


def norm_kernel(hidden_in, forcing_in, gain, normed, inverse_rms, hidden, forcing, load):
    loads = [
        pltpu.make_async_copy(hidden_in, hidden, load.at[0]),
        pltpu.make_async_copy(forcing_in, forcing, load.at[1]),
    ]
    for copy in loads:
        copy.start()
    for copy in loads:
        copy.wait()
    xfield = hidden[0].astype(f32) + forcing[...].astype(f32)
    inverse = lax.rsqrt(jnp.mean(xfield * xfield, -1, keepdims=True) + EPS_NORM)
    normed[...] = (xfield * inverse * gain[...]).astype(b16)
    inverse_rms[...] = inverse


def pack_kernel(w_query, w_key, w_value, w_out_in, decode_t, packed, w_out, load):
    width = w_out.shape[1]
    loads = [pltpu.make_async_copy(w_out_in, w_out, load.at[0])]
    for index, part in enumerate((w_query, w_key, w_value)):
        cols = packed.at[:, index * width : (index + 1) * width]
        loads.append(pltpu.make_async_copy(part, cols, load.at[index + 1]))
    for copy in loads:
        copy.start()
    loads[0].wait()
    variables = decode_t.shape[0]
    packed[:, 3 * width : 3 * width + variables] = nt(w_out[...], decode_t[...]).astype(b16)
    blank = jnp.zeros((w_out.shape[0], LANES - variables), b16)
    packed[:, 3 * width + variables :] = blank
    for copy in loads[1:]:
        copy.wait()


def forward_kernel(scale, place, near, own, far, hidden, forcing, decode_t, *refs):
    pieces, refs = refs[: 2 * len(HOPS)], refs[2 * len(HOPS) :]
    (
        queries_out, keys_out, values_out, attended, lse_out, pred, mixed, full,
        queries, keys, values, lse, normed, weights, store,
    ) = refs
    rows, width = own.shape
    span = rows + 2 * HALO
    x, z, core = place[0], place[1], place[2]
    side = len(HOPS)
    block = pieces[0].shape[0] // side
    for mine in (True, False):
        which = core if mine else 1 - core
        for outer, second in enumerate(HOPS):
            piece = pieces[outer if mine else side + outer]
            for inner, first in enumerate(HOPS):
                along_x = jnp.where(which == 0, first, second)
                along_z = jnp.where(which == 0, second, first)
                chip = lax.rem(x + along_x, side) * side + lax.rem(z + along_z, side)
                at = pl.multiple_of((chip * 2 + which) * block, block)
                weights[pl.ds(at, block), :] = piece[inner * block : (inner + 1) * block, :]
    stores = [pltpu.make_async_copy(weights, full, store.at[0])]
    stores[0].start()
    mixed[...] = weights[:, 3 * width :]
    even = place[3] == 0
    normed[:HALO] = jnp.where(even, near[...], far[...])
    normed[HALO : HALO + rows] = own[...]
    normed[HALO + rows :] = jnp.where(even, far[...], near[...])
    total = nt(hidden[0], decode_t[...]) + nt(forcing[...], decode_t[...])
    window = window_mask(rows, span)
    masks = head_masks(scale)
    lower = lax.broadcasted_iota(jnp.int32, (rows, LANES), 1) < LANES // 2
    pairs = STEP // LANES
    for at in range(0, width, STEP):
        cols = slice(at, at + STEP)
        field = normed[...]
        projected = [
            nn(field, weights[:, index * width + at : index * width + at + STEP]).astype(b16)
            for index in range(3)
        ]
        query, key, value = projected
        for part, scratch, out in zip(
            projected, (queries, keys, values), (queries_out, keys_out, values_out), strict=True
        ):
            scratch[:, cols] = part
            stores.append(
                pltpu.make_async_copy(scratch.at[:, cols], out.at[:, cols], store.at[len(stores)])
            )
            stores[-1].start()
        scores = []
        for pair in range(pairs):
            lanes = slice(pair * LANES, (pair + 1) * LANES)
            for mask in masks:
                scores.append(nt(query[HALO : HALO + rows, lanes] * mask, key[:, lanes]))
        scores = [jnp.where(window, score, FAR) for score in scores]
        tops = [jnp.max(score, -1, keepdims=True) for score in scores]
        expos = [jnp.exp(score - top) for score, top in zip(scores, tops, strict=True)]
        norms = [jnp.sum(expo, -1, keepdims=True) for expo in expos]
        probs = [(expo * (1.0 / norm)).astype(b16) for expo, norm in zip(expos, norms, strict=True)]
        outs = [
            nn(prob, value[:, index // 2 * LANES : (index // 2 + 1) * LANES])
            for index, prob in enumerate(probs)
        ]
        stats = [top + jnp.log(norm) for top, norm in zip(tops, norms, strict=True)]
        result = jnp.concatenate(
            [jnp.where(lower, outs[2 * n], outs[2 * n + 1]).astype(b16) for n in range(pairs)], 1
        )
        attended[:, cols] = result
        lse[:, cols] = jnp.concatenate(
            [jnp.where(lower, stats[2 * n], stats[2 * n + 1]) for n in range(pairs)], 1
        )
        stores.append(
            pltpu.make_async_copy(lse.at[:, cols], lse_out.at[:, cols], store.at[len(stores)])
        )
        stores[-1].start()
        total = total + nn(result, mixed[cols, :])
    pred[...] = total.T[:VROWS].astype(b16)
    for copy in stores:
        copy.wait()


def loss_kernel(
    coeff, variables, others, theirs, pred, targets, weight, attended, mixed, lse,
    gram, halo,
):
    own = pred[...].astype(f32)
    rows = attended.shape[0]
    width = attended.shape[1]

    def member(index, carry):
        pair_abs, pair_slope = carry
        for part in (others, theirs):
            delta = own - part[index].astype(f32)
            square = delta * delta + KAPPA * KAPPA
            inverse = lax.rsqrt(square)
            pair_abs = pair_abs + (square * inverse - KAPPA)
            pair_slope = pair_slope + delta * inverse
        return pair_abs, pair_slope

    zero = jnp.zeros((VROWS, LANES), f32)
    pair_abs, pair_slope = lax.fori_loop(0, others.shape[0], member, (zero, zero), unroll=2)
    delta = own - targets[...].astype(f32)
    square = delta * delta + KAPPA * KAPPA
    inverse = lax.rsqrt(square)
    real = lax.broadcasted_iota(jnp.int32, (VROWS, LANES), 0) < variables
    scale = weight[...]
    entries = jnp.where(real, scale * (square * inverse - KAPPA - coeff * pair_abs), 0.0)
    loss = jnp.sum(jnp.sum(entries, 0, keepdims=True), 1, keepdims=True)
    grad = jnp.where(real, scale * (delta * inverse - 2.0 * coeff * pair_slope), 0.0)
    grad_b = grad.astype(b16)
    halo[:VROWS] = grad_b
    grad_full = jnp.concatenate([grad, jnp.zeros((LANES - VROWS, LANES), f32)], 0)
    grad_t = grad_full.T.astype(b16)
    parts = nn(grad_full.astype(b16), attended[...])
    parts = parts.T
    column = lax.broadcasted_iota(jnp.int32, (width, LANES), 1)
    for index, piece in enumerate(split_bf16(loss, 3)):
        parts = jnp.where(column == variables + index, piece.astype(f32), parts)
    gram[...] = parts.astype(b16)
    grad_att = nt(grad_t, mixed[...]).astype(b16)
    size = width // HEADS
    head = lax.broadcasted_iota(jnp.int32, (HEADS, width), 0)
    feature = lax.broadcasted_iota(jnp.int32, (HEADS, width), 1)
    inside = jnp.where((feature >= head * size) & (feature < (head + 1) * size), 1.0, 0.0)
    chosen = jnp.where(feature == head * size, 1.0, 0.0).astype(b16)
    inside = inside.astype(b16)
    product = grad_att.astype(f32) * attended[...].astype(f32)
    row_delta = sum(nt(inside, piece) for piece in split_bf16(product, 2))
    row_lse = sum(nt(chosen, piece) for piece in split_bf16(lse[...], 3))
    at = VROWS
    for piece in split_bf16(row_delta, 2) + split_bf16(row_lse, 3):
        halo[at : at + HEADS] = piece
        at += HEADS


def middle_kernel(variables, parts, spread):
    total = parts[0].astype(f32)
    for index in range(1, parts.shape[0]):
        total = total + parts[index].astype(f32)
    column = lax.broadcasted_iota(jnp.int32, total.shape, 1)
    spare = (column >= variables) & (column < variables + 3)
    loss = jnp.sum(jnp.where(spare, total, 0.0), 1, keepdims=True)
    for index, piece in enumerate(split_bf16(loss, 3)):
        total = jnp.where(column == variables + index, piece.astype(f32), total)
    total = total.astype(b16)
    for index in range(spread.shape[0]):
        spread[index] = total


def last_kernel(variables, factor, parts, decode_t, grad_out, loss):
    total = parts[0].astype(f32)
    for index in range(1, parts.shape[0]):
        total = total + parts[index].astype(f32)
    column = lax.broadcasted_iota(jnp.int32, total.shape, 1)
    spare = (column >= variables) & (column < variables + 3)
    first = jnp.sum(jnp.where(spare, total, 0.0), 1, keepdims=True)[:1]
    loss[...] = jnp.broadcast_to(first * factor, loss.shape)
    real = jnp.where(column < variables, total, 0.0)
    grad_out[...] = sum(nn(piece, decode_t[...]) for piece in split_bf16(real, 2))


def backward_kernel(
    scale, place, near, own, far, hidden, forcing, inverse_rms, gain, decode_t, mixed,
    queries_in, keys_in, values_in, lse_in, full,
    grad_hidden, queries, keys, values, lse, weights, grad_t, stats, load,
):
    rows, width = lse.shape
    span = keys.shape[0]
    loads = []

    def fetch(source, target):
        loads.append(pltpu.make_async_copy(source, target, load.at[len(loads)]))
        loads[-1].start()

    fetch(queries_in, queries)
    fetch(keys_in, keys)
    fetch(values_in, values)
    fetch(lse_in, lse)
    for at in range(0, width, STEP):
        for index in range(3):
            cols = slice(index * width + at, index * width + at + STEP)
            fetch(full.at[:, cols], weights.at[:, cols])

    even = place[3] == 0
    low = jnp.where(even, near[...], far[...])
    high = jnp.where(even, far[...], near[...])
    zero = jnp.zeros((LANES - VROWS, LANES), b16)
    for side, part in enumerate((own[...], low, high)):
        grad = jnp.concatenate([part[:VROWS], zero], 0)
        grad_t[side * rows : (side + 1) * rows] = grad.astype(f32).T.astype(b16)
    for side, part in enumerate((low, high)):
        at = slice(side * HALO, (side + 1) * HALO)
        pieces = [part[VROWS + HEADS * n : VROWS + HEADS * (n + 1)].astype(f32) for n in range(5)]
        stats[0, :, at] = pieces[0] + pieces[1]
        stats[1, :, at] = pieces[2] + pieces[3] + pieces[4]
    grad_resid = nn(grad_t[:rows], decode_t[...])

    window = window_mask(rows, span)
    key_at = lax.broadcasted_iota(jnp.int32, (rows, 2 * HALO), 0)
    query_at = lax.broadcasted_iota(jnp.int32, (rows, 2 * HALO), 1)
    reach = ((query_at < HALO) & (query_at >= key_at)) | (
        (query_at >= HALO) & (query_at - HALO <= key_at)
    )
    scaled = head_masks(scale)
    plain = head_masks(1.0)
    center = slice(HALO, HALO + rows)
    halves = [(pair, half) for pair in range(STEP // LANES) for half in range(2)]
    total = jnp.zeros((rows, width), f32)
    for copy in loads[:4]:
        copy.wait()
    for at in range(0, width, STEP):
        step = at // STEP
        grad_att = nt(grad_t[...], mixed[at : at + STEP, :]).astype(b16)
        lanes = [slice(at + pair * LANES, at + (pair + 1) * LANES) for pair in range(STEP // LANES)]
        query = [queries[center, cols] for cols in lanes]
        key = [keys[:, cols] for cols in lanes]
        value = [values[:, cols] for cols in lanes]
        far_query = [
            jnp.concatenate([queries[:HALO, cols], queries[HALO + rows :, cols]], 0)
            for cols in lanes
        ]
        grad = [grad_att[:rows, n * LANES : (n + 1) * LANES] for n in range(len(lanes))]
        far_grad = [grad_att[rows:, n * LANES : (n + 1) * LANES] for n in range(len(lanes))]
        scores = [nt(query[p] * scaled[h], key[p]) for p, h in halves]
        d_probs = [nt(grad[p] * plain[h], value[p]) for p, h in halves]
        probs = []
        for (p, h), score in zip(halves, scores, strict=True):
            start = lanes[p].start + h * (LANES // 2)
            probs.append(jnp.where(window, jnp.exp(score - lse[:, start : start + 1]), 0.0))
        deltas = [
            jnp.sum(prob * d_prob, -1, keepdims=True)
            for prob, d_prob in zip(probs, d_probs, strict=True)
        ]
        d_scores = [
            (prob * (d_prob - delta)).astype(b16)
            for prob, d_prob, delta in zip(probs, d_probs, deltas, strict=True)
        ]
        probs = [prob.astype(b16) for prob in probs]
        far_scores = [nt(key[p][center] * scaled[h], far_query[p]) for p, h in halves]
        far_d_probs = [nt(value[p][center] * plain[h], far_grad[p]) for p, h in halves]
        far_probs, far_d_scores = [], []
        for (p, h), score, d_prob in zip(halves, far_scores, far_d_probs, strict=True):
            row = 2 * (step * len(lanes) + p) + h
            prob = jnp.where(reach, jnp.exp(score - stats[1, row : row + 1, :]), 0.0)
            far_d_scores.append((prob * (d_prob - stats[0, row : row + 1, :])).astype(b16))
            far_probs.append(prob.astype(b16))
        d_query, d_key, d_value = [], [], []
        for p in range(len(lanes)):
            first, second = 2 * p, 2 * p + 1
            d_query.append(
                nn(d_scores[first], key[p] * scaled[0]) + nn(d_scores[second], key[p] * scaled[1])
            )
            d_key.append(
                tn(d_scores[first][:, center], query[p] * scaled[0])
                + tn(d_scores[second][:, center], query[p] * scaled[1])
                + nn(far_d_scores[first], far_query[p] * scaled[0])
                + nn(far_d_scores[second], far_query[p] * scaled[1])
            )
            d_value.append(
                tn(probs[first][:, center], grad[p] * plain[0])
                + tn(probs[second][:, center], grad[p] * plain[1])
                + nn(far_probs[first], far_grad[p] * plain[0])
                + nn(far_probs[second], far_grad[p] * plain[1])
            )
        for index, part in enumerate((d_query, d_key, d_value)):
            loads[4 + 3 * step + index].wait()
            part = jnp.concatenate(part, 1).astype(b16)
            cols = slice(index * width + at, index * width + at + STEP)
            total = total + nt(part, weights[:, cols])
    xfield = hidden[0].astype(f32) + forcing[...].astype(f32)
    inverse = inverse_rms[...]
    grad = gain[...] * total
    mean = jnp.mean(xfield * grad, -1, keepdims=True)
    result = grad_resid + inverse * grad - xfield * (inverse * inverse * inverse * mean)
    grad_hidden[0] = result.astype(b16)


def halos(value):
    count = 2 * RING_Y
    return tuple(
        lax.ppermute(value, "node", [(n, (n + (1 if n % 2 == odd else -1)) % count) for n in range(count)])
        for odd in (1, 0)
    )


def permute(value, moves):
    pairs = []
    for x in range(SIDE):
        for z in range(RING_Z):
            for y in range(RING_Y):
                for core in range(2):
                    dx, dz, dc = moves[core]
                    dz = -dz if dz == -2 and z % 2 == 0 else dz
                    dx = -dx if dx == -2 and x % 2 == 0 else dx
                    at = (x, z, core)
                    to = ((x + dx) % SIDE, (z + dz) % RING_Z, core ^ dc)
                    pairs.append(
                        tuple(
                            ((px * SIDE + pz % SIDE) * 2 + pc) * 2 * RING_Y + pz // SIDE * RING_Y + y
                            for px, pz, pc in (at, to)
                        )
                    )
    return lax.ppermute(value, ("ens", "node"), pairs)


def ring(value, along, before=()):
    blocks = {0: value}
    for hop in (-2, 1, -1):
        if hop == -1 and before:
            value, *before = lax.optimization_barrier((value, *before))
        moves = [(hop, 0, 0) if axis == 0 else (0, hop, 0) for axis in along]
        blocks[hop] = permute(value, moves)
    return [blocks[0], blocks[1], blocks[-1], blocks[-2], *before]


def swapped(value):
    return permute(value, [(0, 0, 1)] * 2)


def everyone(value):
    value = value[None]
    chips = [[x * SIDE + z for z in range(SIDE)] for x in range(SIDE)]
    for lines in (chips, list(zip(*chips, strict=True))):
        groups = [[2 * chip + core for chip in line] for core in range(2) for line in lines]
        spread = jnp.broadcast_to(value[None], (SIDE,) + value.shape)
        spread = spread.reshape((-1,) + value.shape[1:])
        value = lax.all_to_all(spread, "ens", 0, 0, tiled=True, axis_index_groups=groups)
    return value


def per_device(
    hidden, forcing, norm_gain, w_query, w_key, w_value, w_out, w_decode, targets, area_weight
):
    node_rows = hidden.shape[1]
    width = hidden.shape[2]
    head_size = width // HEADS
    span = node_rows + 2 * HALO
    scale = 1.0 / math.sqrt(head_size)
    members = lax.axis_size("ens")
    shards = lax.axis_size("node")
    rows = w_query.shape[0]
    variables = w_decode.shape[1]
    steps = width // STEP
    shape = jax.ShapeDtypeStruct

    def params(mebibytes):
        return pltpu.CompilerParams(vmem_limit_bytes=mebibytes * 1024 * 1024)

    def cost(us):
        return pl.CostEstimate(
            flops=us * 10**9, transcendentals=0, bytes_accessed=us * 3 * 10**6
        )
    decode_t = jnp.pad(w_decode.T, ((0, LANES - variables), (0, 0)))
    position = lax.axis_index("ens")
    core = position % 2
    parity = lax.axis_index("node") % 2
    place = jnp.stack([position // (2 * SIDE), position // 2 % SIDE, core, parity])
    place = place.astype(jnp.int32)
    in_smem = pl.BlockSpec(memory_space=pltpu.SMEM)
    in_vmem = pl.BlockSpec(memory_space=pltpu.VMEM)
    in_hbm = pl.BlockSpec(memory_space=pltpu.HBM)
    packed_width = 3 * width + LANES

    def held(value):
        return pltpu.with_memory_space_constraint(value, pltpu.HBM)

    packed = pl.pallas_call(
        pack_kernel,
        in_specs=[in_hbm] * 4 + [in_vmem],
        out_specs=in_vmem,
        out_shape=shape((rows, packed_width), b16),
        scratch_shapes=[pltpu.VMEM((rows, width), b16), pltpu.SemaphoreType.DMA((4,))],
        compiler_params=params(8),
        cost_estimate=cost(1),
        name="pack",
    )(held(w_query), held(w_key), held(w_value), held(w_out), w_decode.T)
    normed, inverse_rms = pl.pallas_call(
        norm_kernel,
        in_specs=[in_hbm, in_hbm, in_vmem],
        out_specs=[in_vmem] * 2,
        out_shape=[shape((node_rows, width), b16), shape((node_rows, 1), f32)],
        scratch_shapes=[
            pltpu.VMEM((1, node_rows, width), b16),
            pltpu.VMEM((node_rows, width), b16),
            pltpu.SemaphoreType.DMA((2,)),
        ],
        compiler_params=params(8),
        cost_estimate=cost(1),
        name="norm",
    )(held(hidden), held(forcing), norm_gain[None])
    near, far = halos(normed)
    row = ring(packed, (0, 1))
    *mine, near, far = ring(jnp.concatenate(row, 0), (1, 0), (near, far))
    pieces = mine + [swapped(piece) for piece in mine]


    queries, keys, values, attended, lse, pred, mixed, full = pl.pallas_call(
        lambda *refs: forward_kernel(scale, *refs),
        in_specs=[in_smem] + [in_vmem] * (6 + len(pieces)),
        out_specs=[in_hbm, in_hbm, in_hbm, in_vmem, in_hbm, in_vmem, in_vmem, in_hbm],
        out_shape=[
            pltpu.HBM((span, width), b16),
            pltpu.HBM((span, width), b16),
            pltpu.HBM((span, width), b16),
            shape((node_rows, width), b16),
            pltpu.HBM((node_rows, width), f32),
            shape((VROWS, node_rows), b16),
            shape((width, LANES), b16),
            pltpu.HBM((width, packed_width), b16),
        ],
        scratch_shapes=[
            pltpu.VMEM((span, width), b16),
            pltpu.VMEM((span, width), b16),
            pltpu.VMEM((span, width), b16),
            pltpu.VMEM((node_rows, width), f32),
            pltpu.VMEM((span, width), b16),
            pltpu.VMEM((width, packed_width), b16),
            pltpu.SemaphoreType.DMA((1 + 4 * steps,)),
        ],
        compiler_params=params(24),
        cost_estimate=cost(9),
        name="forward",
    )(place, near, normed, far, hidden, forcing, decode_t, *pieces)

    others = everyone(pred)
    theirs = swapped(others)
    eps = (1.0 - ALPHA) / members
    coeff = (1.0 - eps) / (2.0 * (members - 1))
    truth = jnp.pad(targets, ((0, VROWS - variables), (0, 0)))
    payload = VROWS + 5 * HEADS
    gram, halo = pl.pallas_call(
        lambda *refs: loss_kernel(coeff, variables, *refs),
        grid=(1,),
        in_specs=[
            whole(others.shape),
            whole(others.shape),
            whole((VROWS, node_rows)),
            whole((VROWS, node_rows)),
            whole((1, node_rows)),
            whole((node_rows, width)),
            whole((width, LANES)),
            whole((node_rows, width)),
        ],
        out_specs=[
            whole((width, LANES)),
            whole((payload, node_rows)),
        ],
        out_shape=[
            shape((width, LANES), b16),
            shape((payload, node_rows), b16),
        ],
        compiler_params=params(12),
        cost_estimate=cost(3),
        name="crps",
    )(others, theirs, pred, truth, area_weight[None], attended, mixed, lse)

    halo_near, halo_far = halos(halo)
    parts = lax.all_to_all(gram.reshape(members, rows, LANES), "ens", 0, 0, tiled=True)
    spread = pl.pallas_call(
        lambda *refs: middle_kernel(variables, *refs),
        in_specs=[in_vmem],
        out_specs=in_vmem,
        out_shape=shape((shards, rows, LANES), b16),
        compiler_params=params(8),
        cost_estimate=cost(1),
        name="middle",
    )(parts)
    halo, spread = lax.optimization_barrier((halo, spread))
    parts = lax.all_to_all(spread, "node", 0, 0, tiled=True)
    factor = 1.0 / (members * node_rows * shards * variables)
    grad_out_proj, loss = pl.pallas_call(
        lambda *refs: last_kernel(variables, factor, *refs),
        in_specs=[in_vmem] * 2,
        out_specs=[in_vmem] * 2,
        out_shape=[shape((rows, width), f32), shape((1, LANES), f32)],
        compiler_params=params(8),
        cost_estimate=cost(1),
        name="last",
    )(parts, decode_t)

    grad_hidden = pl.pallas_call(
        lambda *refs: backward_kernel(scale, *refs),
        in_specs=[in_smem] + [in_vmem] * 9 + [in_hbm] * 5,
        out_specs=in_vmem,
        out_shape=shape((1, node_rows, width), b16),
        scratch_shapes=[
            pltpu.VMEM((span, width), b16),
            pltpu.VMEM((span, width), b16),
            pltpu.VMEM((span, width), b16),
            pltpu.VMEM((node_rows, width), f32),
            pltpu.VMEM((width, 3 * width), b16),
            pltpu.VMEM((span, LANES), b16),
            pltpu.VMEM((2, HEADS, 2 * HALO), f32),
            pltpu.SemaphoreType.DMA((4 + 3 * steps,)),
        ],
        compiler_params=params(24),
        cost_estimate=cost(12),
        name="backward",
    )(
        place, halo_near, halo, halo_far, hidden, forcing, inverse_rms,
        norm_gain[None], decode_t, mixed,
        *[held(part) for part in (queries, keys, values, lse, full)],
    )
    return (grad_hidden, grad_out_proj, loss[0, 0])


def solution(mesh):
    placed = (
        P("ens", "node", None),
        P("node", None),
        P(),
        P("ens", None),
        P("ens", None),
        P("ens", None),
        P("ens", None),
        P(),
        P(None, "node"),
        P("node"),
    )
    return jax.shard_map(
        per_device,
        mesh=mesh,
        in_specs=placed,
        out_specs=(P("ens", "node", None), P("ens", None), P()),
        check_vma=False,
    )
```
